128 devices in a mesh: fsdp: 128 (over x, y, z, core).
Axes of the slice: x: 4, y: 4, z: 4, core: 2. Of those that a mesh axis runs over, the one named last changes fastest.
Arguments:
- tokens: bfloat16 [32768, 768], P('fsdp'), may hold values from -24 to 24
- cotangent: bfloat16 [32768, 768], P('fsdp'), may hold values from -6 to 6
- segment: int32 [32768], P('fsdp'), may hold values from -1 to 15, as said below
- ln1_gain: bfloat16 [768], P('fsdp'), may hold values from 0.5 to 1.5
- ln1_bias: bfloat16 [768], P('fsdp'), may hold values from -1.1953125 to 1.1953125
- qkv_weight: bfloat16 [768, 2304], P('fsdp'), may hold values from -0.21875 to 0.21875
- qkv_bias: bfloat16 [2304], P('fsdp'), may hold values from -1.1953125 to 1.1953125
- out_weight: bfloat16 [768, 768], P('fsdp'), may hold values from -0.625 to 0.625
- out_bias: bfloat16 [768], P('fsdp'), may hold values from -1.1953125 to 1.1953125
- ln2_gain: bfloat16 [768], P('fsdp'), may hold values from 0.5 to 1.5
- ln2_bias: bfloat16 [768], P('fsdp'), may hold values from -1.1953125 to 1.1953125
- up_weight: bfloat16 [768, 3072], P('fsdp'), may hold values from -0.21875 to 0.21875
- up_bias: bfloat16 [3072], P('fsdp'), may hold values from -1.1953125 to 1.1953125
- down_weight: bfloat16 [3072, 768], P('fsdp'), may hold values from -0.109375 to 0.109375
- down_bias: bfloat16 [768], P('fsdp'), may hold values from -1.1953125 to 1.1953125
Outputs:
- output: bfloat16 [32768, 768], P('fsdp')
- grad_tokens: float32 [32768, 768], P('fsdp')
- grad_ln1_gain: float32 [768], P('fsdp')
- grad_ln1_bias: float32 [768], P('fsdp')
- grad_qkv_weight: float32 [768, 2304], P('fsdp')
- grad_qkv_bias: float32 [2304], P('fsdp')
- grad_out_weight: float32 [768, 768], P('fsdp')
- grad_out_bias: float32 [768], P('fsdp')
- grad_ln2_gain: float32 [768], P('fsdp')
- grad_ln2_bias: float32 [768], P('fsdp')
- grad_up_weight: float32 [768, 3072], P('fsdp')
- grad_up_bias: float32 [3072], P('fsdp')
- grad_down_weight: float32 [3072, 768], P('fsdp')
- grad_down_bias: float32 [768], P('fsdp')
The draws below stay inside these ranges and needn't reach their ends.
Inputs may be any that keep to these rules, and one draw needn't show every extreme that they name: `segment`: within each aligned block of 128 rows (one micro-batch of one device, 2 to a device) the ids of live rows start at 0 at the block's first row and rise by 0 or 1 from row to row, rising only at rows whose place in the block is a multiple of 8; -1 marks padding and fills whole blocks, never a device's first block; in every draw some block is a single sequence of 128 rows, some block is padding, and some block holds 16 sequences.
All inputs are finite; a program needn't handle non-finite values.
Results may differ from the reference program's by a relative error of at most 0.0087.
Values may be sent and summed in bfloat16 or wider, within the bound.
No kernel may reach another device: no remote copies, remote signals or barrier semaphores. Data moves between devices by JAX's collectives and lax.ppermute only.
A program may use at most 128 MiB of HBM per device.

```python
import math
import jax
import jax.numpy as jnp
from jax import lax

D = 768
HEADS = 12
HEAD_DIM = 64
ROTARY = 16
FF = 3072
MB_ROWS = 128
MICRO = 2
TOKENS = 32768
QKV = 2304


def draw_segment(key, part):
    key = jax.random.fold_in(key, 7)
    cut_key, empty_key, whole_key, blank_key = jax.random.split(key, 4)
    block_count = TOKENS // MB_ROWS
    owner_count = block_count // MICRO
    block_ids = jnp.arange(block_count)
    column = jnp.arange(MB_ROWS)
    on_grid = (column % 8 == 0) & (column > 0)
    cut_marks = (jax.random.randint(cut_key, (block_count, MB_ROWS), 0, 6) == 0) & on_grid[None, :]
    whole_block = jax.random.randint(whole_key, (), 0, owner_count) * MICRO
    many_block = (whole_block + MICRO) % block_count
    cut_marks = cut_marks & (block_ids[:, None] != whole_block)
    cut_marks = cut_marks | (block_ids[:, None] == many_block) & on_grid[None, :]
    starts = (cut_marks | (column[None, :] == 0)).astype(jnp.int32)
    segment_ids = jnp.cumsum(starts, axis=1) - 1
    empty_block = (jax.random.randint(empty_key, (block_count,), 0, 2) == 1) & (block_ids % MICRO > 0)
    forced_block = jax.random.randint(blank_key, (), 0, owner_count) * MICRO + 1
    empty_block = empty_block | (block_ids == forced_block)
    segment_ids = jnp.where(empty_block[:, None], -1, segment_ids)
    return segment_ids.reshape(TOKENS).astype(jnp.int32)


def raised(entries, stream_key, source, target, shards_of, factor):
    owner, partner = [(jnp.arange(entries.shape[axis_at]) // (entries.shape[axis_at] // shards_of)).reshape([-1 if axis == axis_at else 1 for axis in range(entries.ndim)]) for axis_at in (source, target)]
    chosen = jax.random.permutation(stream_key, shards_of)[partner]
    strong = (owner == chosen) | (owner == (partner + shards_of // 2) % shards_of)
    return jnp.where(strong, factor * entries, entries)


def shard_levels(rng, extent, pieces, least, high):
    def one(axis_at, parts):
        heights = jax.random.uniform(jax.random.fold_in(jax.random.fold_in(rng, 6), axis_at), (parts,), jnp.float32, least / len(pieces), high / len(pieces))
        return jnp.repeat(jnp.exp(heights), extent[axis_at] // parts).reshape((-1,) + (1,) * (len(extent) - axis_at - 1))

    factor_of = one(*pieces[0])
    for cut in pieces[1:]:
        factor_of = factor_of * one(*cut)
    return factor_of


def normal_values(rng, dims, width, reach, cuts=(), kind=jnp.bfloat16):
    values = width * jax.random.normal(rng, dims, jnp.float32)
    if cuts:
        values = values * shard_levels(rng, dims, cuts, -0.22, 0.18)
    return jnp.clip(values, -reach, reach).astype(kind)


def bell_draw_with(own_key, shape, spread, most, shards, heavy, held_as=jnp.bfloat16):
    entries = spread * jax.random.normal(own_key, shape, jnp.float32)
    if shards:
        entries = entries * shard_levels(own_key, shape, shards, -0.22, 0.18)
    return jnp.clip(raised(entries, jax.random.fold_in(own_key, 3), *heavy), -most, most).astype(held_as)


def setup_inputs(seed: int = 0) -> dict:
    key_list = jax.random.split(jax.random.key(seed), 16)
    tokens = bell_draw_with(key_list[0], (TOKENS, D), 1.0, 24.0, ((0, 128),), (0, 1, 128, 5.5))
    cotangent = normal_values(key_list[1], (TOKENS, D), 1.0, 6.0, ((0, 128),))
    segment = draw_segment(jax.random.fold_in(key_list[15], 71), 0)
    ln1_gain = jnp.clip(1.0 + 0.1 * jax.random.normal(key_list[3], (D,), jnp.float32), 0.5, 1.5).astype(jnp.bfloat16)
    ln1_bias = normal_values(key_list[4], (D,), 0.2, 1.1953125, ((0, 128),))
    qkv_weight = normal_values(key_list[5], (D, QKV), D ** -0.5, 0.21875, ((0, 128),))
    qkv_bias = normal_values(key_list[6], (QKV,), 0.2, 1.1953125, ((0, 128),))
    out_weight = normal_values(key_list[7], (D, D), (D // 8) ** -0.5, 0.625, ((0, 128),))
    out_bias = normal_values(key_list[8], (D,), 0.2, 1.1953125, ((0, 128),))
    ln2_gain = jnp.clip(1.0 + 0.1 * jax.random.normal(key_list[9], (D,), jnp.float32), 0.5, 1.5).astype(jnp.bfloat16)
    ln2_bias = normal_values(key_list[10], (D,), 0.2, 1.1953125, ((0, 128),))
    up_weight = normal_values(key_list[11], (D, FF), D ** -0.5, 0.21875, ((0, 128),))
    up_bias = normal_values(key_list[12], (FF,), 0.2, 1.1953125, ((0, 128),))
    down_weight = normal_values(key_list[13], (FF, D), FF ** -0.5, 0.109375, ((0, 128),))
    down_bias = normal_values(key_list[14], (D,), 0.2, 1.1953125, ((0, 128),))
    return {"tokens": tokens, "cotangent": cotangent, "segment": segment, "ln1_gain": ln1_gain, "ln1_bias": ln1_bias, "qkv_weight": qkv_weight, "qkv_bias": qkv_bias, "out_weight": out_weight, "out_bias": out_bias, "ln2_gain": ln2_gain, "ln2_bias": ln2_bias, "up_weight": up_weight, "up_bias": up_bias, "down_weight": down_weight, "down_bias": down_bias}


@jax.custom_vjp
def low(v):
    return lax.optimization_barrier(v.astype(jnp.bfloat16)).astype(jnp.float32)

@jax.custom_vjp
def low_back(v):
    return v

def low_keep(v):
    return (low(v), None)

def low_pass(kept, grad):
    return (grad,)

def back_keep(v):
    return (v, None)

def back_low(kept, grad):
    return (low(grad),)
low.defvjp(low_keep, low_pass)
low_back.defvjp(back_keep, back_low)
highest = lax.Precision.HIGHEST
masked_score = -1e+30

def layer_norm(values, gain, shift):
    centred = values - lax.optimization_barrier(jnp.mean(values, axis=-1, keepdims=True))
    inverse = lax.rsqrt(lax.optimization_barrier(jnp.mean(centred * centred, axis=-1, keepdims=True)) + 1e-05)
    return centred * inverse * gain + shift

def tables(segment):
    row_count = segment.shape[0]
    same_doc = segment[:, None] == segment[None, :]
    earlier = jnp.arange(row_count)[None, :] <= jnp.arange(row_count)[:, None]
    allowed = same_doc & earlier
    position = lax.optimization_barrier(jnp.sum(allowed.astype(jnp.int32), axis=1)) - 1
    frequency = jnp.exp(jnp.arange(ROTARY // 2, dtype=jnp.float32) * (-2.0 * math.log(10000.0) / ROTARY))
    angles = position.astype(jnp.float32)[:, None] * frequency[None, :]
    return (allowed, jnp.cos(angles), jnp.sin(angles))

def rotate(heads_in, cosine, sine):
    half_rot = ROTARY // 2
    first = heads_in[..., :half_rot]
    second = heads_in[..., half_rot:2 * half_rot]
    cos_rows = cosine[:, None, :]
    sin_rows = sine[:, None, :]
    return jnp.concatenate([first * cos_rows - second * sin_rows, second * cos_rows + first * sin_rows, heads_in[..., 2 * half_rot:]], axis=-1)

def block_forward(params, rows32, segment):
    ln1_gain, ln1_bias, qkv_weight, qkv_bias, out_weight, out_bias, ln2_gain, ln2_bias, up_weight, up_bias, down_weight, down_bias = params
    row_count = rows32.shape[0]
    is_live = (segment >= 0).astype(jnp.float32)[:, None]
    normed_one = low(layer_norm(rows32, ln1_gain, ln1_bias))
    normed_two = low(layer_norm(rows32, ln2_gain, ln2_bias))
    joint = low_back(jnp.dot(normed_one, qkv_weight, precision=highest) + qkv_bias)
    split = joint.reshape(row_count, 3, HEADS, HEAD_DIM)
    allowed, cosine, sine = tables(segment)
    query = low(rotate(split[:, 0], cosine, sine))
    keys_rot = low(rotate(split[:, 1], cosine, sine))
    values_head = low(split[:, 2])
    scores = low_back(jnp.einsum('rhd,shd->hrs', query, keys_rot, precision=highest) * HEAD_DIM ** (-0.5))
    scores = jnp.where(allowed[None], scores, masked_score)
    row_max = lax.optimization_barrier(jnp.max(scores, axis=-1, keepdims=True))
    expd = jnp.exp(scores - row_max)
    probs = low(expd / lax.optimization_barrier(jnp.sum(expd, axis=-1, keepdims=True)))
    mixed = jnp.einsum('hrs,shd->rhd', probs, values_head, precision=highest).reshape(row_count, HEADS * HEAD_DIM)
    mixed = low_back(low(mixed))
    attn_out = low_back(jnp.dot(mixed, out_weight, precision=highest) + out_bias)
    pre_act = low_back(jnp.dot(normed_two, up_weight, precision=highest) + up_bias)
    activation = low(jax.nn.gelu(pre_act, approximate=False))
    mlp_out = low_back(jnp.dot(activation, down_weight, precision=highest) + down_bias)
    return rows32 + is_live * (attn_out + mlp_out)

def reference(tokens, cotangent, segment, ln1_gain, ln1_bias, qkv_weight, qkv_bias, out_weight, out_bias, ln2_gain, ln2_bias, up_weight, up_bias, down_weight, down_bias):
    params = tuple((item.astype(jnp.float32) for item in (ln1_gain, ln1_bias, qkv_weight, qkv_bias, out_weight, out_bias, ln2_gain, ln2_bias, up_weight, up_bias, down_weight, down_bias)))
    block_count = TOKENS // MB_ROWS
    group = math.gcd(max(1, 4096 // MB_ROWS), block_count)
    rounds = block_count // group
    token_blocks = tokens.astype(jnp.float32).reshape(rounds, group, MB_ROWS, D)
    cot_blocks = cotangent.astype(jnp.float32).reshape(rounds, group, MB_ROWS, D)
    seg_blocks = segment.reshape(rounds, group, MB_ROWS)

    def one_round(totals, item):
        token_group, cot_group, seg_group = item

        def run(weights, inputs):
            return jax.vmap(block_forward, in_axes=(None, 0, 0))(weights, inputs, seg_group)
        result, pull = jax.vjp(run, params, token_group)
        grad_params, grad_inputs = pull(cot_group)
        totals = jax.tree.map(lambda left, right: left + right, totals, grad_params)
        return (totals, (result.astype(jnp.bfloat16), grad_inputs))
    zeros = jax.tree.map(jnp.zeros_like, params)
    totals, (results, grad_rows) = lax.scan(one_round, zeros, (token_blocks, cot_blocks, seg_blocks))
    return (results.reshape(TOKENS, D), grad_rows.reshape(TOKENS, D), totals[0], totals[1], totals[2], totals[3], totals[4], totals[5], totals[6], totals[7], totals[8], totals[9], totals[10], totals[11])
```

```python
import math

import jax
import jax.numpy as jnp
from jax import lax
from jax.sharding import PartitionSpec as P

D = 768
HEADS = 12
HEAD_DIM = 64
ROTARY = 16
FF = 3072
MB_ROWS = 128
ROWS = 256
HH = HEADS // 2
HD = D // 2
HF = FF // 2
QW = 3 * HD

epsilon = 1e-05
masked_score = -1e30
inv_sqrt_two = 1.0 / math.sqrt(2.0)
inv_sqrt_two_pi = 1.0 / math.sqrt(2.0 * math.pi)
bf16 = jnp.bfloat16
f32 = jnp.float32

STRIDE = {"x": 32, "y": 8, "z": 2, "c": 1}
SIZE = {"x": 4, "y": 4, "z": 4, "c": 2}
SMALL = (("ln1g", 6), ("ln1b", 6), ("qkvb", 18), ("outb", 6), ("ln2g", 6), ("ln2b", 6), ("upb", 24), ("downb", 6))


def digit(index, axis):
    return (index // STRIDE[axis]) % SIZE[axis]


def shift(axis, step):
    pairs = []
    for source in range(128):
        at = digit(source, axis)
        target = source + ((at + step) % SIZE[axis] - at) * STRIDE[axis]
        pairs.append((source, target))
    return pairs


def down_target(source):
    half, block = source // 64, source % 64
    z, x, y = block // 16, (block // 4) % 4, block % 4
    return ((x * 4 + y) * 4 + z) * 2 + half


def out_target(source):
    return 2 * (source % 64) + source // 64


OUT_PAIRS = [(s, out_target(s)) for s in range(128)]
DOWN_PAIRS = [(s, down_target(s)) for s in range(128)]
OUT_BACK = [(t, s) for s, t in OUT_PAIRS]
DOWN_BACK = [(t, s) for s, t in DOWN_PAIRS]


def permute(values, pairs):
    return lax.ppermute(values, "fsdp", pairs)


def swap(values):
    return permute(values, shift("c", 1))


def ring_gather(block, axis, at):
    pieces = (
        block,
        permute(block, shift(axis, -1)),
        permute(block, shift(axis, 2)),
        permute(block, shift(axis, 1)),
    )
    whole = jnp.zeros((4,) + block.shape, block.dtype)
    for step, piece in enumerate(pieces):
        whole = lax.dynamic_update_index_in_dim(whole, piece, (at + step) % 4, 0)
    return whole


def ring_reduce(blocks, axis, at):
    def pick(step):
        return lax.dynamic_index_in_dim(blocks, (at + step) % 4, 0, keepdims=False)

    arrived = [
        permute(pick(step).astype(bf16), shift(axis, step)) for step in (1, -1, 2)
    ]
    total = pick(0).astype(f32)
    for piece in arrived:
        total = total + piece.astype(f32)
    return total


def layer_norm(values, gain, shift_by):
    centred = values - jnp.mean(values, axis=-1, keepdims=True)
    inverse = lax.rsqrt(jnp.mean(centred * centred, axis=-1, keepdims=True) + epsilon)
    scaled = centred * inverse
    return scaled * gain + shift_by, scaled, inverse


def norm_back(upstream, scaled, inverse, gain):
    weighted = upstream * gain
    grad_in = inverse * (
        weighted
        - jnp.mean(weighted, axis=-1, keepdims=True)
        - scaled * jnp.mean(weighted * scaled, axis=-1, keepdims=True)
    )
    return grad_in, jnp.sum(upstream * scaled, axis=0), jnp.sum(upstream, axis=0)


def tables(segment_rows):
    same_doc = segment_rows[:, :, None] == segment_rows[:, None, :]
    earlier = jnp.arange(MB_ROWS)[None, :] <= jnp.arange(MB_ROWS)[:, None]
    allowed = same_doc & earlier[None]
    position = jnp.sum(allowed.astype(jnp.int32), axis=2) - 1
    frequency = jnp.exp(
        jnp.arange(ROTARY // 2, dtype=f32) * (-2.0 * math.log(10000.0) / ROTARY)
    )
    angles = position.astype(f32)[:, :, None] * frequency
    return allowed, jnp.cos(angles), jnp.sin(angles)


def rotate(heads_in, cosine, sine):
    half = ROTARY // 2
    first = heads_in[..., :half]
    second = heads_in[..., half : 2 * half]
    cos_rows = cosine[:, :, None, :]
    sin_rows = sine[:, :, None, :]
    return jnp.concatenate(
        [
            first * cos_rows - second * sin_rows,
            second * cos_rows + first * sin_rows,
            heads_in[..., 2 * half :],
        ],
        axis=-1,
    )


def dot(a, b, dims):
    return lax.dot_general(a, b, (dims, ((), ())), preferred_element_type=f32)


NN = ((1,), (0,))
NT = ((1,), (1,))
TN = ((0,), (0,))


def compute(tokens, cotangent, segment, qkv_w, out_w, up_w, down_w, small, core):
    count = tokens.shape[0]
    blocks = count // MB_ROWS
    rows32 = tokens.astype(f32)
    live = (segment >= 0).astype(f32)[:, None]
    qkv_b, up_b = small["qkvb"], small["upb"]
    share = jnp.where(core == 0, 1.0, 0.0)
    h1, scaled1, inverse1 = layer_norm(rows32, small["ln1g"], small["ln1b"])
    h2, scaled2, inverse2 = layer_norm(rows32, small["ln2g"], small["ln2b"])
    h1 = h1.astype(bf16)
    h2 = h2.astype(bf16)
    g = (cotangent.astype(f32) * live).astype(bf16)

    pre = dot(h2, up_w, NN) + up_b
    cumulative = 0.5 * (1.0 + lax.erf(pre * inv_sqrt_two))
    density = jnp.exp(-0.5 * pre * pre) * inv_sqrt_two_pi
    act = (pre * cumulative).astype(bf16)
    grad_down = dot(act, g, TN)
    grad_pre = (dot(g, down_w, NT) * (cumulative + pre * density)).astype(bf16)
    grad_up = dot(h2, grad_pre, TN)
    grad_up_b = jnp.sum(grad_pre.astype(f32), axis=0)
    grad_h2 = dot(grad_pre, up_w, NT)
    mlp = dot(act, down_w, NN)

    joint = dot(h1, qkv_w, NN) + qkv_b
    split = joint.reshape(blocks, MB_ROWS, 3, HH, HEAD_DIM)
    allowed, cosine, sine = tables(segment.reshape(blocks, MB_ROWS))
    q = rotate(split[:, :, 0], cosine, sine).astype(bf16)
    k = rotate(split[:, :, 1], cosine, sine).astype(bf16)
    v = split[:, :, 2].astype(bf16)
    scale = HEAD_DIM ** (-0.5)

    def ein(spec, a, b):
        return jnp.einsum(spec, a, b, preferred_element_type=f32)

    scores = jnp.where(allowed[:, None], ein("brhd,bshd->bhrs", q, k) * scale, masked_score)
    expd = jnp.exp(scores - jnp.max(scores, axis=-1, keepdims=True))
    probs = expd / jnp.sum(expd, axis=-1, keepdims=True)
    p = probs.astype(bf16)
    attn = ein("bhrs,bshd->brhd", p, v).reshape(count, HD).astype(bf16)
    attn_out = dot(attn, out_w, NN)
    grad_out = dot(attn, g, TN)
    grad_attn = dot(g, out_w, NT).astype(bf16).reshape(blocks, MB_ROWS, HH, HEAD_DIM)
    grad_p = ein("brhd,bshd->bhrs", grad_attn, v)
    grad_v = ein("bhrs,brhd->bshd", p, grad_attn)
    delta = jnp.sum(probs * grad_p, axis=-1, keepdims=True)
    ds = (probs * (grad_p - delta)).astype(bf16)
    grad_q = rotate(ein("bhrs,bshd->brhd", ds, k) * scale, cosine, -sine)
    grad_k = rotate(ein("bhrs,brhd->bshd", ds, q) * scale, cosine, -sine)
    grad_joint = jnp.stack([grad_q, grad_k, grad_v], axis=2).reshape(count, QW).astype(bf16)
    grad_qkv = dot(h1, grad_joint, TN)
    grad_qkv_b = jnp.sum(grad_joint.astype(f32), axis=0)
    grad_h1 = dot(grad_joint, qkv_w, NT)

    back1, gain1, shift1 = norm_back(grad_h1, scaled1, inverse1, small["ln1g"])
    back2, gain2, shift2 = norm_back(grad_h2, scaled2, inverse2, small["ln2g"])
    branch_sum = share * jnp.sum(g.astype(f32), axis=0)
    out_part = attn_out + mlp
    grad_part = back1 + back2
    grad_small = {
        "ln1g": gain1,
        "ln1b": shift1,
        "qkvb": grad_qkv_b,
        "outb": branch_sum,
        "ln2g": gain2,
        "ln2b": shift2,
        "upb": grad_up_b,
        "downb": branch_sum,
    }
    return out_part, grad_part, grad_qkv, grad_out, grad_up, grad_down, grad_small


def body(
    tokens,
    cotangent,
    segment,
    ln1_gain,
    ln1_bias,
    qkv_weight,
    qkv_bias,
    out_weight,
    out_bias,
    ln2_gain,
    ln2_bias,
    up_weight,
    up_bias,
    down_weight,
    down_bias,
):
    me = lax.axis_index("fsdp")
    core, z, y, x = me % 2, (me // 2) % 4, (me // 8) % 4, me // 32

    both_tokens = jnp.concatenate([tokens, swap(tokens)], axis=0)
    both_cot = jnp.concatenate([cotangent, swap(cotangent)], axis=0)
    both_segment = jnp.concatenate([segment, swap(segment)], axis=0)

    row = jnp.concatenate(
        [ln1_gain, ln1_bias, qkv_bias, out_bias, ln2_gain, ln2_bias, up_bias, down_bias]
    )
    extra = jnp.pad(row[None], ((0, 5), (0, 50)))

    def half_columns(which):
        q3 = lax.dynamic_index_in_dim(qkv_weight.reshape(6, 3, 2, HD), which, 2, keepdims=False)
        up = lax.dynamic_index_in_dim(up_weight.reshape(6, 2, HF), which, 1, keepdims=False)
        return jnp.concatenate([q3.reshape(6, QW), extra, up], axis=1)

    mine = half_columns(core)
    theirs = swap(half_columns(1 - core))
    pair = jnp.where(
        core == 0,
        jnp.concatenate([mine, theirs], axis=0),
        jnp.concatenate([theirs, mine], axis=0),
    )
    out_rows = permute(out_weight, OUT_PAIRS)
    out_rows = jnp.concatenate([out_rows[:, :HD], out_rows[:, HD:]], axis=0)
    down_rows = permute(down_weight, DOWN_PAIRS)
    pair = jnp.concatenate([out_rows, pair], axis=1)
    CUT = HD + QW + 128

    joint1 = ring_gather(pair, "z", z).reshape(48, CUT + HF)
    down1 = ring_gather(down_rows, "y", y).reshape(96, D)
    q2 = ring_gather(joint1[:, :CUT], "x", x)
    up2 = ring_gather(joint1[:, CUT:], "y", y).reshape(192, HF)
    down2 = ring_gather(down1, "x", x).reshape(384, D)
    q3 = ring_gather(q2, "y", y).transpose(1, 0, 2, 3).reshape(D, CUT)
    up_w = ring_gather(up2, "x", x).reshape(D, HF)
    down_w = ring_gather(down2, "z", z).reshape(HF, D)
    out_w = q3[:, :HD].reshape(64, 2, 6, HD).transpose(0, 2, 1, 3).reshape(HD, D)
    qkv_w = q3[:, HD : HD + QW]
    table = q3[:, HD + QW :].reshape(128, 6, 128)[:, 0].astype(f32)

    small = {}
    at = 0
    for name, width in SMALL:
        small[name] = table[:, at : at + width].reshape(128 * width)
        at += width
    small["qkvb"] = lax.dynamic_index_in_dim(
        small["qkvb"].reshape(3, 2, HD), core, 1, keepdims=False
    ).reshape(QW)
    small["upb"] = lax.dynamic_slice(small["upb"], (core * HF,), (HF,))

    out_part, grad_part, grad_qkv, grad_out, grad_up, grad_down, grad_small = compute(
        both_tokens, both_cot, both_segment, qkv_w, out_w, up_w, down_w, small, core
    )

    wide = jnp.zeros((3, 2, HD), f32)
    wide = lax.dynamic_update_slice(wide, grad_small["qkvb"].reshape(3, 1, HD), (0, core, 0))
    grad_small["qkvb"] = wide.reshape(3 * D)
    grad_small["upb"] = lax.dynamic_update_slice(
        jnp.zeros((FF,), f32), grad_small["upb"], (core * HF,)
    )
    table = jnp.concatenate(
        [grad_small[name].reshape(128, width) for name, width in SMALL], axis=1
    )
    table = jnp.pad(table[:, None, :], ((0, 0), (0, 5), (0, 50))).reshape(D, 128)
    grad_out = grad_out.reshape(64, 6, 2, HD).transpose(0, 2, 1, 3).reshape(D, HD)
    q3 = jnp.concatenate([grad_out, grad_qkv, table], axis=1)

    down2 = ring_reduce(grad_down.reshape(4, 384, D), "z", z)
    up2 = ring_reduce(grad_up.reshape(4, 192, HF), "x", x)
    q2 = ring_reduce(q3.reshape(4, 4, 48, CUT).transpose(1, 0, 2, 3), "y", y)
    down1 = ring_reduce(down2.reshape(4, 96, D), "x", x)
    up1 = ring_reduce(up2.reshape(4, 48, HF), "y", y)
    q1 = ring_reduce(q2, "x", x)
    down_rows = ring_reduce(down1.reshape(4, 24, D), "y", y)
    joint = ring_reduce(jnp.concatenate([q1, up1], axis=1).reshape(4, 12, CUT + HF), "z", z)

    own_down = permute(down_rows, DOWN_BACK)
    out_rows = jnp.concatenate([joint[:6, :HD], joint[6:, :HD]], axis=1)
    own_out = permute(out_rows, OUT_BACK)
    rows = joint[:, HD:].reshape(2, 6, QW + 128 + HF)
    mine = lax.dynamic_index_in_dim(rows, core, 0, keepdims=False)
    theirs = swap(lax.dynamic_index_in_dim(rows, 1 - core, 0, keepdims=False))
    low = jnp.where(core == 0, mine, theirs)
    high = jnp.where(core == 0, theirs, mine)
    own_qkv = jnp.stack(
        [low[:, :QW].reshape(6, 3, HD), high[:, :QW].reshape(6, 3, HD)], axis=2
    ).reshape(6, 3 * D)
    own_up = jnp.concatenate([low[:, QW + 128 :], high[:, QW + 128 :]], axis=1)
    line = (low + high)[0, QW : QW + 128]
    own = {}
    at = 0
    for name, width in SMALL:
        own[name] = line[at : at + width]
        at += width

    live = (segment >= 0).astype(f32)[:, None]
    out_sum = out_part[:ROWS] + swap(out_part[ROWS:])
    out_sum = out_sum + small["outb"] + small["downb"]
    output = (tokens.astype(f32) + live * out_sum).astype(bf16)
    grad_tokens = cotangent.astype(f32) + (grad_part[:ROWS] + swap(grad_part[ROWS:]))
    return (
        output,
        grad_tokens,
        own["ln1g"],
        own["ln1b"],
        own_qkv,
        own["qkvb"],
        own_out,
        own["outb"],
        own["ln2g"],
        own["ln2b"],
        own_up,
        own["upb"],
        own_down,
        own["downb"],
    )


def solution(mesh):
    row = P("fsdp", None)
    flat = P("fsdp")
    return jax.shard_map(
        body,
        mesh=mesh,
        in_specs=(
            row, row, flat, flat, flat, row, flat, row, flat, flat, flat, row, flat, row, flat,
        ),
        out_specs=(
            row, row, flat, flat, row, flat, row, flat, flat, flat, row, flat, row, flat,
        ),
        check_vma=False,
    )
```

```python
import math

import jax
import jax.numpy as jnp
from jax import lax
from jax.experimental import pallas as pl
from jax.experimental.pallas import tpu as pltpu
from jax.sharding import PartitionSpec as P

D = 768
HEADS = 12
HEAD_DIM = 64
ROTARY = 16
FF = 3072
MB_ROWS = 128
ROWS = 256
HH = HEADS // 2
HD = D // 2
HF = FF // 2
QW = 3 * HD

epsilon = 1e-05
masked_score = -1e30
inv_sqrt_two = 1.0 / math.sqrt(2.0)
inv_sqrt_two_pi = 1.0 / math.sqrt(2.0 * math.pi)
bf16 = jnp.bfloat16
f32 = jnp.float32

STRIDE = {"x": 32, "y": 8, "z": 2, "c": 1}
SIZE = {"x": 4, "y": 4, "z": 4, "c": 2}
SMALL = (("ln1g", 6), ("ln1b", 6), ("qkvb", 18), ("outb", 6), ("ln2g", 6), ("ln2b", 6), ("upb", 24), ("downb", 6))


def digit(index, axis):
    return (index // STRIDE[axis]) % SIZE[axis]


def shift(axis, step):
    pairs = []
    for source in range(128):
        at = digit(source, axis)
        target = source + ((at + step) % SIZE[axis] - at) * STRIDE[axis]
        pairs.append((source, target))
    return pairs


def down_target(source):
    half, block = source // 64, source % 64
    z, x, y = block // 16, (block // 4) % 4, block % 4
    return ((x * 4 + y) * 4 + z) * 2 + half


def out_target(source):
    return 2 * (source % 64) + source // 64


OUT_PAIRS = [(s, out_target(s)) for s in range(128)]
DOWN_PAIRS = [(s, down_target(s)) for s in range(128)]
OUT_BACK = [(t, s) for s, t in OUT_PAIRS]
DOWN_BACK = [(t, s) for s, t in DOWN_PAIRS]


def permute(values, pairs):
    return lax.ppermute(values, "fsdp", pairs)


def swap(values):
    return permute(values, shift("c", 1))


def ring_gather(block, axis, at):
    pieces = (
        block,
        permute(block, shift(axis, -1)),
        permute(block, shift(axis, 2)),
        permute(block, shift(axis, 1)),
    )
    whole = jnp.zeros((4,) + block.shape, block.dtype)
    for step, piece in enumerate(pieces):
        whole = lax.dynamic_update_index_in_dim(whole, piece, (at + step) % 4, 0)
    return whole


def ring_sum(parts, axis):
    own, after, across, before = parts
    arrived = (
        permute(across.astype(bf16), shift(axis, 2)),
        permute(after.astype(bf16), shift(axis, 1)),
        permute(before.astype(bf16), shift(axis, -1)),
    )
    total = own.astype(f32)
    for piece in arrived:
        total = total + piece.astype(f32)
    return total


def ring_reduce(blocks, axis, at):
    parts = [
        lax.dynamic_index_in_dim(blocks, (at + step) % 4, 0, keepdims=False) for step in range(4)
    ]
    return ring_sum(parts, axis)


CUT = HD + QW + 128

def dot(a, b, dims):
    return lax.dot_general(a, b, (dims, ((), ())), preferred_element_type=f32)


NN = ((1,), (0,))
NT = ((1,), (1,))
TN = ((0,), (0,))
ALL = 2 * ROWS
BLOCKS = ALL // MB_ROWS
WIDE = 6 * D + QW + HF
VMEM = pl.BlockSpec(memory_space=pltpu.VMEM)
SMEM = pl.BlockSpec(memory_space=pltpu.SMEM)


def struct(shape, kind):
    return jax.ShapeDtypeStruct(shape, kind)


def spot(name):
    at = 0
    for key, width in SMALL:
        span = QW if key == "qkvb" else HF if key == "upb" else 128 * width
        if key == name:
            return slice(at, at + span)
        at += span


def small_maps(core):
    device, lane = [], []
    at = 0
    for key, width in SMALL:
        if key == "qkvb":
            flat = (jnp.arange(3)[:, None] * D + core * HD + jnp.arange(HD)[None]).reshape(QW)
        elif key == "upb":
            flat = core * HF + jnp.arange(HF)
        else:
            flat = jnp.arange(128 * width)
        device.append(flat // width)
        lane.append(at + flat % width)
        at += width
    return jnp.stack([jnp.concatenate(device), jnp.concatenate(lane)]).astype(jnp.int32)


def small_kernel(extra_ref, maps_ref, rows_ref):
    pick = lax.broadcasted_iota(jnp.int32, (128, D), 1) == 6 * lax.broadcasted_iota(
        jnp.int32, (128, D), 0
    )
    table = dot(pick.astype(f32).astype(bf16), extra_ref[...], NN).astype(bf16)
    step = 2432
    for at in range(0, WIDE, step):
        index = lax.broadcasted_iota(jnp.int32, (128, step), 0)
        hot = (index == maps_ref[1:2, at : at + step]).astype(f32).astype(bf16)
        spread = dot(table, hot, NN)
        held = jnp.where(index == maps_ref[0:1, at : at + step], spread, 0.0)
        rows_ref[:, at : at + step] = jnp.sum(held, axis=0, keepdims=True)


def read_small(extra, maps):
    return pl.pallas_call(
        small_kernel,
        out_shape=struct((1, WIDE), f32),
        in_specs=[VMEM, VMEM],
        out_specs=VMEM,
        compiler_params=pltpu.CompilerParams(vmem_limit_bytes=40 << 20),
    )(extra, maps)


def norm_back(upstream, scaled, inverse, gain):
    weighted = upstream * gain
    middle = jnp.mean(weighted, axis=-1, keepdims=True)
    slope = jnp.mean(weighted * scaled, axis=-1, keepdims=True)
    grad_in = inverse * (weighted - middle - scaled * slope)
    gain_sum = jnp.sum(upstream * scaled, axis=0, keepdims=True)
    return grad_in, gain_sum, jnp.sum(upstream, axis=0, keepdims=True)


def mlp_kernel(
    at_ref, scaled_ref, inverse_ref, g_ref, up_ref, down_ref, rows_ref,
    mlp_ref, back_ref, sums_ref, d0, d1, d2, d3, u0, u1, u2, u3,
    h_s, ht_s, act_s, gp_s, gh_s,
):
    x, z = at_ref[0], at_ref[2]
    gain = rows_ref[:, spot("ln2g")]
    h = scaled_ref[...] * gain + rows_ref[:, spot("ln2b")]
    h_s[...] = h.astype(bf16)
    ht_s[...] = h.T.astype(bf16)
    step = 384
    first = spot("upb").start
    for at in range(0, HF, step):
        cut = slice(at, at + step)
        pre = dot(h_s[...], up_ref[:, cut], NN) + rows_ref[:, first + at : first + at + step]
        cumulative = 0.5 * (1.0 + lax.erf(pre * inv_sqrt_two))
        density = jnp.exp(-0.5 * pre * pre) * inv_sqrt_two_pi
        act_s[:, cut] = (pre * cumulative).astype(bf16)
        grad_act = dot(g_ref[...], down_ref[cut, :], NT)
        grad_pre = (grad_act * (cumulative + pre * density)).astype(bf16)
        gp_s[:, cut] = grad_pre
        sums_ref[0:1, cut] = jnp.sum(grad_pre.astype(f32), axis=0, keepdims=True)
    for rel, ref in enumerate((d0, d1, d2, d3)):
        begin = pl.multiple_of(384 * lax.rem(z + rel, 4), 128)
        ref[...] = dot(act_s[:, pl.ds(begin, 384)], g_ref[...], TN).astype(bf16)
    for rel, ref in enumerate((u0, u1, u2, u3)):
        begin = pl.multiple_of(192 * lax.rem(x + rel, 4), 64)
        ref[...] = dot(ht_s[pl.ds(begin, 192), :], gp_s[...], NN).astype(bf16)
    mlp_ref[...] = dot(act_s[...], down_ref[...], NN)
    gh_s[...] = dot(gp_s[...], up_ref[...], NT)
    back, gain_sum, shift_sum = norm_back(gh_s[...], scaled_ref[...], inverse_ref[...], gain)
    back_ref[...] = back
    sums_ref[1:2, :D] = gain_sum
    sums_ref[2:3, :D] = shift_sum
    sums_ref[3:4, :D] = jnp.sum(g_ref[:ROWS, :].astype(f32), axis=0, keepdims=True)


def run_mlp(at, scaled, inverse, g, up_w, down_w, rows):
    return pl.pallas_call(
        mlp_kernel,
        out_shape=(
            struct((ALL, D), f32),
            struct((ALL, D), f32),
            struct((8, HF), f32),
        )
        + (struct((384, D), bf16),) * 4
        + (struct((192, HF), bf16),) * 4,
        in_specs=[SMEM] + [VMEM] * 6,
        out_specs=(VMEM,) * 11,
        scratch_shapes=[
            pltpu.VMEM((ALL, D), bf16),
            pltpu.VMEM((D, ALL), bf16),
            pltpu.VMEM((ALL, HF), bf16),
            pltpu.VMEM((ALL, HF), bf16),
            pltpu.VMEM((ALL, D), f32),
        ],
        compiler_params=pltpu.CompilerParams(vmem_limit_bytes=44 << 20),
        cost_estimate=pl.CostEstimate(
            flops=6 * 2 * ALL * D * HF, bytes_accessed=20 << 20, transcendentals=2 * ALL * HF
        ),
    )(at, scaled, inverse, g, up_w, down_w, rows)


def turn(values, cosine, sine_a, sine_b):
    parts = []
    for at in range(0, values.shape[1], 128):
        part = values[:, at : at + 128]
        parts.append(
            part * cosine
            + pltpu.roll(part, 120, 1) * sine_a
            + pltpu.roll(part, 8, 1) * sine_b
        )
    return jnp.concatenate(parts, axis=1) if len(parts) > 1 else parts[0]


def attention_kernel(
    at_ref, scaled_ref, inverse_ref, g_ref, q3_ref, rows_ref, cos_ref, sina_ref, sinb_ref,
    bias_ref, left_ref, right_ref, scramble_ref, spread_ref, maps_ref, sums_ref, mlp_ref, back2_ref,
    out0, out1, grad0, grad1, b0, b1, b2, b3,
    h_s, ht_s, hp_s, ow_s, q_s, k_s, v_s, ga_s, attn_s, gj_s, gh_s, sa_s,
):
    y = at_ref[1]
    gain = rows_ref[:, spot("ln1g")]
    h = scaled_ref[...] * gain + rows_ref[:, spot("ln1b")]
    h_s[...] = h.astype(bf16)
    ht_s[...] = h.T.astype(bf16)
    for rel in range(4):
        for xx in range(4):
            begin = pl.multiple_of(48 * (4 * xx + lax.rem(y + rel, 4)), 16)
            to = (rel * 4 + xx) * 48
            hp_s[to : to + 48, :] = ht_s[pl.ds(begin, 48), :]
    ow_s[:, :HD] = dot(left_ref[...], q3_ref[:, :HD], TN).astype(bf16)
    ow_s[:, HD:] = dot(right_ref[...], q3_ref[:, :HD], TN).astype(bf16)
    first = spot("qkvb").start
    cosine, sine_a, sine_b = cos_ref[...], sina_ref[...], sinb_ref[...]
    for part, ref in enumerate((q_s, k_s, v_s)):
        cut = slice(HD + part * HD, 2 * HD + part * HD)
        bias = rows_ref[:, first + part * HD : first + (part + 1) * HD]
        joint = dot(h_s[...], q3_ref[:, cut], NN) + bias
        if part < 2:
            joint = turn(joint, cosine, sine_a, sine_b)
        ref[...] = joint.astype(bf16)
    ga_s[...] = dot(g_ref[...], ow_s[...], NT).astype(bf16)

    scale = HEAD_DIM ** (-0.5)
    lanes = lax.broadcasted_iota(jnp.int32, (MB_ROWS, 128), 1) < HEAD_DIM
    low = lanes.astype(f32).astype(bf16)
    high = (1.0 - lanes.astype(f32)).astype(bf16)

    def one_block(block, carry):
        rs = pl.ds(pl.multiple_of(block * MB_ROWS, MB_ROWS), MB_ROWS)
        bias = bias_ref[rs, :]
        bias = jnp.concatenate([bias, bias], axis=0)
        turn_c, turn_a, turn_b = cos_ref[rs, :], -sina_ref[rs, :], -sinb_ref[rs, :]
        for pair in range(HH // 2):
            cs = slice(pair * 128, pair * 128 + 128)
            qp, kp, vp, ga = q_s[rs, cs], k_s[rs, cs], v_s[rs, cs], ga_s[rs, cs]
            qm = jnp.concatenate([qp * low, qp * high], axis=0)
            gm = jnp.concatenate([ga * low, ga * high], axis=0)
            scores = dot(qm, kp, NT) * scale + bias
            expd = jnp.exp(scores - jnp.max(scores, axis=-1, keepdims=True))
            probs = expd / jnp.sum(expd, axis=-1, keepdims=True)
            p = probs.astype(bf16)
            mixed = dot(p, vp, NN)
            attn_s[rs, cs] = jnp.where(lanes, mixed[:MB_ROWS], mixed[MB_ROWS:]).astype(bf16)
            grad_p = dot(gm, vp, NT)
            grad_v = dot(p, gm, TN)
            delta = jnp.sum(probs * grad_p, axis=-1, keepdims=True)
            ds = (probs * (grad_p - delta)).astype(bf16)
            both = dot(ds, kp, NN)
            grad_q = jnp.where(lanes, both[:MB_ROWS], both[MB_ROWS:]) * scale
            grad_k = dot(ds, qm, TN) * scale
            gj_s[rs, cs] = turn(grad_q, turn_c, turn_a, turn_b).astype(bf16)
            ck = slice(HD + pair * 128, HD + pair * 128 + 128)
            cv = slice(2 * HD + pair * 128, 2 * HD + pair * 128 + 128)
            gj_s[rs, ck] = turn(grad_k, turn_c, turn_a, turn_b).astype(bf16)
            gj_s[rs, cv] = grad_v.astype(bf16)
        return carry

    lax.fori_loop(0, BLOCKS, one_block, 0)

    sa_s[...] = dot(scramble_ref[...], attn_s[...], NT).astype(bf16)
    gh_s[...] = dot(gj_s[...], q3_ref[:, HD : HD + QW], NT)
    back, gain_sum, shift_sum = norm_back(gh_s[...], scaled_ref[...], inverse_ref[...], gain)
    back = back + back2_ref[...]
    grad0[...] = back[:ROWS]
    grad1[...] = back[ROWS:]
    part = mlp_ref[...] + dot(attn_s[...], ow_s[...], NN)
    out0[...] = part[:ROWS]
    out1[...] = part[ROWS:]

    branch = sums_ref[3:4, :D]
    joint_sum = jnp.sum(gj_s[...].astype(f32), axis=0, keepdims=True)
    values = {
        "ln1g": gain_sum,
        "ln1b": shift_sum,
        "qkvb": joint_sum,
        "outb": branch,
        "ln2g": sums_ref[1:2, :D],
        "ln2b": sums_ref[2:3, :D],
        "upb": sums_ref[0:1, :],
        "downb": branch,
    }
    table = jnp.zeros((128, 128), f32)
    for key, _ in SMALL:
        span = spot(key)
        index = lax.broadcasted_iota(jnp.int32, (128, span.stop - span.start), 0)
        hot = (index == maps_ref[1:2, span]).astype(f32).astype(bf16)
        held = jnp.where(index == maps_ref[0:1, span], values[key], 0.0).astype(bf16)
        table = table + dot(held, hot, NT)
    table = table.astype(bf16)
    for rel, ref in enumerate((b0, b1, b2, b3)):
        rs = slice(rel * 192, rel * 192 + 192)
        one = dot(sa_s[rs, :], g_ref[:, :HD], NN)
        two = dot(sa_s[rs, :], g_ref[:, HD:], NN)
        pick = spread_ref[rs, 128:129].astype(f32) > 0.5
        ref[:, :HD] = jnp.where(pick, two, one).astype(bf16)
        ref[:, HD : HD + QW] = dot(hp_s[rs, :], gj_s[...], NN).astype(bf16)
        ref[:, HD + QW :] = dot(spread_ref[rs, :128], table, NN).astype(bf16)


def run_attention(*operands):
    half = (struct((ROWS, D), f32),) * 4
    return pl.pallas_call(
        attention_kernel,
        out_shape=half + (struct((192, CUT), bf16),) * 4,
        in_specs=[SMEM] + [VMEM] * (len(operands) - 1),
        out_specs=(VMEM,) * 8,
        scratch_shapes=[
            pltpu.VMEM((ALL, D), bf16),
            pltpu.VMEM((D, ALL), bf16),
            pltpu.VMEM((D, ALL), bf16),
            pltpu.VMEM((HD, D), bf16),
            pltpu.VMEM((ALL, HD), bf16),
            pltpu.VMEM((ALL, HD), bf16),
            pltpu.VMEM((ALL, HD), bf16),
            pltpu.VMEM((ALL, HD), bf16),
            pltpu.VMEM((ALL, HD), bf16),
            pltpu.VMEM((ALL, QW), bf16),
            pltpu.VMEM((ALL, D), f32),
            pltpu.VMEM((D, ALL), bf16),
        ],
        compiler_params=pltpu.CompilerParams(vmem_limit_bytes=44 << 20),
        cost_estimate=pl.CostEstimate(
            flops=6 * 2 * ALL * D * (QW + HD), bytes_accessed=20 << 20, transcendentals=ALL * 128 * HH
        ),
    )(*operands)


def prepare(tokens, cotangent, segment):
    rows32 = tokens.astype(f32)
    centred = rows32 - jnp.mean(rows32, axis=-1, keepdims=True)
    inverse = lax.rsqrt(jnp.mean(centred * centred, axis=-1, keepdims=True) + epsilon)
    live = (segment >= 0).astype(f32)[:, None]
    g = (cotangent.astype(f32) * live).astype(bf16)
    blocks = segment.reshape(BLOCKS, MB_ROWS)
    same = blocks[:, :, None] == blocks[:, None, :]
    earlier = jnp.arange(MB_ROWS)[None, :] <= jnp.arange(MB_ROWS)[:, None]
    allowed = (same & earlier[None]).reshape(ALL, MB_ROWS)
    bias = jnp.where(allowed, 0.0, masked_score)
    place = (jnp.sum(allowed.astype(jnp.int32), axis=1) - 1).astype(f32)
    lane = jnp.arange(128) % HEAD_DIM
    frequency = jnp.exp(
        (lane % 8).astype(f32) * (-2.0 * math.log(10000.0) / ROTARY)
    )
    angle = place[:, None] * frequency[None, :]
    cosine = jnp.where(lane < 16, jnp.cos(angle), 1.0)
    sine = jnp.sin(angle)
    sine_a = jnp.where(lane < 8, -sine, 0.0)
    sine_b = jnp.where((lane >= 8) & (lane < 16), sine, 0.0)
    return centred * inverse, inverse, g, cosine, sine_a, sine_b, bias


def row_maps(y):
    natural = jnp.arange(D)
    rel = natural // 192
    order = ((natural % 192) // 48 * 4 + (y + rel) % 4) * 48 + natural % 48
    columns = jnp.arange(HD)[None]
    target = natural // 12 * 6 + natural % 6
    half = (natural % 12) // 6
    left = ((target[:, None] == columns) & (half[:, None] == 0)).astype(bf16)
    right = ((target[:, None] == columns) & (half[:, None] == 1)).astype(bf16)
    wanted = order // 12 * 6 + order % 6
    scramble = (wanted[:, None] == columns).astype(bf16)
    device = jnp.arange(128)[None]
    spread = (order[:, None] == 6 * device).astype(bf16)
    side = jnp.broadcast_to(((order % 12) // 6).astype(bf16)[:, None], (D, 128))
    return left, right, scramble, jnp.concatenate([spread, side], axis=1)


def body(
    tokens,
    cotangent,
    segment,
    ln1_gain,
    ln1_bias,
    qkv_weight,
    qkv_bias,
    out_weight,
    out_bias,
    ln2_gain,
    ln2_bias,
    up_weight,
    up_bias,
    down_weight,
    down_bias,
):
    me = lax.axis_index("fsdp")
    core, z, y, x = me % 2, (me // 2) % 4, (me // 8) % 4, me // 32

    both_tokens = jnp.concatenate([tokens, swap(tokens)], axis=0)
    both_cot = jnp.concatenate([cotangent, swap(cotangent)], axis=0)
    both_segment = jnp.concatenate([segment, swap(segment)], axis=0)
    scaled, inverse, g, cosine, sine_a, sine_b, bias = prepare(
        both_tokens, both_cot, both_segment
    )
    at = jnp.stack([x, y, z, core]).astype(jnp.int32)
    maps = small_maps(core)
    left, right, scramble, spread = row_maps(y)

    row = jnp.concatenate(
        [ln1_gain, ln1_bias, qkv_bias, out_bias, ln2_gain, ln2_bias, up_bias, down_bias]
    )
    extra = jnp.pad(row[None], ((0, 5), (0, 50)))

    def half_columns(which):
        q3 = lax.dynamic_index_in_dim(qkv_weight.reshape(6, 3, 2, HD), which, 2, keepdims=False)
        up = lax.dynamic_index_in_dim(up_weight.reshape(6, 2, HF), which, 1, keepdims=False)
        return jnp.concatenate([q3.reshape(6, QW), extra, up], axis=1)

    mine = half_columns(core)
    theirs = swap(half_columns(1 - core))
    pair = jnp.where(
        core == 0,
        jnp.concatenate([mine, theirs], axis=0),
        jnp.concatenate([theirs, mine], axis=0),
    )
    out_rows = permute(out_weight, OUT_PAIRS)
    out_rows = jnp.concatenate([out_rows[:, :HD], out_rows[:, HD:]], axis=0)
    down_rows = permute(down_weight, DOWN_PAIRS)
    pair = jnp.concatenate([out_rows, pair], axis=1)

    joint1 = ring_gather(pair, "z", z).reshape(48, CUT + HF)
    down1 = ring_gather(down_rows, "y", y).reshape(96, D)
    q2 = ring_gather(joint1[:, :CUT], "x", x)
    up2 = ring_gather(joint1[:, CUT:], "y", y).reshape(192, HF)
    down2 = ring_gather(down1, "x", x).reshape(384, D)
    q3 = ring_gather(q2, "y", y).transpose(1, 0, 2, 3).reshape(D, CUT)
    up_w = ring_gather(up2, "x", x).reshape(D, HF)
    down_w = ring_gather(down2, "z", z).reshape(HF, D)
    vectors = read_small(q3[:, HD + QW :], maps)
    mlp, back2, sums, d0, d1, d2, d3, u0, u1, u2, u3 = run_mlp(
        at, scaled, inverse, g, up_w, down_w, vectors
    )
    out0, out1, grad0, grad1, b0, b1, b2, b3 = run_attention(
        at, scaled, inverse, g, q3, vectors, cosine, sine_a, sine_b, bias,
        left, right, scramble, spread, maps, sums, mlp, back2,
    )

    down2 = ring_sum((d0, d1, d2, d3), "z")
    up2 = ring_sum((u0, u1, u2, u3), "x")
    q2 = ring_sum((b0, b1, b2, b3), "y").reshape(4, 48, CUT)
    down1 = ring_reduce(down2.reshape(4, 96, D), "x", x)
    up1 = ring_reduce(up2.reshape(4, 48, HF), "y", y)
    q1 = ring_reduce(q2, "x", x)
    down_rows = ring_reduce(down1.reshape(4, 24, D), "y", y)
    joint = ring_reduce(jnp.concatenate([q1, up1], axis=1).reshape(4, 12, CUT + HF), "z", z)

    own_down = permute(down_rows, DOWN_BACK)
    out_rows = jnp.concatenate([joint[:6, :HD], joint[6:, :HD]], axis=1)
    own_out = permute(out_rows, OUT_BACK)
    rows = joint[:, HD:].reshape(2, 6, QW + 128 + HF)
    mine = lax.dynamic_index_in_dim(rows, core, 0, keepdims=False)
    theirs = swap(lax.dynamic_index_in_dim(rows, 1 - core, 0, keepdims=False))
    low = jnp.where(core == 0, mine, theirs)
    high = jnp.where(core == 0, theirs, mine)
    own_qkv = jnp.stack(
        [low[:, :QW].reshape(6, 3, HD), high[:, :QW].reshape(6, 3, HD)], axis=2
    ).reshape(6, 3 * D)
    own_up = jnp.concatenate([low[:, QW + 128 :], high[:, QW + 128 :]], axis=1)
    line = (low + high)[0, QW : QW + 128]
    own = {}
    at = 0
    for name, width in SMALL:
        own[name] = line[at : at + width]
        at += width

    live = (segment >= 0).astype(f32)[:, None]
    out_sum = out0 + swap(out1) + vectors[:, spot("outb")] + vectors[:, spot("downb")]
    output = (tokens.astype(f32) + live * out_sum).astype(bf16)
    grad_tokens = cotangent.astype(f32) + (grad0 + swap(grad1))
    return (
        output,
        grad_tokens,
        own["ln1g"],
        own["ln1b"],
        own_qkv,
        own["qkvb"],
        own_out,
        own["outb"],
        own["ln2g"],
        own["ln2b"],
        own_up,
        own["upb"],
        own_down,
        own["downb"],
    )


def solution(mesh):
    row = P("fsdp", None)
    flat = P("fsdp")
    return jax.shard_map(
        body,
        mesh=mesh,
        in_specs=(
            row, row, flat, flat, flat, row, flat, row, flat, flat, flat, row, flat, row, flat,
        ),
        out_specs=(
            row, row, flat, flat, row, flat, row, flat, flat, flat, row, flat, row, flat,
        ),
        check_vma=False,
    )
```

```python
import math

import jax
import jax.numpy as jnp
from jax import lax
from jax.experimental import pallas as pl
from jax.experimental.pallas import tpu as pltpu
from jax.sharding import PartitionSpec as P

D = 768
HEADS = 12
HEAD_DIM = 64
ROTARY = 16
FF = 3072
MB_ROWS = 128
ROWS = 256
HH = HEADS // 2
HD = D // 2
HF = FF // 2
QW = 3 * HD

epsilon = 1e-05
masked_score = -1e30
inv_sqrt_two = 1.0 / math.sqrt(2.0)
inv_sqrt_two_pi = 1.0 / math.sqrt(2.0 * math.pi)
bf16 = jnp.bfloat16
f32 = jnp.float32

STRIDE = {"x": 32, "y": 8, "z": 2, "c": 1}
SIZE = {"x": 4, "y": 4, "z": 4, "c": 2}
SMALL = (("ln1g", 6), ("ln1b", 6), ("qkvb", 18), ("outb", 6), ("ln2g", 6), ("ln2b", 6), ("upb", 24), ("downb", 6))


def digit(index, axis):
    return (index // STRIDE[axis]) % SIZE[axis]


ORDER = (("x", "z", "y"), ("z", "x", "y"))


def shift(axis, step):
    pairs = []
    for source in range(128):
        at = digit(source, axis)
        target = source + ((at + step) % SIZE[axis] - at) * STRIDE[axis]
        pairs.append((source, target))
    return pairs


def stage_shift(stage, step):
    pairs = []
    for source in range(128):
        axis = ORDER[source % 2][stage]
        at = digit(source, axis)
        pairs.append((source, source + ((at + step) % 4 - at) * STRIDE[axis]))
    return pairs


def holder(half, block):
    digits = (block // 16, (block // 4) % 4, block % 4)
    return half + sum(STRIDE[axis] * at for axis, at in zip(ORDER[half], digits))


ROW_PAIRS = [
    (holder(half, block), 64 * half + block) for half in range(2) for block in range(64)
]


def permute(values, pairs):
    return lax.ppermute(values, "fsdp", pairs)


def swap(values):
    return permute(values, shift("c", 1))


def exchange(parts, stage):
    _, after, across, before = parts
    return (
        permute(after, stage_shift(stage, 1)),
        permute(before, stage_shift(stage, -1)),
        permute(across, stage_shift(stage, 2)),
    )


def added(own, arrived):
    total = own.astype(f32)
    for piece in arrived:
        total = total + piece.astype(f32)
    return total


def sum_kernel(at_ref, own_ref, one_ref, two_ref, three_ref, own_out, *outs):
    refs = (own_ref, one_ref, two_ref, three_ref)
    for rel in range(4):
        rs = pl.ds(pl.multiple_of(48 * lax.rem(at_ref[1] + rel, 4), 16), 48)
        total = added(own_ref[rs, :], [ref[rs, :] for ref in refs[1:]])
        if rel == 0:
            own_out[...] = total
        else:
            outs[rel - 1][...] = total.astype(bf16)


def sum_first(at, own, arrived):
    width = own.shape[1]
    return pl.pallas_call(
        sum_kernel,
        out_shape=(struct((48, width), f32),) + (struct((48, width), bf16),) * 3,
        in_specs=[SMEM] + [VMEM] * 4,
        out_specs=(VMEM,) * 4,
        compiler_params=pltpu.CompilerParams(vmem_limit_bytes=24 << 20),
        cost_estimate=pl.CostEstimate(
            flops=4 * 192 * width, bytes_accessed=10 * 192 * width, transcendentals=0
        ),
    )(at, own, *arrived)


CUT = HD + QW + 128
HALF = QW + HF
OUT_AT = 2 * HALF
EXTRA_AT = OUT_AT + D
DOWN_AT = EXTRA_AT + 128
PACK = DOWN_AT + 3 * D

def dot(a, b, dims):
    return lax.dot_general(a, b, (dims, ((), ())), preferred_element_type=f32)


NN = ((1,), (0,))
NT = ((1,), (1,))
TN = ((0,), (0,))
ALL = 2 * ROWS
BLOCKS = ALL // MB_ROWS
WIDE = 6 * D + QW + HF
VMEM = pl.BlockSpec(memory_space=pltpu.VMEM)
SMEM = pl.BlockSpec(memory_space=pltpu.SMEM)
ANY = pl.BlockSpec(memory_space=pl.ANY)


def struct(shape, kind):
    return jax.ShapeDtypeStruct(shape, kind)


def spot(name):
    at = 0
    for key, width in SMALL:
        span = QW if key == "qkvb" else HF if key == "upb" else 128 * width
        if key == name:
            return slice(at, at + span)
        at += span


def small_maps(core):
    device, lane = [], []
    at = 0
    for key, width in SMALL:
        if key == "qkvb":
            flat = (jnp.arange(3)[:, None] * D + core * HD + jnp.arange(HD)[None]).reshape(QW)
        elif key == "upb":
            flat = core * HF + jnp.arange(HF)
        else:
            flat = jnp.arange(128 * width)
        device.append(flat // width)
        lane.append(at + flat % width)
        at += width
    return jnp.stack([jnp.concatenate(device), jnp.concatenate(lane)]).astype(jnp.int32)


def pack_kernel(qkv_ref, out_ref, up_ref, extra_ref, down_ref, to_ref):
    to_ref[...] = jnp.zeros((8, PACK), bf16)
    for half in range(2):
        base = half * HALF
        for part in range(3):
            at = part * D + half * HD
            to_ref[0:6, base + part * HD : base + (part + 1) * HD] = qkv_ref[:, at : at + HD]
        to_ref[0:6, base + QW : base + HALF] = up_ref[:, half * HF : (half + 1) * HF]
    to_ref[0:6, OUT_AT : OUT_AT + D] = out_ref[...]
    to_ref[0:1, EXTRA_AT : EXTRA_AT + 128] = extra_ref[...]
    for part in range(3):
        at = DOWN_AT + part * D
        to_ref[:, at : at + D] = down_ref[part * 8 : part * 8 + 8, :]


def pack_weights(qkv, out, up, extra, down):
    return pl.pallas_call(
        pack_kernel,
        out_shape=struct((8, PACK), bf16),
        in_specs=[VMEM] * 5,
        out_specs=VMEM,
    )(qkv, out, up, extra, down)


def one_hot(condition):
    return condition.astype(f32).astype(bf16)


def columns(at, width):
    return pl.ds(pl.multiple_of(at, 128), width)


def compact(source, target, groups):
    row = lax.broadcasted_iota(jnp.int32, (192, 256), 0)
    column = lax.broadcasted_iota(jnp.int32, (192, 256), 1)
    device, inner = column >> 3, column & 7
    pick = one_hot((row == device * 6 + inner) & (inner < 6))
    for group in range(groups):
        block = source[group * 256 : group * 256 + 256, :]
        target[group * 192 : group * 192 + 192, :] = dot(pick, block, NN).astype(bf16)


def spread_small(extra, maps_ref, rows_ref):
    device_row = lax.broadcasted_iota(jnp.int32, (128, 1024), 0) * 8
    first = one_hot(device_row == lax.broadcasted_iota(jnp.int32, (128, 1024), 1))
    table = dot(first, extra, NN).astype(bf16)
    step = 2432
    for at in range(0, WIDE, step):
        index = lax.broadcasted_iota(jnp.int32, (128, step), 0)
        hot = one_hot(index == maps_ref[1:2, at : at + step])
        spread = dot(table, hot, NN)
        held = jnp.where(index == maps_ref[0:1, at : at + step], spread, 0.0)
        rows_ref[:, at : at + step] = jnp.sum(held, axis=0, keepdims=True)


def place_down(source, target):
    row = lax.broadcasted_iota(jnp.int32, (768, 256), 0)
    column = lax.broadcasted_iota(jnp.int32, (768, 256), 1)
    wanted = (column >> 3) * 24 + (column & 7)
    for group in range(2):
        total = None
        for part in range(3):
            block = source[group * 256 : group * 256 + 256, part * D : part * D + D]
            placed = dot(one_hot(row == wanted + 8 * part), block, NN)
            total = placed if total is None else total + placed
        target[group * 768 : group * 768 + 768, :] = total.astype(bf16)


def norm_back(upstream, scaled, inverse, gain):
    weighted = upstream * gain
    middle = jnp.mean(weighted, axis=-1, keepdims=True)
    slope = jnp.mean(weighted * scaled, axis=-1, keepdims=True)
    grad_in = inverse * (weighted - middle - scaled * slope)
    gain_sum = jnp.sum(upstream * scaled, axis=0, keepdims=True)
    return grad_in, gain_sum, jnp.sum(upstream, axis=0, keepdims=True)


def mlp_kernel(
    at_ref, maps_ref, all_ref, scaled_ref, inverse_ref, g_ref, order_ref,
    mlp0, mlp1, back0, back1, sums_ref, rows_ref, w0, w1, w2, w3,
    raw_up_s, raw_down_s, extra_s, up_ref, down_ref,
    h_s, ht_s, act_s, order_s, gp_s, gh_s, sems,
):
    core = at_ref[3]
    rs = pl.ds(pl.multiple_of(core * 512, 512), 512)
    copies = (
        pltpu.make_async_copy(all_ref.at[:, columns(EXTRA_AT, 128)], extra_s, sems.at[0]),
        pltpu.make_async_copy(
            all_ref.at[:, columns(core * HALF + QW, HF)], raw_up_s, sems.at[1]
        ),
        pltpu.make_async_copy(all_ref.at[rs, columns(DOWN_AT, 3 * D)], raw_down_s, sems.at[2]),
    )
    for copy in copies:
        copy.start()
    copies[0].wait()
    spread_small(extra_s[...], maps_ref, rows_ref)
    copies[1].wait()
    compact(raw_up_s, up_ref, 4)
    copies[2].wait()
    place_down(raw_down_s, down_ref)
    gain = rows_ref[:, spot("ln2g")]
    h = scaled_ref[...] * gain + rows_ref[:, spot("ln2b")]
    h_s[...] = h.astype(bf16)
    ht_s[...] = dot(order_ref[...], h_s[...], NT).astype(bf16)
    step = 384
    row = lax.broadcasted_iota(jnp.int32, (step, step), 0)
    column = lax.broadcasted_iota(jnp.int32, (step, step), 1)
    block = lax.rem(row, 192) // 12
    wanted = block * 24 + lax.rem(row, 12) + jnp.where(row >= 192, 12, 0)
    deal = one_hot(column == wanted)
    first = spot("upb").start
    for turn_at, at in enumerate(range(0, HF, step)):
        cut = slice(at, at + step)
        pre = dot(h_s[...], up_ref[:, cut], NN) + rows_ref[:, first + at : first + at + step]
        cumulative = 0.5 * (1.0 + lax.erf(pre * inv_sqrt_two))
        density = jnp.exp(-0.5 * pre * pre) * inv_sqrt_two_pi
        act = (pre * cumulative).astype(bf16)
        act_s[:, cut] = act
        order_s[turn_at] = dot(deal, act, NT).astype(bf16)
        grad_act = dot(g_ref[...], down_ref[cut, :], NT)
        grad_pre = (grad_act * (cumulative + pre * density)).astype(bf16)
        gp_s[:, cut] = grad_pre
        sums_ref[0:1, cut] = jnp.sum(grad_pre.astype(f32), axis=0, keepdims=True)
    for rel, ref in enumerate((w0, w1, w2, w3)):
        which = lax.rem(at_ref[0] + rel, 4)
        begin = pl.multiple_of(192 * which, 64)
        ref[:, :HF] = dot(ht_s[pl.ds(begin, 192), :], gp_s[...], NN).astype(bf16)
        dealt = order_s[which]
        ref[:, HF : HF + D] = dot(dealt[:192], g_ref[...], NN).astype(bf16)
        ref[:, HF + D :] = dot(dealt[192:], g_ref[...], NN).astype(bf16)
    mlp0[...] = dot(act_s[:ROWS, :], down_ref[...], NN)
    mlp1[...] = dot(act_s[ROWS:, :], down_ref[...], NN)
    gh_s[...] = dot(gp_s[...], up_ref[...], NT)
    back, gain_sum, shift_sum = norm_back(gh_s[...], scaled_ref[...], inverse_ref[...], gain)
    back0[...] = back[:ROWS]
    back1[...] = back[ROWS:]
    sums_ref[1:2, :D] = gain_sum
    sums_ref[2:3, :D] = shift_sum
    sums_ref[3:4, :D] = jnp.sum(g_ref[:ROWS, :].astype(f32), axis=0, keepdims=True)


def run_mlp(*operands):
    return pl.pallas_call(
        mlp_kernel,
        out_shape=(struct((ROWS, D), f32),) * 4
        + (struct((8, HF), f32), struct((1, WIDE), f32))
        + (struct((192, 2 * HF), bf16),) * 4,
        in_specs=[SMEM, VMEM, ANY] + [VMEM] * 4,
        out_specs=(VMEM,) * 10,
        scratch_shapes=[
            pltpu.VMEM((1024, HF), bf16),
            pltpu.VMEM((512, 3 * D), bf16),
            pltpu.VMEM((1024, 128), bf16),
            pltpu.VMEM((D, HF), bf16),
            pltpu.VMEM((HF, D), bf16),
            pltpu.VMEM((ALL, D), bf16),
            pltpu.VMEM((D, ALL), bf16),
            pltpu.VMEM((ALL, HF), bf16),
            pltpu.VMEM((4, 384, ALL), bf16),
            pltpu.VMEM((ALL, HF), bf16),
            pltpu.VMEM((ALL, D), f32),
            pltpu.SemaphoreType.DMA((3,)),
        ],
        compiler_params=pltpu.CompilerParams(vmem_limit_bytes=44 << 20),
        cost_estimate=pl.CostEstimate(
            flops=8 * 2 * ALL * D * HF, bytes_accessed=20 << 20, transcendentals=2 * ALL * HF
        ),
    )(*operands)


def turn(values, cosine, sine_a, sine_b):
    parts = []
    for at in range(0, values.shape[1], 128):
        part = values[:, at : at + 128]
        parts.append(
            part * cosine
            + pltpu.roll(part, 120, 1) * sine_a
            + pltpu.roll(part, 8, 1) * sine_b
        )
    return jnp.concatenate(parts, axis=1) if len(parts) > 1 else parts[0]


def attention_kernel(
    at_ref, all_ref, scaled_ref, inverse_ref, g_ref, rows_ref, cos_ref, sina_ref, sinb_ref,
    bias_ref, order_ref, scramble_ref, spread_ref, maps_ref, sums_ref,
    out0, out1, grad0, grad1, b0, b1, b2, b3,
    raw_qkv_s, raw_out_s, qkv_ref, ow_ref,
    h_s, ht_s, q_s, k_s, v_s, ga_s, attn_s, gj_s, gh_s, sa_s, sems,
):
    core = at_ref[3]
    rs = pl.ds(pl.multiple_of(core * 512, 512), 512)
    copies = (
        pltpu.make_async_copy(all_ref.at[:, columns(core * HALF, QW)], raw_qkv_s, sems.at[0]),
        pltpu.make_async_copy(all_ref.at[rs, columns(OUT_AT, D)], raw_out_s, sems.at[1]),
    )
    for copy in copies:
        copy.start()
    gain = rows_ref[:, spot("ln1g")]
    h = scaled_ref[...] * gain + rows_ref[:, spot("ln1b")]
    h_s[...] = h.astype(bf16)
    ht_s[...] = dot(order_ref[...], h_s[...], NT).astype(bf16)
    copies[0].wait()
    compact(raw_qkv_s, qkv_ref, 4)
    copies[1].wait()
    compact(raw_out_s, ow_ref, 2)
    first = spot("qkvb").start
    cosine, sine_a, sine_b = cos_ref[...], sina_ref[...], sinb_ref[...]
    for part, ref in enumerate((q_s, k_s, v_s)):
        cut = slice(part * HD, part * HD + HD)
        bias = rows_ref[:, first + part * HD : first + (part + 1) * HD]
        joint = dot(h_s[...], qkv_ref[:, cut], NN) + bias
        if part < 2:
            joint = turn(joint, cosine, sine_a, sine_b)
        ref[...] = joint.astype(bf16)
    ga_s[...] = dot(g_ref[...], ow_ref[...], NT).astype(bf16)

    scale = HEAD_DIM ** (-0.5)
    lanes = lax.broadcasted_iota(jnp.int32, (MB_ROWS, 128), 1) < HEAD_DIM
    low = lanes.astype(f32).astype(bf16)
    high = (1.0 - lanes.astype(f32)).astype(bf16)

    def one_block(block, carry):
        rs = pl.ds(pl.multiple_of(block * MB_ROWS, MB_ROWS), MB_ROWS)
        bias = bias_ref[rs, :]
        bias = jnp.concatenate([bias, bias], axis=0)
        turn_c, turn_a, turn_b = cos_ref[rs, :], -sina_ref[rs, :], -sinb_ref[rs, :]
        for pair in range(HH // 2):
            cs = slice(pair * 128, pair * 128 + 128)
            qp, kp, vp, ga = q_s[rs, cs], k_s[rs, cs], v_s[rs, cs], ga_s[rs, cs]
            qm = jnp.concatenate([qp * low, qp * high], axis=0)
            gm = jnp.concatenate([ga * low, ga * high], axis=0)
            scores = dot(qm, kp, NT) * scale + bias
            expd = jnp.exp(scores - jnp.max(scores, axis=-1, keepdims=True))
            probs = expd / jnp.sum(expd, axis=-1, keepdims=True)
            p = probs.astype(bf16)
            mixed = dot(p, vp, NN)
            attn_s[rs, cs] = jnp.where(lanes, mixed[:MB_ROWS], mixed[MB_ROWS:]).astype(bf16)
            grad_p = dot(gm, vp, NT)
            grad_v = dot(p, gm, TN)
            delta = jnp.sum(probs * grad_p, axis=-1, keepdims=True)
            ds = (probs * (grad_p - delta)).astype(bf16)
            both = dot(ds, kp, NN)
            grad_q = jnp.where(lanes, both[:MB_ROWS], both[MB_ROWS:]) * scale
            grad_k = dot(ds, qm, TN) * scale
            gj_s[rs, cs] = turn(grad_q, turn_c, turn_a, turn_b).astype(bf16)
            ck = slice(HD + pair * 128, HD + pair * 128 + 128)
            cv = slice(2 * HD + pair * 128, 2 * HD + pair * 128 + 128)
            gj_s[rs, ck] = turn(grad_k, turn_c, turn_a, turn_b).astype(bf16)
            gj_s[rs, cv] = grad_v.astype(bf16)
        return carry

    lax.fori_loop(0, BLOCKS, one_block, 0)

    sa_s[...] = dot(scramble_ref[...], attn_s[...], NT).astype(bf16)
    gh_s[...] = dot(gj_s[...], qkv_ref[...], NT)
    back, gain_sum, shift_sum = norm_back(gh_s[...], scaled_ref[...], inverse_ref[...], gain)
    grad0[...] = back[:ROWS]
    grad1[...] = back[ROWS:]
    part = dot(attn_s[...], ow_ref[...], NN)
    out0[...] = part[:ROWS]
    out1[...] = part[ROWS:]

    branch = sums_ref[3:4, :D]
    joint_sum = jnp.sum(gj_s[...].astype(f32), axis=0, keepdims=True)
    values = {
        "ln1g": gain_sum,
        "ln1b": shift_sum,
        "qkvb": joint_sum,
        "outb": branch,
        "ln2g": sums_ref[1:2, :D],
        "ln2b": sums_ref[2:3, :D],
        "upb": sums_ref[0:1, :],
        "downb": branch,
    }
    table = jnp.zeros((128, 128), f32)
    for key, _ in SMALL:
        span = spot(key)
        index = lax.broadcasted_iota(jnp.int32, (128, span.stop - span.start), 0)
        hot = (index == maps_ref[1:2, span]).astype(f32).astype(bf16)
        held = jnp.where(index == maps_ref[0:1, span], values[key], 0.0).astype(bf16)
        table = table + dot(held, hot, NT)
    table = table.astype(bf16)
    for rel, ref in enumerate((b0, b1, b2, b3)):
        rs = pl.ds(pl.multiple_of(192 * lax.rem(at_ref[0] + rel, 4), 64), 192)
        one = dot(sa_s[rs, :], g_ref[:, :HD], NN)
        two = dot(sa_s[rs, :], g_ref[:, HD:], NN)
        inner = lax.rem(lax.broadcasted_iota(jnp.int32, (192, HD), 0), 12)
        ref[:, :HD] = jnp.where(inner >= 6, two, one).astype(bf16)
        ref[:, HD : HD + QW] = dot(ht_s[rs, :], gj_s[...], NN).astype(bf16)
        ref[:, HD + QW :] = dot(spread_ref[rs, :], table, NN).astype(bf16)


def run_attention(*operands):
    half = (struct((ROWS, D), f32),) * 4
    return pl.pallas_call(
        attention_kernel,
        out_shape=half + (struct((192, CUT), bf16),) * 4,
        in_specs=[SMEM, ANY] + [VMEM] * (len(operands) - 2),
        out_specs=(VMEM,) * 8,
        scratch_shapes=[
            pltpu.VMEM((1024, QW), bf16),
            pltpu.VMEM((512, D), bf16),
            pltpu.VMEM((D, QW), bf16),
            pltpu.VMEM((HD, D), bf16),
            pltpu.VMEM((ALL, D), bf16),
            pltpu.VMEM((D, ALL), bf16),
            pltpu.VMEM((ALL, HD), bf16),
            pltpu.VMEM((ALL, HD), bf16),
            pltpu.VMEM((ALL, HD), bf16),
            pltpu.VMEM((ALL, HD), bf16),
            pltpu.VMEM((ALL, HD), bf16),
            pltpu.VMEM((ALL, QW), bf16),
            pltpu.VMEM((ALL, D), f32),
            pltpu.VMEM((D, ALL), bf16),
            pltpu.SemaphoreType.DMA((2,)),
        ],
        compiler_params=pltpu.CompilerParams(vmem_limit_bytes=44 << 20),
        cost_estimate=pl.CostEstimate(
            flops=6 * 2 * ALL * D * (QW + HD), bytes_accessed=20 << 20, transcendentals=ALL * 128 * HH
        ),
    )(*operands)


def prepare(tokens, cotangent, segment):
    rows32 = tokens.astype(f32)
    centred = rows32 - jnp.mean(rows32, axis=-1, keepdims=True)
    inverse = lax.rsqrt(jnp.mean(centred * centred, axis=-1, keepdims=True) + epsilon)
    live = (segment >= 0).astype(f32)[:, None]
    g = (cotangent.astype(f32) * live).astype(bf16)
    blocks = segment.reshape(BLOCKS, MB_ROWS)
    same = blocks[:, :, None] == blocks[:, None, :]
    earlier = jnp.arange(MB_ROWS)[None, :] <= jnp.arange(MB_ROWS)[:, None]
    allowed = (same & earlier[None]).reshape(ALL, MB_ROWS)
    bias = jnp.where(allowed, 0.0, masked_score)
    place = (jnp.sum(allowed.astype(jnp.int32), axis=1) - 1).astype(f32)
    lane = jnp.arange(128) % HEAD_DIM
    frequency = jnp.exp(
        (lane % 8).astype(f32) * (-2.0 * math.log(10000.0) / ROTARY)
    )
    angle = place[:, None] * frequency[None, :]
    cosine = jnp.where(lane < 16, jnp.cos(angle), 1.0)
    sine = jnp.sin(angle)
    sine_a = jnp.where(lane < 8, -sine, 0.0)
    sine_b = jnp.where((lane >= 8) & (lane < 16), sine, 0.0)
    return centred * inverse, inverse, g, cosine, sine_a, sine_b, bias


def row_maps(core):
    place = jnp.arange(D)[:, None]
    block, inner = place // 12, place % 12
    first, second, third = block // 16, (block // 4) % 4, block % 4
    x = jnp.where(core == 0, first, second)
    z = jnp.where(core == 0, second, first)
    natural = ((x * 4 + third) * 4 + z) * 12 + inner
    order = (natural == jnp.arange(D)[None]).astype(bf16)
    scramble = (block * 6 + inner % 6 == jnp.arange(HD)[None]).astype(bf16)
    spread = (natural == 6 * jnp.arange(128)[None]).astype(bf16)
    return order, scramble, spread


def body(
    tokens,
    cotangent,
    segment,
    ln1_gain,
    ln1_bias,
    qkv_weight,
    qkv_bias,
    out_weight,
    out_bias,
    ln2_gain,
    ln2_bias,
    up_weight,
    up_bias,
    down_weight,
    down_bias,
):
    me = lax.axis_index("fsdp")
    core, z, y, x = me % 2, (me // 2) % 4, (me // 8) % 4, me // 32

    both_tokens = jnp.concatenate([tokens, swap(tokens)], axis=0)
    both_cot = jnp.concatenate([cotangent, swap(cotangent)], axis=0)
    both_segment = jnp.concatenate([segment, swap(segment)], axis=0)
    scaled, inverse, g, cosine, sine_a, sine_b, bias = prepare(
        both_tokens, both_cot, both_segment
    )
    digits = (jnp.where(core == 0, x, z), jnp.where(core == 0, z, x), y)
    at = jnp.stack(digits + (core,)).astype(jnp.int32)
    maps = small_maps(core)
    order, scramble, spread = row_maps(core)

    extra = jnp.zeros((1, 128), bf16)
    start = 0
    for vector in (
        ln1_gain, ln1_bias, qkv_bias, out_bias, ln2_gain, ln2_bias, up_bias, down_bias
    ):
        width = vector.shape[0]
        extra = extra + jnp.pad(vector[None], ((0, 0), (start, 128 - start - width)))
        start += width
    packed = pack_weights(qkv_weight, out_weight, up_weight, extra, down_weight)
    everything = lax.all_gather(packed, "fsdp", axis=0, tiled=True)
    mlp0, mlp1, back0, back1, sums, vectors, w0, w1, w2, w3 = run_mlp(
        at, maps, everything, scaled, inverse, g, order
    )
    wide = exchange((w0, w1, w2, w3), 0)
    out0, out1, grad0, grad1, b0, b1, b2, b3 = run_attention(
        at, everything, scaled, inverse, g, vectors, cosine, sine_a, sine_b, bias,
        order, scramble, spread, maps, sums,
    )
    wide = sum_first(at, w0, wide)
    wide, b0, b1, b2, b3 = lax.optimization_barrier((wide, b0, b1, b2, b3))
    narrow = exchange((b0, b1, b2, b3), 0)
    wide = added(wide[0], exchange(wide, 1))
    narrow = sum_first(at, b0, narrow)
    narrow = added(narrow[0], exchange(narrow, 1))
    blocks = jnp.concatenate([narrow, wide], axis=1).reshape(4, 12, CUT + 2 * HF)
    last = [
        lax.dynamic_index_in_dim(blocks, (digits[2] + rel) % 4, 0, keepdims=False)
        for rel in range(4)
    ]
    last = added(last[0], exchange([last[0]] + [part.astype(bf16) for part in last[1:]], 2))
    narrow, wide = last[:, :CUT], last[:, CUT:]

    down_rows = jnp.concatenate([wide[:, HF : HF + D], wide[:, HF + D :]], axis=0)
    out_rows = jnp.concatenate([narrow[:6, :HD], narrow[6:, :HD]], axis=1)
    own_rows = permute(jnp.concatenate([down_rows, out_rows], axis=0), ROW_PAIRS)
    own_down, own_out = own_rows[:24], own_rows[24:]
    both = jnp.concatenate([narrow[:, HD:], wide[:, :HF]], axis=1).reshape(2, 6, QW + 128 + HF)
    mine = lax.dynamic_index_in_dim(both, core, 0, keepdims=False)
    theirs = swap(lax.dynamic_index_in_dim(both, 1 - core, 0, keepdims=False))
    low = jnp.where(core == 0, mine, theirs)
    high = jnp.where(core == 0, theirs, mine)
    own_qkv = jnp.stack(
        [low[:, :QW].reshape(6, 3, HD), high[:, :QW].reshape(6, 3, HD)], axis=2
    ).reshape(6, 3 * D)
    own_up = jnp.concatenate([low[:, QW + 128 :], high[:, QW + 128 :]], axis=1)
    line = (low + high)[0, QW : QW + 128]
    own = {}
    start = 0
    for name, width in SMALL:
        own[name] = line[start : start + width]
        start += width

    live = (segment >= 0).astype(f32)[:, None]
    out_sum = out0 + mlp0 + swap(out1 + mlp1) + vectors[:, spot("outb")] + vectors[:, spot("downb")]
    output = (tokens.astype(f32) + live * out_sum).astype(bf16)
    grad_tokens = cotangent.astype(f32) + (grad0 + back0 + swap(grad1 + back1))
    return (
        output,
        grad_tokens,
        own["ln1g"],
        own["ln1b"],
        own_qkv,
        own["qkvb"],
        own_out,
        own["outb"],
        own["ln2g"],
        own["ln2b"],
        own_up,
        own["upb"],
        own_down,
        own["downb"],
    )


def solution(mesh):
    row = P("fsdp", None)
    flat = P("fsdp")
    return jax.shard_map(
        body,
        mesh=mesh,
        in_specs=(
            row, row, flat, flat, flat, row, flat, row, flat, flat, flat, row, flat, row, flat,
        ),
        out_specs=(
            row, row, flat, flat, row, flat, row, flat, flat, flat, row, flat, row, flat,
        ),
        check_vma=False,
    )
```

```python
import math

import jax
import jax.numpy as jnp
from jax import lax
from jax.experimental import pallas as pl
from jax.experimental.pallas import tpu as pltpu
from jax.sharding import PartitionSpec as P

D = 768
HEADS = 12
HEAD_DIM = 64
ROTARY = 16
FF = 3072
MB_ROWS = 128
ROWS = 256
HH = HEADS // 2
HD = D // 2
HF = FF // 2
QW = 3 * HD

epsilon = 1e-05
masked_score = -1e30
inv_sqrt_two = 1.0 / math.sqrt(2.0)
inv_sqrt_two_pi = 1.0 / math.sqrt(2.0 * math.pi)
bf16 = jnp.bfloat16
f32 = jnp.float32

STRIDE = {"x": 32, "y": 8, "z": 2, "c": 1}
SIZE = {"x": 4, "y": 4, "z": 4, "c": 2}
SMALL = (("ln1g", 6), ("ln1b", 6), ("qkvb", 18), ("outb", 6), ("ln2g", 6), ("ln2b", 6), ("upb", 24), ("downb", 6))


def digit(index, axis):
    return (index // STRIDE[axis]) % SIZE[axis]


ORDER = (("x", "y", "z"), ("z", "y", "x"))


def shift(axis, step):
    pairs = []
    for source in range(128):
        at = digit(source, axis)
        target = source + ((at + step) % SIZE[axis] - at) * STRIDE[axis]
        pairs.append((source, target))
    return pairs


def stage_shift(stage, step):
    pairs = []
    for source in range(128):
        axis = ORDER[source % 2][stage]
        at = digit(source, axis)
        pairs.append((source, source + ((at + step) % 4 - at) * STRIDE[axis]))
    return pairs


def holder(half, block):
    digits = (block // 16, (block // 4) % 4, block % 4)
    return half + sum(STRIDE[axis] * at for axis, at in zip(ORDER[half], digits))


ROW_PAIRS = [
    (holder(half, block), 64 * half + block) for half in range(2) for block in range(64)
]


ROW_FROM = [(source, target) for target, source in ROW_PAIRS]


def permute(values, pairs):
    return lax.ppermute(values, "fsdp", pairs)


def swap(values):
    return permute(values, shift("c", 1))


def exchange(parts, stage):
    _, after, across, before = parts
    return (
        permute(after, stage_shift(stage, 1)),
        permute(before, stage_shift(stage, -1)),
        permute(across, stage_shift(stage, 2)),
    )


def added(own, arrived):
    total = own.astype(f32)
    for piece in arrived:
        total = total + piece.astype(f32)
    return total


def sum_kernel(at_ref, own_ref, one_ref, two_ref, three_ref, own_out, *outs):
    refs = (own_ref, one_ref, two_ref, three_ref)
    for rel in range(4):
        rs = pl.ds(pl.multiple_of(48 * lax.rem(at_ref[1] + rel, 4), 16), 48)
        total = added(own_ref[rs, :], [ref[rs, :] for ref in refs[1:]])
        if rel == 0:
            own_out[...] = total
        else:
            outs[rel - 1][...] = total.astype(bf16)


def sum_first(at, own, arrived):
    width = own.shape[1]
    return pl.pallas_call(
        sum_kernel,
        out_shape=(struct((48, width), f32),) + (struct((48, width), bf16),) * 3,
        in_specs=[SMEM] + [VMEM] * 4,
        out_specs=(VMEM,) * 4,
        compiler_params=pltpu.CompilerParams(vmem_limit_bytes=24 << 20),
        cost_estimate=pl.CostEstimate(
            flops=4 * 192 * width, bytes_accessed=10 * 192 * width, transcendentals=0
        ),
    )(at, own, *arrived)


CUT = HD + QW + 128
PAIR = QW + HF + 128
WIDE_COLS = 2 * HF + 128
NARROW_COLS = HD + QW


def dot(a, b, dims):
    return lax.dot_general(a, b, (dims, ((), ())), preferred_element_type=f32)


NN = ((1,), (0,))
NT = ((1,), (1,))
TN = ((0,), (0,))
ALL = 2 * ROWS
BLOCKS = ALL // MB_ROWS
WIDE = 6 * D + QW + HF
VMEM = pl.BlockSpec(memory_space=pltpu.VMEM)
SMEM = pl.BlockSpec(memory_space=pltpu.SMEM)


def struct(shape, kind):
    return jax.ShapeDtypeStruct(shape, kind)


def spot(name):
    at = 0
    for key, width in SMALL:
        span = QW if key == "qkvb" else HF if key == "upb" else 128 * width
        if key == name:
            return slice(at, at + span)
        at += span


def small_maps(core):
    device, lane = [], []
    at = 0
    for key, width in SMALL:
        if key == "qkvb":
            flat = (jnp.arange(3)[:, None] * D + core * HD + jnp.arange(HD)[None]).reshape(QW)
        elif key == "upb":
            flat = core * HF + jnp.arange(HF)
        else:
            flat = jnp.arange(128 * width)
        device.append(flat // width)
        lane.append(at + flat % width)
        at += width
    return jnp.stack([jnp.concatenate(device), jnp.concatenate(lane)]).astype(jnp.int32)


def one_hot(condition):
    return condition.astype(f32).astype(bf16)


def pack_kernel(at_ref, qkv_ref, out_ref, up_ref, extra_ref, down_ref, mine_ref, theirs_ref, rows_ref):
    core = at_ref[3]
    for half, to_ref in ((core, mine_ref), (1 - core, theirs_ref)):
        to_ref[:, QW + HF :] = jnp.zeros((6, 128), bf16)
        to_ref[0:1, QW + HF :] = extra_ref[...]
        for part in range(3):
            begin = pl.multiple_of(part * D + half * HD, 128)
            to_ref[:, part * HD : (part + 1) * HD] = qkv_ref[:, pl.ds(begin, HD)]
        begin = pl.multiple_of(half * HF, 128)
        to_ref[:, QW : QW + HF] = up_ref[:, pl.ds(begin, HF)]
    rows_ref[24:32, :] = jnp.zeros((8, D), bf16)
    rows_ref[0:24, :] = down_ref[...]
    rows_ref[24:30, :] = out_ref[...]


def pack_weights(*operands):
    return pl.pallas_call(
        pack_kernel,
        out_shape=(struct((6, PAIR), bf16), struct((6, PAIR), bf16), struct((32, D), bf16)),
        in_specs=[SMEM] + [VMEM] * 5,
        out_specs=(VMEM,) * 3,
    )(*operands)


def join_kernel(at_ref, mine_ref, got_ref, rows_ref, to_ref):
    first = at_ref[3] == 0
    mine, got = mine_ref[...].astype(f32), got_ref[...].astype(f32)
    low = jnp.where(first, mine, got).astype(bf16)
    high = jnp.where(first, got, mine).astype(bf16)
    for at, rows in ((0, low), (6, high)):
        to_ref[at : at + 6, :HF] = rows[:, QW : QW + HF]
        to_ref[at : at + 6, 2 * HF : WIDE_COLS] = rows[:, QW + HF :]
        to_ref[at : at + 6, WIDE_COLS + HD :] = rows[:, :QW]
    to_ref[:, HF : HF + D] = rows_ref[0:12, :]
    to_ref[:, HF + D : 2 * HF] = rows_ref[12:24, :]
    to_ref[0:6, WIDE_COLS : WIDE_COLS + HD] = rows_ref[24:30, :HD]
    to_ref[6:12, WIDE_COLS : WIDE_COLS + HD] = rows_ref[24:30, HD:]


def join_weights(*operands):
    return pl.pallas_call(
        join_kernel,
        out_shape=struct((12, WIDE_COLS + NARROW_COLS), bf16),
        in_specs=[SMEM] + [VMEM] * 3,
        out_specs=VMEM,
    )(*operands)


def collect(block, stage):
    return (
        block,
        permute(block, stage_shift(stage, -1)),
        permute(block, stage_shift(stage, 2)),
        permute(block, stage_shift(stage, 1)),
    )


def first_kernel(at_ref, one, two, three, four, wide_ref, narrow_ref, held_s):
    held_s[...] = jnp.zeros_like(held_s)
    for rel, ref in enumerate((one, two, three, four)):
        held_s[16 * rel : 16 * rel + 12, :] = ref[...]
    row = lax.broadcasted_iota(jnp.int32, (48, 64), 0)
    column = lax.broadcasted_iota(jnp.int32, (48, 64), 1)
    rel = lax.rem(row // 12 - at_ref[2] + 4, 4)
    pick = one_hot(column == 16 * rel + lax.rem(row, 12))
    wide_ref[...] = dot(pick, held_s[:, :WIDE_COLS], NN).astype(bf16)
    narrow_ref[...] = dot(pick, held_s[:, WIDE_COLS:], NN).astype(bf16)


def place_first(at, pieces):
    return pl.pallas_call(
        first_kernel,
        out_shape=(struct((48, WIDE_COLS), bf16), struct((48, NARROW_COLS), bf16)),
        in_specs=[SMEM] + [VMEM] * 4,
        out_specs=(VMEM,) * 2,
        scratch_shapes=[pltpu.VMEM((64, WIDE_COLS + NARROW_COLS), bf16)],
    )(at, *pieces)


def second_kernel(at_ref, one, two, three, four, to_ref):
    for rel, ref in enumerate((one, two, three, four)):
        begin = pl.multiple_of(48 * lax.rem(at_ref[1] + rel, 4), 16)
        to_ref[pl.ds(begin, 48), :] = ref[...]


def place_second(at, pieces):
    return pl.pallas_call(
        second_kernel,
        out_shape=struct((192, pieces[0].shape[1]), bf16),
        in_specs=[SMEM] + [VMEM] * 4,
        out_specs=VMEM,
    )(at, *pieces)


def place_third(at_ref, refs, target):
    for rel, ref in enumerate(refs):
        begin = pl.multiple_of(192 * lax.rem(at_ref[0] + rel, 4), 64)
        target[pl.ds(begin, 192), :] = ref[...]


def spread_small(table, maps_ref, rows_ref):
    step = 2432
    for at in range(0, WIDE, step):
        index = lax.broadcasted_iota(jnp.int32, (128, step), 0)
        hot = one_hot(index == maps_ref[1:2, at : at + step])
        spread = dot(table, hot, NN)
        held = jnp.where(index == maps_ref[0:1, at : at + step], spread, 0.0)
        rows_ref[:, at : at + step] = jnp.sum(held, axis=0, keepdims=True)


def norm_back(upstream, scaled, inverse, gain):
    weighted = upstream * gain
    middle = jnp.mean(weighted, axis=-1, keepdims=True)
    slope = jnp.mean(weighted * scaled, axis=-1, keepdims=True)
    grad_in = inverse * (weighted - middle - scaled * slope)
    gain_sum = jnp.sum(upstream * scaled, axis=0, keepdims=True)
    return grad_in, gain_sum, jnp.sum(upstream, axis=0, keepdims=True)


def mlp_kernel(
    at_ref, maps_ref, p0, p1, p2, p3, scaled_ref, inverse_ref, g_ref, order_ref, spread_ref,
    mlp0, mlp1, back0, back1, sums_ref, rows_ref, w0, w1, w2, w3,
    held_s, up_ref, down_ref,
    h_s, ht_s, act_s, order_s, gp_s, gh_s,
):
    step = 384
    row = lax.broadcasted_iota(jnp.int32, (step, step), 0)
    column = lax.broadcasted_iota(jnp.int32, (step, step), 1)
    block = lax.rem(row, 192) // 12
    wanted = block * 24 + lax.rem(row, 12) + jnp.where(row >= 192, 12, 0)
    deal = one_hot(column == wanted)
    place_third(at_ref, (p0, p1, p2, p3), held_s)
    table = dot(spread_ref[...], held_s[:, 2 * HF :], TN).astype(bf16)
    spread_small(table, maps_ref, rows_ref)
    up_ref[...] = dot(order_ref[...], held_s[:, :HF], TN).astype(bf16)
    for part in range(4):
        rs = slice(192 * part, 192 * part + 192)
        down_ref[step * part : step * (part + 1), :] = (
            dot(deal[:192], held_s[rs, HF : HF + D], TN)
            + dot(deal[192:], held_s[rs, HF + D : 2 * HF], TN)
        ).astype(bf16)
    gain = rows_ref[:, spot("ln2g")]
    h = scaled_ref[...] * gain + rows_ref[:, spot("ln2b")]
    h_s[...] = h.astype(bf16)
    ht_s[...] = dot(order_ref[...], h_s[...], NT).astype(bf16)
    first = spot("upb").start
    for turn_at, at in enumerate(range(0, HF, step)):
        cut = slice(at, at + step)
        pre = dot(h_s[...], up_ref[:, cut], NN) + rows_ref[:, first + at : first + at + step]
        cumulative = 0.5 * (1.0 + lax.erf(pre * inv_sqrt_two))
        density = jnp.exp(-0.5 * pre * pre) * inv_sqrt_two_pi
        act = (pre * cumulative).astype(bf16)
        act_s[:, cut] = act
        order_s[turn_at] = dot(deal, act, NT).astype(bf16)
        grad_act = dot(g_ref[...], down_ref[cut, :], NT)
        grad_pre = (grad_act * (cumulative + pre * density)).astype(bf16)
        gp_s[:, cut] = grad_pre
        sums_ref[0:1, cut] = jnp.sum(grad_pre.astype(f32), axis=0, keepdims=True)
    for rel, ref in enumerate((w0, w1, w2, w3)):
        which = lax.rem(at_ref[0] + rel, 4)
        begin = pl.multiple_of(192 * which, 64)
        ref[:, :HF] = dot(ht_s[pl.ds(begin, 192), :], gp_s[...], NN).astype(bf16)
        dealt = order_s[which]
        ref[:, HF : HF + D] = dot(dealt[:192], g_ref[...], NN).astype(bf16)
        ref[:, HF + D :] = dot(dealt[192:], g_ref[...], NN).astype(bf16)
    mlp0[...] = dot(act_s[:ROWS, :], down_ref[...], NN)
    mlp1[...] = dot(act_s[ROWS:, :], down_ref[...], NN)
    gh_s[...] = dot(gp_s[...], up_ref[...], NT)
    back, gain_sum, shift_sum = norm_back(gh_s[...], scaled_ref[...], inverse_ref[...], gain)
    back0[...] = back[:ROWS]
    back1[...] = back[ROWS:]
    sums_ref[1:2, :D] = gain_sum
    sums_ref[2:3, :D] = shift_sum
    sums_ref[3:4, :D] = jnp.sum(g_ref[:ROWS, :].astype(f32), axis=0, keepdims=True)


def run_mlp(*operands):
    return pl.pallas_call(
        mlp_kernel,
        out_shape=(struct((ROWS, D), f32),) * 4
        + (struct((8, HF), f32), struct((1, WIDE), f32))
        + (struct((192, 2 * HF), bf16),) * 4,
        in_specs=[SMEM] + [VMEM] * 10,
        out_specs=(VMEM,) * 10,
        scratch_shapes=[
            pltpu.VMEM((D, WIDE_COLS), bf16),
            pltpu.VMEM((D, HF), bf16),
            pltpu.VMEM((HF, D), bf16),
            pltpu.VMEM((ALL, D), bf16),
            pltpu.VMEM((D, ALL), bf16),
            pltpu.VMEM((ALL, HF), bf16),
            pltpu.VMEM((4, 384, ALL), bf16),
            pltpu.VMEM((ALL, HF), bf16),
            pltpu.VMEM((ALL, D), f32),
        ],
        compiler_params=pltpu.CompilerParams(vmem_limit_bytes=44 << 20),
        cost_estimate=pl.CostEstimate(
            flops=8 * 2 * ALL * D * HF, bytes_accessed=20 << 20, transcendentals=2 * ALL * HF
        ),
    )(*operands)


def turn(values, cosine, sine_a, sine_b):
    parts = []
    for at in range(0, values.shape[1], 128):
        part = values[:, at : at + 128]
        parts.append(
            part * cosine
            + pltpu.roll(part, 120, 1) * sine_a
            + pltpu.roll(part, 8, 1) * sine_b
        )
    return jnp.concatenate(parts, axis=1) if len(parts) > 1 else parts[0]


def attention_kernel(
    at_ref, p0, p1, p2, p3, scaled_ref, inverse_ref, g_ref, rows_ref, cos_ref, sina_ref, sinb_ref,
    bias_ref, order_ref, scramble_ref, spread_ref, maps_ref, sums_ref,
    out0, out1, grad0, grad1, b0, b1, b2, b3,
    held_s, qkv_ref, ow_ref,
    h_s, ht_s, q_s, k_s, v_s, ga_s, attn_s, gj_s, gh_s, sa_s,
):
    gain = rows_ref[:, spot("ln1g")]
    h = scaled_ref[...] * gain + rows_ref[:, spot("ln1b")]
    h_s[...] = h.astype(bf16)
    ht_s[...] = dot(order_ref[...], h_s[...], NT).astype(bf16)
    place_third(at_ref, (p0, p1, p2, p3), held_s)
    qkv_ref[...] = dot(order_ref[...], held_s[:, HD:], TN).astype(bf16)
    inner = lax.rem(lax.broadcasted_iota(jnp.int32, (D, HD), 0), 12)
    left = scramble_ref[...] * one_hot(inner < 6)
    right = scramble_ref[...] * one_hot(inner >= 6)
    ow_ref[:, :HD] = dot(left, held_s[:, :HD], TN).astype(bf16)
    ow_ref[:, HD:] = dot(right, held_s[:, :HD], TN).astype(bf16)
    first = spot("qkvb").start
    cosine, sine_a, sine_b = cos_ref[...], sina_ref[...], sinb_ref[...]
    for part, ref in enumerate((q_s, k_s, v_s)):
        cut = slice(part * HD, part * HD + HD)
        bias = rows_ref[:, first + part * HD : first + (part + 1) * HD]
        joint = dot(h_s[...], qkv_ref[:, cut], NN) + bias
        if part < 2:
            joint = turn(joint, cosine, sine_a, sine_b)
        ref[...] = joint.astype(bf16)
    ga_s[...] = dot(g_ref[...], ow_ref[...], NT).astype(bf16)

    scale = HEAD_DIM ** (-0.5)
    lanes = lax.broadcasted_iota(jnp.int32, (MB_ROWS, 128), 1) < HEAD_DIM
    low = lanes.astype(f32).astype(bf16)
    high = (1.0 - lanes.astype(f32)).astype(bf16)

    def one_block(block, carry):
        rs = pl.ds(pl.multiple_of(block * MB_ROWS, MB_ROWS), MB_ROWS)
        bias = bias_ref[rs, :]
        bias = jnp.concatenate([bias, bias], axis=0)
        turn_c, turn_a, turn_b = cos_ref[rs, :], -sina_ref[rs, :], -sinb_ref[rs, :]
        for pair in range(HH // 2):
            cs = slice(pair * 128, pair * 128 + 128)
            qp, kp, vp, ga = q_s[rs, cs], k_s[rs, cs], v_s[rs, cs], ga_s[rs, cs]
            qm = jnp.concatenate([qp * low, qp * high], axis=0)
            gm = jnp.concatenate([ga * low, ga * high], axis=0)
            scores = dot(qm, kp, NT) * scale + bias
            expd = jnp.exp(scores - jnp.max(scores, axis=-1, keepdims=True))
            probs = expd / jnp.sum(expd, axis=-1, keepdims=True)
            p = probs.astype(bf16)
            mixed = dot(p, vp, NN)
            attn_s[rs, cs] = jnp.where(lanes, mixed[:MB_ROWS], mixed[MB_ROWS:]).astype(bf16)
            grad_p = dot(gm, vp, NT)
            grad_v = dot(p, gm, TN)
            delta = jnp.sum(probs * grad_p, axis=-1, keepdims=True)
            ds = (probs * (grad_p - delta)).astype(bf16)
            both = dot(ds, kp, NN)
            grad_q = jnp.where(lanes, both[:MB_ROWS], both[MB_ROWS:]) * scale
            grad_k = dot(ds, qm, TN) * scale
            gj_s[rs, cs] = turn(grad_q, turn_c, turn_a, turn_b).astype(bf16)
            ck = slice(HD + pair * 128, HD + pair * 128 + 128)
            cv = slice(2 * HD + pair * 128, 2 * HD + pair * 128 + 128)
            gj_s[rs, ck] = turn(grad_k, turn_c, turn_a, turn_b).astype(bf16)
            gj_s[rs, cv] = grad_v.astype(bf16)
        return carry

    lax.fori_loop(0, BLOCKS, one_block, 0)

    sa_s[...] = dot(scramble_ref[...], attn_s[...], NT).astype(bf16)
    gh_s[...] = dot(gj_s[...], qkv_ref[...], NT)
    back, gain_sum, shift_sum = norm_back(gh_s[...], scaled_ref[...], inverse_ref[...], gain)
    grad0[...] = back[:ROWS]
    grad1[...] = back[ROWS:]
    part = dot(attn_s[...], ow_ref[...], NN)
    out0[...] = part[:ROWS]
    out1[...] = part[ROWS:]

    branch = sums_ref[3:4, :D]
    joint_sum = jnp.sum(gj_s[...].astype(f32), axis=0, keepdims=True)
    values = {
        "ln1g": gain_sum,
        "ln1b": shift_sum,
        "qkvb": joint_sum,
        "outb": branch,
        "ln2g": sums_ref[1:2, :D],
        "ln2b": sums_ref[2:3, :D],
        "upb": sums_ref[0:1, :],
        "downb": branch,
    }
    table = jnp.zeros((128, 128), f32)
    for key, _ in SMALL:
        span = spot(key)
        index = lax.broadcasted_iota(jnp.int32, (128, span.stop - span.start), 0)
        hot = (index == maps_ref[1:2, span]).astype(f32).astype(bf16)
        held = jnp.where(index == maps_ref[0:1, span], values[key], 0.0).astype(bf16)
        table = table + dot(held, hot, NT)
    table = table.astype(bf16)
    for rel, ref in enumerate((b0, b1, b2, b3)):
        rs = pl.ds(pl.multiple_of(192 * lax.rem(at_ref[0] + rel, 4), 64), 192)
        one = dot(sa_s[rs, :], g_ref[:, :HD], NN)
        two = dot(sa_s[rs, :], g_ref[:, HD:], NN)
        inner = lax.rem(lax.broadcasted_iota(jnp.int32, (192, HD), 0), 12)
        ref[:, :HD] = jnp.where(inner >= 6, two, one).astype(bf16)
        ref[:, HD : HD + QW] = dot(ht_s[rs, :], gj_s[...], NN).astype(bf16)
        ref[:, HD + QW :] = dot(spread_ref[rs, :], table, NN).astype(bf16)


def run_attention(*operands):
    half = (struct((ROWS, D), f32),) * 4
    return pl.pallas_call(
        attention_kernel,
        out_shape=half + (struct((192, CUT), bf16),) * 4,
        in_specs=[SMEM] + [VMEM] * (len(operands) - 1),
        out_specs=(VMEM,) * 8,
        scratch_shapes=[
            pltpu.VMEM((D, NARROW_COLS), bf16),
            pltpu.VMEM((D, QW), bf16),
            pltpu.VMEM((HD, D), bf16),
            pltpu.VMEM((ALL, D), bf16),
            pltpu.VMEM((D, ALL), bf16),
            pltpu.VMEM((ALL, HD), bf16),
            pltpu.VMEM((ALL, HD), bf16),
            pltpu.VMEM((ALL, HD), bf16),
            pltpu.VMEM((ALL, HD), bf16),
            pltpu.VMEM((ALL, HD), bf16),
            pltpu.VMEM((ALL, QW), bf16),
            pltpu.VMEM((ALL, D), f32),
            pltpu.VMEM((D, ALL), bf16),
        ],
        compiler_params=pltpu.CompilerParams(vmem_limit_bytes=44 << 20),
        cost_estimate=pl.CostEstimate(
            flops=6 * 2 * ALL * D * (QW + HD), bytes_accessed=20 << 20, transcendentals=ALL * 128 * HH
        ),
    )(*operands)


def prepare(tokens, cotangent, segment):
    rows32 = tokens.astype(f32)
    centred = rows32 - jnp.mean(rows32, axis=-1, keepdims=True)
    inverse = lax.rsqrt(jnp.mean(centred * centred, axis=-1, keepdims=True) + epsilon)
    live = (segment >= 0).astype(f32)[:, None]
    g = (cotangent.astype(f32) * live).astype(bf16)
    blocks = segment.reshape(BLOCKS, MB_ROWS)
    same = blocks[:, :, None] == blocks[:, None, :]
    earlier = jnp.arange(MB_ROWS)[None, :] <= jnp.arange(MB_ROWS)[:, None]
    allowed = (same & earlier[None]).reshape(ALL, MB_ROWS)
    bias = jnp.where(allowed, 0.0, masked_score)
    place = (jnp.sum(allowed.astype(jnp.int32), axis=1) - 1).astype(f32)
    lane = jnp.arange(128) % HEAD_DIM
    frequency = jnp.exp(
        (lane % 8).astype(f32) * (-2.0 * math.log(10000.0) / ROTARY)
    )
    angle = place[:, None] * frequency[None, :]
    cosine = jnp.where(lane < 16, jnp.cos(angle), 1.0)
    sine = jnp.sin(angle)
    sine_a = jnp.where(lane < 8, -sine, 0.0)
    sine_b = jnp.where((lane >= 8) & (lane < 16), sine, 0.0)
    return centred * inverse, inverse, g, cosine, sine_a, sine_b, bias


def row_maps(core):
    place = jnp.arange(D)[:, None]
    block, inner = place // 12, place % 12
    first, second, third = block // 16, (block // 4) % 4, block % 4
    x = jnp.where(core == 0, first, third)
    z = jnp.where(core == 0, third, first)
    natural = ((x * 4 + second) * 4 + z) * 12 + inner
    order = (natural == jnp.arange(D)[None]).astype(bf16)
    scramble = (block * 6 + inner % 6 == jnp.arange(HD)[None]).astype(bf16)
    spread = (natural == 6 * jnp.arange(128)[None]).astype(bf16)
    return order, scramble, spread


def body(
    tokens,
    cotangent,
    segment,
    ln1_gain,
    ln1_bias,
    qkv_weight,
    qkv_bias,
    out_weight,
    out_bias,
    ln2_gain,
    ln2_bias,
    up_weight,
    up_bias,
    down_weight,
    down_bias,
):
    me = lax.axis_index("fsdp")
    core, z, y, x = me % 2, (me // 2) % 4, (me // 8) % 4, me // 32

    both_tokens = jnp.concatenate([tokens, swap(tokens)], axis=0)
    both_cot = jnp.concatenate([cotangent, swap(cotangent)], axis=0)
    both_segment = jnp.concatenate([segment, swap(segment)], axis=0)
    scaled, inverse, g, cosine, sine_a, sine_b, bias = prepare(
        both_tokens, both_cot, both_segment
    )
    digits = (jnp.where(core == 0, x, z), y, jnp.where(core == 0, z, x))
    at = jnp.stack(digits + (core,)).astype(jnp.int32)
    maps = small_maps(core)
    order, scramble, spread = row_maps(core)

    extra = jnp.zeros((1, 128), bf16)
    start = 0
    for vector in (
        ln1_gain, ln1_bias, qkv_bias, out_bias, ln2_gain, ln2_bias, up_bias, down_bias
    ):
        width = vector.shape[0]
        extra = extra + jnp.pad(vector[None], ((0, 0), (start, 128 - start - width)))
        start += width
    mine, theirs, whole_rows = pack_weights(
        at, qkv_weight, out_weight, up_weight, extra, down_weight
    )
    joint = join_weights(at, mine, swap(theirs), permute(whole_rows, ROW_FROM))
    wide_w, narrow_w = place_first(at, collect(joint, 2))
    wide_w = place_second(at, collect(wide_w, 1))
    wide_w, narrow_w = lax.optimization_barrier((wide_w, narrow_w))
    wide_w = collect(wide_w, 0)
    narrow_w = place_second(at, collect(narrow_w, 1))
    narrow_w = collect(narrow_w, 0)
    mlp0, mlp1, back0, back1, sums, vectors, w0, w1, w2, w3 = run_mlp(
        at, maps, *wide_w, scaled, inverse, g, order, spread
    )
    wide = exchange((w0, w1, w2, w3), 0)
    out0, out1, grad0, grad1, b0, b1, b2, b3 = run_attention(
        at, *narrow_w, scaled, inverse, g, vectors, cosine, sine_a, sine_b, bias,
        order, scramble, spread, maps, sums,
    )
    wide = sum_first(at, w0, wide)
    wide, b0, b1, b2, b3 = lax.optimization_barrier((wide, b0, b1, b2, b3))
    narrow = exchange((b0, b1, b2, b3), 0)
    wide = added(wide[0], exchange(wide, 1))
    narrow = sum_first(at, b0, narrow)
    narrow = added(narrow[0], exchange(narrow, 1))
    blocks = jnp.concatenate([narrow, wide], axis=1).reshape(4, 12, CUT + 2 * HF)
    last = [
        lax.dynamic_index_in_dim(blocks, (digits[2] + rel) % 4, 0, keepdims=False)
        for rel in range(4)
    ]
    last = added(last[0], exchange([last[0]] + [part.astype(bf16) for part in last[1:]], 2))
    narrow, wide = last[:, :CUT], last[:, CUT:]

    down_rows = jnp.concatenate([wide[:, HF : HF + D], wide[:, HF + D :]], axis=0)
    out_rows = jnp.concatenate([narrow[:6, :HD], narrow[6:, :HD]], axis=1)
    own_rows = permute(jnp.concatenate([down_rows, out_rows], axis=0), ROW_PAIRS)
    own_down, own_out = own_rows[:24], own_rows[24:]
    both = jnp.concatenate([narrow[:, HD:], wide[:, :HF]], axis=1).reshape(2, 6, QW + 128 + HF)
    mine = lax.dynamic_index_in_dim(both, core, 0, keepdims=False)
    theirs = swap(lax.dynamic_index_in_dim(both, 1 - core, 0, keepdims=False))
    low = jnp.where(core == 0, mine, theirs)
    high = jnp.where(core == 0, theirs, mine)
    own_qkv = jnp.stack(
        [low[:, :QW].reshape(6, 3, HD), high[:, :QW].reshape(6, 3, HD)], axis=2
    ).reshape(6, 3 * D)
    own_up = jnp.concatenate([low[:, QW + 128 :], high[:, QW + 128 :]], axis=1)
    line = (low + high)[0, QW : QW + 128]
    own = {}
    start = 0
    for name, width in SMALL:
        own[name] = line[start : start + width]
        start += width

    live = (segment >= 0).astype(f32)[:, None]
    out_sum = out0 + mlp0 + swap(out1 + mlp1) + vectors[:, spot("outb")] + vectors[:, spot("downb")]
    output = (tokens.astype(f32) + live * out_sum).astype(bf16)
    grad_tokens = cotangent.astype(f32) + (grad0 + back0 + swap(grad1 + back1))
    return (
        output,
        grad_tokens,
        own["ln1g"],
        own["ln1b"],
        own_qkv,
        own["qkvb"],
        own_out,
        own["outb"],
        own["ln2g"],
        own["ln2b"],
        own_up,
        own["upb"],
        own_down,
        own["downb"],
    )


def solution(mesh):
    row = P("fsdp", None)
    flat = P("fsdp")
    return jax.shard_map(
        body,
        mesh=mesh,
        in_specs=(
            row, row, flat, flat, flat, row, flat, row, flat, flat, flat, row, flat, row, flat,
        ),
        out_specs=(
            row, row, flat, flat, row, flat, row, flat, flat, flat, row, flat, row, flat,
        ),
        check_vma=False,
    )
```

```python
import math

import jax
import jax.numpy as jnp
from jax import lax
from jax.experimental import pallas as pl
from jax.experimental.pallas import tpu as pltpu
from jax.sharding import PartitionSpec as P

D = 768
HEADS = 12
HEAD_DIM = 64
ROTARY = 16
FF = 3072
MB_ROWS = 128
ROWS = 256
HH = HEADS // 2
HD = D // 2
HF = FF // 2
QW = 3 * HD

epsilon = 1e-05
masked_score = -1e30
inv_sqrt_two = 1.0 / math.sqrt(2.0)
inv_sqrt_two_pi = 1.0 / math.sqrt(2.0 * math.pi)
bf16 = jnp.bfloat16
f32 = jnp.float32

STRIDE = {"x": 32, "y": 8, "z": 2, "c": 1}
SIZE = {"x": 4, "y": 4, "z": 4, "c": 2}
SMALL = (("ln1g", 6), ("ln1b", 6), ("qkvb", 18), ("outb", 6), ("ln2g", 6), ("ln2b", 6), ("upb", 24), ("downb", 6))


def digit(index, axis):
    return (index // STRIDE[axis]) % SIZE[axis]


ORDER = (("x", "y", "z"), ("z", "y", "x"))


def shift(axis, step):
    pairs = []
    for source in range(128):
        at = digit(source, axis)
        target = source + ((at + step) % SIZE[axis] - at) * STRIDE[axis]
        pairs.append((source, target))
    return pairs


def stage_shift(stage, step):
    pairs = []
    for source in range(128):
        axis = ORDER[source % 2][stage]
        at = digit(source, axis)
        pairs.append((source, source + ((at + step) % 4 - at) * STRIDE[axis]))
    return pairs


def holder(half, block):
    digits = (block // 16, (block // 4) % 4, block % 4)
    return half + sum(STRIDE[axis] * at for axis, at in zip(ORDER[half], digits))


ROW_PAIRS = [
    (holder(half, block), 64 * half + block) for half in range(2) for block in range(64)
]


ROW_FROM = [(source, target) for target, source in ROW_PAIRS]


def permute(values, pairs):
    return lax.ppermute(values, "fsdp", pairs)


def swap(values):
    return permute(values, shift("c", 1))


def exchange(parts, stage):
    _, after, across, before = parts
    return (
        permute(after, stage_shift(stage, 1)),
        permute(before, stage_shift(stage, -1)),
        permute(across, stage_shift(stage, 2)),
    )


def added(own, arrived):
    total = own.astype(f32)
    for piece in arrived:
        total = total + piece.astype(f32)
    return total


def sum_kernel(at_ref, own_ref, one_ref, two_ref, three_ref, own_out, *outs):
    refs = (own_ref, one_ref, two_ref, three_ref)
    for rel in range(4):
        rs = pl.ds(pl.multiple_of(48 * lax.rem(at_ref[1] + rel, 4), 16), 48)
        total = added(own_ref[rs, :], [ref[rs, :] for ref in refs[1:]])
        if rel == 0:
            own_out[...] = total
        else:
            outs[rel - 1][...] = total.astype(bf16)


def sum_first(at, own, arrived):
    width = own.shape[1]
    return pl.pallas_call(
        sum_kernel,
        out_shape=(struct((48, width), f32),) + (struct((48, width), bf16),) * 3,
        in_specs=[SMEM] + [VMEM] * 4,
        out_specs=(VMEM,) * 4,
        compiler_params=pltpu.CompilerParams(vmem_limit_bytes=12 << 20),
        cost_estimate=pl.CostEstimate(
            flops=4 * 192 * width, bytes_accessed=10 * 192 * width, transcendentals=0
        ),
    )(at, own, *arrived)


CUT = HD + QW + 128
PAIR = QW + HF + 128
WIDE_COLS = 2 * HF + 128
NARROW_COLS = HD + QW


def dot(a, b, dims):
    return lax.dot_general(a, b, (dims, ((), ())), preferred_element_type=f32)


NN = ((1,), (0,))
NT = ((1,), (1,))
TN = ((0,), (0,))
ALL = 2 * ROWS
BLOCKS = ALL // MB_ROWS
WIDE = 6 * D + QW + HF
VMEM = pl.BlockSpec(memory_space=pltpu.VMEM)
SMEM = pl.BlockSpec(memory_space=pltpu.SMEM)
ANY = pl.BlockSpec(memory_space=pl.ANY)


def struct(shape, kind):
    return jax.ShapeDtypeStruct(shape, kind)


def spot(name):
    at = 0
    for key, width in SMALL:
        span = QW if key == "qkvb" else HF if key == "upb" else 128 * width
        if key == name:
            return slice(at, at + span)
        at += span


def small_maps(core, natural):
    device, lane = [], []
    at = 0
    for key, width in SMALL:
        if key == "qkvb":
            flat = (jnp.arange(3)[:, None] * D + core * HD + jnp.arange(HD)[None]).reshape(QW)
        elif key == "upb":
            flat = core * HF + jnp.arange(HF)
        else:
            flat = natural if key.startswith("ln") else jnp.arange(128 * width)
        device.append(flat // width)
        lane.append(at + flat % width)
        at += width
    return jnp.stack([jnp.concatenate(device), jnp.concatenate(lane)]).astype(jnp.int32)


def one_hot(condition):
    return condition.astype(f32).astype(bf16)


def pack_kernel(at_ref, qkv_ref, out_ref, up_ref, extra_ref, down_ref, mine_ref, theirs_ref, rows_ref):
    core = at_ref[3]
    for half, to_ref in ((core, mine_ref), (1 - core, theirs_ref)):
        to_ref[:, QW + HF :] = jnp.zeros((6, 128), bf16)
        to_ref[0:1, QW + HF :] = extra_ref[...]
        for part in range(3):
            begin = pl.multiple_of(part * D + half * HD, 128)
            to_ref[:, part * HD : (part + 1) * HD] = qkv_ref[:, pl.ds(begin, HD)]
        begin = pl.multiple_of(half * HF, 128)
        to_ref[:, QW : QW + HF] = up_ref[:, pl.ds(begin, HF)]
    rows_ref[24:32, :] = jnp.zeros((8, D), bf16)
    rows_ref[0:24, :] = down_ref[...]
    rows_ref[24:30, :] = out_ref[...]


def pack_weights(*operands):
    return pl.pallas_call(
        pack_kernel,
        out_shape=(struct((6, PAIR), bf16), struct((6, PAIR), bf16), struct((32, D), bf16)),
        in_specs=[SMEM] + [VMEM] * 5,
        out_specs=(VMEM,) * 3,
        compiler_params=pltpu.CompilerParams(vmem_limit_bytes=4 << 20),
    )(*operands)


def join_kernel(at_ref, mine_ref, got_ref, rows_ref, to_ref):
    first = at_ref[3] == 0
    mine, got = mine_ref[...].astype(f32), got_ref[...].astype(f32)
    low = jnp.where(first, mine, got).astype(bf16)
    high = jnp.where(first, got, mine).astype(bf16)
    for at, rows in ((0, low), (6, high)):
        to_ref[at : at + 6, :HF] = rows[:, QW : QW + HF]
        to_ref[at : at + 6, 2 * HF : WIDE_COLS] = rows[:, QW + HF :]
        to_ref[at : at + 6, WIDE_COLS + HD :] = rows[:, :QW]
    to_ref[:, HF : HF + D] = rows_ref[0:12, :]
    to_ref[:, HF + D : 2 * HF] = rows_ref[12:24, :]
    to_ref[0:6, WIDE_COLS : WIDE_COLS + HD] = rows_ref[24:30, :HD]
    to_ref[6:12, WIDE_COLS : WIDE_COLS + HD] = rows_ref[24:30, HD:]


def join_weights(*operands):
    return pl.pallas_call(
        join_kernel,
        out_shape=struct((12, WIDE_COLS + NARROW_COLS), bf16),
        in_specs=[SMEM] + [VMEM] * 3,
        out_specs=VMEM,
        compiler_params=pltpu.CompilerParams(vmem_limit_bytes=4 << 20),
    )(*operands)


def collect(block, stage):
    return (
        block,
        permute(block, stage_shift(stage, -1)),
        permute(block, stage_shift(stage, 2)),
        permute(block, stage_shift(stage, 1)),
    )


def first_kernel(at_ref, one, two, three, four, wide_ref, narrow_ref, held_s):
    held_s[...] = jnp.zeros_like(held_s)
    for rel, ref in enumerate((one, two, three, four)):
        held_s[16 * rel : 16 * rel + 12, :] = ref[...]
    row = lax.broadcasted_iota(jnp.int32, (48, 64), 0)
    column = lax.broadcasted_iota(jnp.int32, (48, 64), 1)
    rel = lax.rem(row // 12 - at_ref[2] + 4, 4)
    pick = one_hot(column == 16 * rel + lax.rem(row, 12))
    wide_ref[...] = dot(pick, held_s[:, :WIDE_COLS], NN).astype(bf16)
    narrow_ref[...] = dot(pick, held_s[:, WIDE_COLS:], NN).astype(bf16)


def place_first(at, pieces):
    return pl.pallas_call(
        first_kernel,
        out_shape=(struct((48, WIDE_COLS), bf16), struct((48, NARROW_COLS), bf16)),
        in_specs=[SMEM] + [VMEM] * 4,
        out_specs=(VMEM,) * 2,
        scratch_shapes=[pltpu.VMEM((64, WIDE_COLS + NARROW_COLS), bf16)],
        compiler_params=pltpu.CompilerParams(vmem_limit_bytes=6 << 20),
    )(at, *pieces)


def second_kernel(at_ref, one, two, three, four, to_ref):
    for rel, ref in enumerate((one, two, three, four)):
        begin = pl.multiple_of(48 * lax.rem(at_ref[1] + rel, 4), 16)
        to_ref[pl.ds(begin, 48), :] = ref[...]


def place_second(at, pieces):
    return pl.pallas_call(
        second_kernel,
        out_shape=struct((192, pieces[0].shape[1]), bf16),
        in_specs=[SMEM] + [VMEM] * 4,
        out_specs=VMEM,
        compiler_params=pltpu.CompilerParams(vmem_limit_bytes=6 << 20),
    )(at, *pieces)


def place_third(at_ref, refs, target, sems):
    copies = []
    for rel, ref in enumerate(refs):
        begin = pl.multiple_of(192 * lax.rem(at_ref[0] + rel, 4), 64)
        copies.append(pltpu.make_async_copy(ref, target.at[pl.ds(begin, 192), :], sems.at[rel]))
        copies[-1].start()
    return copies


def spread_small(table, maps_ref, rows_ref):
    step = 2432
    for at in range(0, WIDE, step):
        index = lax.broadcasted_iota(jnp.int32, (128, step), 0)
        hot = one_hot(index == maps_ref[1:2, at : at + step])
        spread = dot(table, hot, NN)
        held = jnp.where(index == maps_ref[0:1, at : at + step], spread, 0.0)
        rows_ref[:, at : at + step] = jnp.sum(held, axis=0, keepdims=True)


def norm_back(upstream, scaled, inverse, gain):
    weighted = upstream * gain
    middle = jnp.mean(weighted, axis=-1, keepdims=True)
    slope = jnp.mean(weighted * scaled, axis=-1, keepdims=True)
    grad_in = inverse * (weighted - middle - scaled * slope)
    gain_sum = jnp.sum(upstream * scaled, axis=0, keepdims=True)
    return grad_in, gain_sum, jnp.sum(upstream, axis=0, keepdims=True)


def mlp_kernel(
    at_ref, maps_ref, p0, p1, p2, p3, scaled_ref, inverse_ref, g_ref, spread_ref,
    mlp0, mlp1, back0, back1, sums_ref, rows_ref, w0, w1, w2, w3,
    held_s, down_ref,
    h_s, ht_s, act_s, order_s, gp_s, gh_s, sems,
):
    copies = place_third(at_ref, (p0, p1, p2, p3), held_s, sems)
    step = 384
    row = lax.broadcasted_iota(jnp.int32, (step, step), 0)
    column = lax.broadcasted_iota(jnp.int32, (step, step), 1)
    block = lax.rem(row, 192) // 12
    wanted = block * 24 + lax.rem(row, 12) + jnp.where(row >= 192, 12, 0)
    deal = one_hot(column == wanted)
    for copy in copies:
        copy.wait()
    table = dot(spread_ref[...], held_s[:, 2 * HF :], TN).astype(bf16)
    spread_small(table, maps_ref, rows_ref)
    for part in range(4):
        rs = slice(192 * part, 192 * part + 192)
        down_ref[step * part : step * (part + 1), :] = (
            dot(deal[:192], held_s[rs, HF : HF + D], TN)
            + dot(deal[192:], held_s[rs, HF + D : 2 * HF], TN)
        ).astype(bf16)
    gain = rows_ref[:, spot("ln2g")]
    h = scaled_ref[...] * gain + rows_ref[:, spot("ln2b")]
    h_s[...] = h.astype(bf16)
    ht_s[...] = h.T.astype(bf16)
    first = spot("upb").start
    for turn_at, at in enumerate(range(0, HF, step)):
        cut = slice(at, at + step)
        pre = dot(h_s[...], held_s[:, cut], NN) + rows_ref[:, first + at : first + at + step]
        cumulative = 0.5 * (1.0 + lax.erf(pre * inv_sqrt_two))
        density = jnp.exp(-0.5 * pre * pre) * inv_sqrt_two_pi
        act = (pre * cumulative).astype(bf16)
        act_s[:, cut] = act
        order_s[turn_at] = dot(deal, act, NT).astype(bf16)
        grad_act = dot(g_ref[...], down_ref[cut, :], NT)
        grad_pre = (grad_act * (cumulative + pre * density)).astype(bf16)
        gp_s[:, cut] = grad_pre
        sums_ref[0:1, cut] = jnp.sum(grad_pre.astype(f32), axis=0, keepdims=True)
    for rel, ref in enumerate((w0, w1, w2, w3)):
        which = lax.rem(at_ref[0] + rel, 4)
        begin = pl.multiple_of(192 * which, 64)
        ref[:, :HF] = dot(ht_s[pl.ds(begin, 192), :], gp_s[...], NN).astype(bf16)
        dealt = order_s[which]
        ref[:, HF : HF + D] = dot(dealt[:192], g_ref[...], NN).astype(bf16)
        ref[:, HF + D :] = dot(dealt[192:], g_ref[...], NN).astype(bf16)
    mlp0[...] = dot(act_s[:ROWS, :], down_ref[...], NN)
    mlp1[...] = dot(act_s[ROWS:, :], down_ref[...], NN)
    gh_s[...] = dot(gp_s[...], held_s[:, :HF], NT)
    back, gain_sum, shift_sum = norm_back(gh_s[...], scaled_ref[...], inverse_ref[...], gain)
    back0[...] = back[:ROWS]
    back1[...] = back[ROWS:]
    sums_ref[1:2, :D] = gain_sum
    sums_ref[2:3, :D] = shift_sum
    sums_ref[3:4, :D] = jnp.sum(g_ref[:ROWS, :].astype(f32), axis=0, keepdims=True)


def run_mlp(*operands):
    return pl.pallas_call(
        mlp_kernel,
        out_shape=(struct((ROWS, D), f32),) * 4
        + (struct((8, HF), f32), struct((1, WIDE), f32))
        + (struct((192, 2 * HF), bf16),) * 4,
        in_specs=[SMEM, VMEM] + [ANY] * 4 + [VMEM] * 4,
        out_specs=(VMEM,) * 10,
        scratch_shapes=[
            pltpu.VMEM((D, WIDE_COLS), bf16),
            pltpu.VMEM((HF, D), bf16),
            pltpu.VMEM((ALL, D), bf16),
            pltpu.VMEM((D, ALL), bf16),
            pltpu.VMEM((ALL, HF), bf16),
            pltpu.VMEM((4, 384, ALL), bf16),
            pltpu.VMEM((ALL, HF), bf16),
            pltpu.VMEM((ALL, D), f32),
            pltpu.SemaphoreType.DMA((4,)),
        ],
        compiler_params=pltpu.CompilerParams(vmem_limit_bytes=38 << 20),
        cost_estimate=pl.CostEstimate(
            flops=8 * 2 * ALL * D * HF, bytes_accessed=20 << 20, transcendentals=2 * ALL * HF
        ),
    )(*operands)


def turn(values, cosine, sine_a, sine_b):
    parts = []
    for at in range(0, values.shape[1], 128):
        part = values[:, at : at + 128]
        parts.append(
            part * cosine
            + pltpu.roll(part, 120, 1) * sine_a
            + pltpu.roll(part, 8, 1) * sine_b
        )
    return jnp.concatenate(parts, axis=1) if len(parts) > 1 else parts[0]


def attention_kernel(
    at_ref, p0, p1, p2, p3, scaled_ref, inverse_ref, g_ref, rows_ref, cos_ref, sina_ref, sinb_ref,
    bias_ref, scramble_ref, spread_ref, maps_ref, sums_ref,
    out0, out1, grad0, grad1, b0, b1, b2, b3,
    held_s, ow_ref,
    h_s, ht_s, q_s, k_s, v_s, ga_s, attn_s, gj_s, gh_s, sa_s, sems,
):
    copies = place_third(at_ref, (p0, p1, p2, p3), held_s, sems)
    gain = rows_ref[:, spot("ln1g")]
    h = scaled_ref[...] * gain + rows_ref[:, spot("ln1b")]
    h_s[...] = h.astype(bf16)
    ht_s[...] = h.T.astype(bf16)
    for copy in copies:
        copy.wait()
    inner = lax.rem(lax.broadcasted_iota(jnp.int32, (D, HD), 0), 12)
    left = scramble_ref[...] * one_hot(inner < 6)
    right = scramble_ref[...] * one_hot(inner >= 6)
    ow_ref[:, :HD] = dot(left, held_s[:, :HD], TN).astype(bf16)
    ow_ref[:, HD:] = dot(right, held_s[:, :HD], TN).astype(bf16)
    first = spot("qkvb").start
    cosine, sine_a, sine_b = cos_ref[...], sina_ref[...], sinb_ref[...]
    for part, ref in enumerate((q_s, k_s, v_s)):
        cut = slice(HD + part * HD, 2 * HD + part * HD)
        bias = rows_ref[:, first + part * HD : first + (part + 1) * HD]
        joint = dot(h_s[...], held_s[:, cut], NN) + bias
        if part < 2:
            joint = turn(joint, cosine, sine_a, sine_b)
        ref[...] = joint.astype(bf16)
    ga_s[...] = dot(g_ref[...], ow_ref[...], NT).astype(bf16)

    scale = HEAD_DIM ** (-0.5)
    lanes = lax.broadcasted_iota(jnp.int32, (MB_ROWS, 128), 1) < HEAD_DIM
    low = lanes.astype(f32).astype(bf16)
    high = (1.0 - lanes.astype(f32)).astype(bf16)

    def one_block(block, carry):
        rs = pl.ds(pl.multiple_of(block * MB_ROWS, MB_ROWS), MB_ROWS)
        bias = bias_ref[rs, :]
        bias = jnp.concatenate([bias, bias], axis=0)
        turn_c, turn_a, turn_b = cos_ref[rs, :], -sina_ref[rs, :], -sinb_ref[rs, :]
        for pair in range(HH // 2):
            cs = slice(pair * 128, pair * 128 + 128)
            qp, kp, vp, ga = q_s[rs, cs], k_s[rs, cs], v_s[rs, cs], ga_s[rs, cs]
            qm = jnp.concatenate([qp * low, qp * high], axis=0)
            gm = jnp.concatenate([ga * low, ga * high], axis=0)
            scores = dot(qm, kp, NT) * scale + bias
            expd = jnp.exp(scores - jnp.max(scores, axis=-1, keepdims=True))
            probs = expd / jnp.sum(expd, axis=-1, keepdims=True)
            p = probs.astype(bf16)
            mixed = dot(p, vp, NN)
            attn_s[rs, cs] = jnp.where(lanes, mixed[:MB_ROWS], mixed[MB_ROWS:]).astype(bf16)
            grad_p = dot(gm, vp, NT)
            grad_v = dot(p, gm, TN)
            delta = jnp.sum(probs * grad_p, axis=-1, keepdims=True)
            ds = (probs * (grad_p - delta)).astype(bf16)
            both = dot(ds, kp, NN)
            grad_q = jnp.where(lanes, both[:MB_ROWS], both[MB_ROWS:]) * scale
            grad_k = dot(ds, qm, TN) * scale
            gj_s[rs, cs] = turn(grad_q, turn_c, turn_a, turn_b).astype(bf16)
            ck = slice(HD + pair * 128, HD + pair * 128 + 128)
            cv = slice(2 * HD + pair * 128, 2 * HD + pair * 128 + 128)
            gj_s[rs, ck] = turn(grad_k, turn_c, turn_a, turn_b).astype(bf16)
            gj_s[rs, cv] = grad_v.astype(bf16)
        return carry

    lax.fori_loop(0, BLOCKS, one_block, 0)

    sa_s[...] = dot(scramble_ref[...], attn_s[...], NT).astype(bf16)
    gh_s[...] = dot(gj_s[...], held_s[:, HD:], NT)
    back, gain_sum, shift_sum = norm_back(gh_s[...], scaled_ref[...], inverse_ref[...], gain)
    grad0[...] = back[:ROWS]
    grad1[...] = back[ROWS:]
    part = dot(attn_s[...], ow_ref[...], NN)
    out0[...] = part[:ROWS]
    out1[...] = part[ROWS:]

    branch = sums_ref[3:4, :D]
    joint_sum = jnp.sum(gj_s[...].astype(f32), axis=0, keepdims=True)
    values = {
        "ln1g": gain_sum,
        "ln1b": shift_sum,
        "qkvb": joint_sum,
        "outb": branch,
        "ln2g": sums_ref[1:2, :D],
        "ln2b": sums_ref[2:3, :D],
        "upb": sums_ref[0:1, :],
        "downb": branch,
    }
    table = jnp.zeros((128, 128), f32)
    for key, _ in SMALL:
        span = spot(key)
        index = lax.broadcasted_iota(jnp.int32, (128, span.stop - span.start), 0)
        hot = (index == maps_ref[1:2, span]).astype(f32).astype(bf16)
        held = jnp.where(index == maps_ref[0:1, span], values[key], 0.0).astype(bf16)
        table = table + dot(held, hot, NT)
    table = table.astype(bf16)
    for rel, ref in enumerate((b0, b1, b2, b3)):
        rs = pl.ds(pl.multiple_of(192 * lax.rem(at_ref[0] + rel, 4), 64), 192)
        one = dot(sa_s[rs, :], g_ref[:, :HD], NN)
        two = dot(sa_s[rs, :], g_ref[:, HD:], NN)
        inner = lax.rem(lax.broadcasted_iota(jnp.int32, (192, HD), 0), 12)
        ref[:, :HD] = jnp.where(inner >= 6, two, one).astype(bf16)
        ref[:, HD : HD + QW] = dot(ht_s[rs, :], gj_s[...], NN).astype(bf16)
        ref[:, HD + QW :] = dot(spread_ref[rs, :], table, NN).astype(bf16)


def run_attention(*operands):
    half = (struct((ROWS, D), f32),) * 4
    return pl.pallas_call(
        attention_kernel,
        out_shape=half + (struct((192, CUT), bf16),) * 4,
        in_specs=[SMEM] + [ANY] * 4 + [VMEM] * (len(operands) - 5),
        out_specs=(VMEM,) * 8,
        scratch_shapes=[
            pltpu.VMEM((D, NARROW_COLS), bf16),
            pltpu.VMEM((HD, D), bf16),
            pltpu.VMEM((ALL, D), bf16),
            pltpu.VMEM((D, ALL), bf16),
            pltpu.VMEM((ALL, HD), bf16),
            pltpu.VMEM((ALL, HD), bf16),
            pltpu.VMEM((ALL, HD), bf16),
            pltpu.VMEM((ALL, HD), bf16),
            pltpu.VMEM((ALL, HD), bf16),
            pltpu.VMEM((ALL, QW), bf16),
            pltpu.VMEM((ALL, D), f32),
            pltpu.VMEM((D, ALL), bf16),
            pltpu.SemaphoreType.DMA((4,)),
        ],
        compiler_params=pltpu.CompilerParams(vmem_limit_bytes=34 << 20),
        cost_estimate=pl.CostEstimate(
            flops=6 * 2 * ALL * D * (QW + HD), bytes_accessed=20 << 20, transcendentals=ALL * 128 * HH
        ),
    )(*operands)


def prepare(tokens, cotangent, segment):
    rows32 = tokens.astype(f32)
    centred = rows32 - jnp.mean(rows32, axis=-1, keepdims=True)
    inverse = lax.rsqrt(jnp.mean(centred * centred, axis=-1, keepdims=True) + epsilon)
    live = (segment >= 0).astype(f32)[:, None]
    g = (cotangent.astype(f32) * live).astype(bf16)
    blocks = segment.reshape(BLOCKS, MB_ROWS)
    same = blocks[:, :, None] == blocks[:, None, :]
    earlier = jnp.arange(MB_ROWS)[None, :] <= jnp.arange(MB_ROWS)[:, None]
    allowed = (same & earlier[None]).reshape(ALL, MB_ROWS)
    bias = jnp.where(allowed, 0.0, masked_score)
    place = (jnp.sum(allowed.astype(jnp.int32), axis=1) - 1).astype(f32)
    lane = jnp.arange(128) % HEAD_DIM
    frequency = jnp.exp(
        (lane % 8).astype(f32) * (-2.0 * math.log(10000.0) / ROTARY)
    )
    angle = place[:, None] * frequency[None, :]
    cosine = jnp.where(lane < 16, jnp.cos(angle), 1.0)
    sine = jnp.sin(angle)
    sine_a = jnp.where(lane < 8, -sine, 0.0)
    sine_b = jnp.where((lane >= 8) & (lane < 16), sine, 0.0)
    return centred * inverse, inverse, g, cosine, sine_a, sine_b, bias


def row_maps(core):
    place = jnp.arange(D)[:, None]
    block, inner = place // 12, place % 12
    first, second, third = block // 16, (block // 4) % 4, block % 4
    x = jnp.where(core == 0, first, third)
    z = jnp.where(core == 0, third, first)
    natural = ((x * 4 + second) * 4 + z) * 12 + inner
    order = (natural == jnp.arange(D)[None]).astype(bf16)
    scramble = (block * 6 + inner % 6 == jnp.arange(HD)[None]).astype(bf16)
    spread = (natural == 6 * jnp.arange(128)[None]).astype(bf16)
    return natural[:, 0], order, scramble, spread


def body(
    tokens,
    cotangent,
    segment,
    ln1_gain,
    ln1_bias,
    qkv_weight,
    qkv_bias,
    out_weight,
    out_bias,
    ln2_gain,
    ln2_bias,
    up_weight,
    up_bias,
    down_weight,
    down_bias,
):
    me = lax.axis_index("fsdp")
    core, z, y, x = me % 2, (me // 2) % 4, (me // 8) % 4, me // 32

    both_tokens = jnp.concatenate([tokens, swap(tokens)], axis=0)
    both_cot = jnp.concatenate([cotangent, swap(cotangent)], axis=0)
    both_segment = jnp.concatenate([segment, swap(segment)], axis=0)
    digits = (jnp.where(core == 0, x, z), y, jnp.where(core == 0, z, x))
    at = jnp.stack(digits + (core,)).astype(jnp.int32)
    natural, order, scramble, spread = row_maps(core)
    maps = small_maps(core, natural)
    scaled, inverse, g, cosine, sine_a, sine_b, bias = prepare(
        dot(both_tokens, order, NT).astype(bf16), both_cot, both_segment
    )

    extra = jnp.zeros((1, 128), bf16)
    start = 0
    for vector in (
        ln1_gain, ln1_bias, qkv_bias, out_bias, ln2_gain, ln2_bias, up_bias, down_bias
    ):
        width = vector.shape[0]
        extra = extra + jnp.pad(vector[None], ((0, 0), (start, 128 - start - width)))
        start += width
    mine, theirs, whole_rows = pack_weights(
        at, qkv_weight, out_weight, up_weight, extra, down_weight
    )
    joint = join_weights(at, mine, swap(theirs), permute(whole_rows, ROW_FROM))
    wide_w, narrow_w = place_first(at, collect(joint, 2))
    wide_w = place_second(at, collect(wide_w, 1))
    wide_w, narrow_w = lax.optimization_barrier((wide_w, narrow_w))
    wide_w = collect(wide_w, 0)
    narrow_w = place_second(at, collect(narrow_w, 1))
    narrow_w = collect(narrow_w, 0)
    mlp0, mlp1, back0, back1, sums, vectors, w0, w1, w2, w3 = run_mlp(
        at, maps, *wide_w, scaled, inverse, g, spread
    )
    wide = exchange((w0, w1, w2, w3), 0)
    out0, out1, grad0, grad1, b0, b1, b2, b3 = run_attention(
        at, *narrow_w, scaled, inverse, g, vectors, cosine, sine_a, sine_b, bias,
        scramble, spread, maps, sums,
    )
    wide, b0, b1, b2, b3 = lax.optimization_barrier((wide, b0, b1, b2, b3))
    narrow = exchange((b0, b1, b2, b3), 0)
    wide = sum_first(at, w0, wide)
    wide = added(wide[0], exchange(wide, 1))
    narrow = sum_first(at, b0, narrow)
    narrow = added(narrow[0], exchange(narrow, 1))
    blocks = jnp.concatenate([narrow, wide], axis=1).reshape(4, 12, CUT + 2 * HF)
    last = [
        lax.dynamic_index_in_dim(blocks, (digits[2] + rel) % 4, 0, keepdims=False)
        for rel in range(4)
    ]
    last = added(last[0], exchange([last[0]] + [part.astype(bf16) for part in last[1:]], 2))
    narrow, wide = last[:, :CUT], last[:, CUT:]

    down_rows = jnp.concatenate([wide[:, HF : HF + D], wide[:, HF + D :]], axis=0)
    out_rows = jnp.concatenate([narrow[:6, :HD], narrow[6:, :HD]], axis=1)
    own_rows = permute(jnp.concatenate([down_rows, out_rows], axis=0), ROW_PAIRS)
    own_down, own_out = own_rows[:24], own_rows[24:]
    both = jnp.concatenate([narrow[:, HD:], wide[:, :HF]], axis=1).reshape(2, 6, QW + 128 + HF)
    mine = lax.dynamic_index_in_dim(both, core, 0, keepdims=False)
    theirs = swap(lax.dynamic_index_in_dim(both, 1 - core, 0, keepdims=False))
    low = jnp.where(core == 0, mine, theirs)
    high = jnp.where(core == 0, theirs, mine)
    own_qkv = jnp.stack(
        [low[:, :QW].reshape(6, 3, HD), high[:, :QW].reshape(6, 3, HD)], axis=2
    ).reshape(6, 3 * D)
    own_up = jnp.concatenate([low[:, QW + 128 :], high[:, QW + 128 :]], axis=1)
    line = (low + high)[0, QW : QW + 128]
    own = {}
    start = 0
    for name, width in SMALL:
        own[name] = line[start : start + width]
        start += width

    live = (segment >= 0).astype(f32)[:, None]
    out_sum = out0 + mlp0 + swap(out1 + mlp1) + vectors[:, spot("outb")] + vectors[:, spot("downb")]
    output = (tokens.astype(f32) + live * out_sum).astype(bf16)
    def restore(values):
        return lax.dot_general(
            values, order.astype(f32), (NN, ((), ())), precision=lax.Precision.HIGHEST
        )

    grad_tokens = cotangent.astype(f32) + (restore(grad0 + back0) + swap(restore(grad1 + back1)))
    return (
        output,
        grad_tokens,
        own["ln1g"],
        own["ln1b"],
        own_qkv,
        own["qkvb"],
        own_out,
        own["outb"],
        own["ln2g"],
        own["ln2b"],
        own_up,
        own["upb"],
        own_down,
        own["downb"],
    )


def solution(mesh):
    row = P("fsdp", None)
    flat = P("fsdp")
    return jax.shard_map(
        body,
        mesh=mesh,
        in_specs=(
            row, row, flat, flat, flat, row, flat, row, flat, flat, flat, row, flat, row, flat,
        ),
        out_specs=(
            row, row, flat, flat, row, flat, row, flat, flat, flat, row, flat, row, flat,
        ),
        check_vma=False,
    )
```

```python
import math

import jax
import jax.numpy as jnp
from jax import lax
from jax.experimental import pallas as pl
from jax.experimental.pallas import tpu as pltpu
from jax.sharding import PartitionSpec as P

D = 768
HEADS = 12
HEAD_DIM = 64
ROTARY = 16
FF = 3072
MB_ROWS = 128
ROWS = 256
HH = HEADS // 2
HD = D // 2
HF = FF // 2
QW = 3 * HD

epsilon = 1e-05
masked_score = -1e30
inv_sqrt_two = 1.0 / math.sqrt(2.0)
inv_sqrt_two_pi = 1.0 / math.sqrt(2.0 * math.pi)
bf16 = jnp.bfloat16
f32 = jnp.float32

STRIDE = {"x": 32, "y": 8, "z": 2, "c": 1}
SIZE = {"x": 4, "y": 4, "z": 4, "c": 2}
SMALL = (("ln1g", 6), ("ln1b", 6), ("qkvb", 18), ("outb", 6), ("ln2g", 6), ("ln2b", 6), ("upb", 24), ("downb", 6))


def digit(index, axis):
    return (index // STRIDE[axis]) % SIZE[axis]


ORDER = (("x", "y", "z"), ("z", "y", "x"))


def shift(axis, step):
    pairs = []
    for source in range(128):
        at = digit(source, axis)
        target = source + ((at + step) % SIZE[axis] - at) * STRIDE[axis]
        pairs.append((source, target))
    return pairs


def stage_shift(stage, step):
    pairs = []
    for source in range(128):
        axis = ORDER[source % 2][stage]
        at = digit(source, axis)
        pairs.append((source, source + ((at + step) % 4 - at) * STRIDE[axis]))
    return pairs


def holder(half, block):
    digits = (block // 16, (block // 4) % 4, block % 4)
    return half + sum(STRIDE[axis] * at for axis, at in zip(ORDER[half], digits))


ROW_PAIRS = [
    (holder(half, block), 64 * half + block) for half in range(2) for block in range(64)
]


ROW_FROM = [(source, target) for target, source in ROW_PAIRS]


def permute(values, pairs):
    return lax.ppermute(values, "fsdp", pairs)


def swap(values):
    return permute(values, shift("c", 1))


def exchange(parts, stage):
    _, after, across, before = parts
    return (
        permute(after, stage_shift(stage, 1)),
        permute(before, stage_shift(stage, -1)),
        permute(across, stage_shift(stage, 2)),
    )


def added(own, arrived):
    total = own.astype(f32)
    for piece in arrived:
        total = total + piece.astype(f32)
    return total


def sum_kernel(at_ref, own_ref, one_ref, two_ref, three_ref, own_out, *outs):
    refs = (own_ref, one_ref, two_ref, three_ref)
    for rel in range(4):
        rs = pl.ds(pl.multiple_of(48 * lax.rem(at_ref[1] + rel, 4), 16), 48)
        total = added(own_ref[rs, :], [ref[rs, :] for ref in refs[1:]])
        if rel == 0:
            own_out[...] = total
        else:
            outs[rel - 1][...] = total.astype(bf16)


def sum_first(at, own, arrived):
    width = own.shape[1]
    return pl.pallas_call(
        sum_kernel,
        out_shape=(struct((48, width), f32),) + (struct((48, width), bf16),) * 3,
        in_specs=[SMEM] + [VMEM] * 4,
        out_specs=(VMEM,) * 4,
        compiler_params=pltpu.CompilerParams(vmem_limit_bytes=12 << 20),
        cost_estimate=pl.CostEstimate(
            flops=4 * 192 * width, bytes_accessed=10 * 192 * width, transcendentals=0
        ),
    )(at, own, *arrived)


CUT = HD + QW + 128
PAIR = QW + HF + 128
WIDE_COLS = 2 * HF + 128
NARROW_COLS = HD + QW


def dot(a, b, dims):
    return lax.dot_general(a, b, (dims, ((), ())), preferred_element_type=f32)


NN = ((1,), (0,))
NT = ((1,), (1,))
TN = ((0,), (0,))
ALL = 2 * ROWS
BLOCKS = ALL // MB_ROWS
WIDE = 6 * D + QW + HF
VMEM = pl.BlockSpec(memory_space=pltpu.VMEM)
SMEM = pl.BlockSpec(memory_space=pltpu.SMEM)
ANY = pl.BlockSpec(memory_space=pl.ANY)


def struct(shape, kind):
    return jax.ShapeDtypeStruct(shape, kind)


def spot(name):
    at = 0
    for key, width in SMALL:
        span = QW if key == "qkvb" else HF if key == "upb" else 128 * width
        if key == name:
            return slice(at, at + span)
        at += span


def small_maps(core, natural):
    device, lane = [], []
    at = 0
    for key, width in SMALL:
        if key == "qkvb":
            flat = (jnp.arange(3)[:, None] * D + core * HD + jnp.arange(HD)[None]).reshape(QW)
        elif key == "upb":
            flat = core * HF + jnp.arange(HF)
        else:
            flat = natural if key.startswith("ln") else jnp.arange(128 * width)
        device.append(flat // width)
        lane.append(at + flat % width)
        at += width
    return jnp.stack([jnp.concatenate(device), jnp.concatenate(lane)]).astype(jnp.int32)


def one_hot(condition):
    return condition.astype(f32).astype(bf16)


def pack_kernel(at_ref, qkv_ref, out_ref, up_ref, extra_ref, down_ref, mine_ref, theirs_ref, rows_ref):
    core = at_ref[3]
    for half, to_ref in ((core, mine_ref), (1 - core, theirs_ref)):
        to_ref[:, QW + HF :] = jnp.zeros((6, 128), bf16)
        to_ref[0:1, QW + HF :] = extra_ref[...]
        for part in range(3):
            begin = pl.multiple_of(part * D + half * HD, 128)
            to_ref[:, part * HD : (part + 1) * HD] = qkv_ref[:, pl.ds(begin, HD)]
        begin = pl.multiple_of(half * HF, 128)
        to_ref[:, QW : QW + HF] = up_ref[:, pl.ds(begin, HF)]
    rows_ref[24:32, :] = jnp.zeros((8, D), bf16)
    rows_ref[0:24, :] = down_ref[...]
    rows_ref[24:30, :] = out_ref[...]


def pack_weights(*operands):
    return pl.pallas_call(
        pack_kernel,
        out_shape=(struct((6, PAIR), bf16), struct((6, PAIR), bf16), struct((32, D), bf16)),
        in_specs=[SMEM] + [VMEM] * 5,
        out_specs=(VMEM,) * 3,
        compiler_params=pltpu.CompilerParams(vmem_limit_bytes=4 << 20),
    )(*operands)


def join_kernel(at_ref, mine_ref, got_ref, rows_ref, to_ref):
    first = at_ref[3] == 0
    mine, got = mine_ref[...].astype(f32), got_ref[...].astype(f32)
    low = jnp.where(first, mine, got).astype(bf16)
    high = jnp.where(first, got, mine).astype(bf16)
    for at, rows in ((0, low), (6, high)):
        to_ref[at : at + 6, :HF] = rows[:, QW : QW + HF]
        to_ref[at : at + 6, 2 * HF : WIDE_COLS] = rows[:, QW + HF :]
        to_ref[at : at + 6, WIDE_COLS + HD :] = rows[:, :QW]
    to_ref[:, HF : HF + D] = rows_ref[0:12, :]
    to_ref[:, HF + D : 2 * HF] = rows_ref[12:24, :]
    to_ref[0:6, WIDE_COLS : WIDE_COLS + HD] = rows_ref[24:30, :HD]
    to_ref[6:12, WIDE_COLS : WIDE_COLS + HD] = rows_ref[24:30, HD:]


def join_weights(*operands):
    return pl.pallas_call(
        join_kernel,
        out_shape=struct((12, WIDE_COLS + NARROW_COLS), bf16),
        in_specs=[SMEM] + [VMEM] * 3,
        out_specs=VMEM,
        compiler_params=pltpu.CompilerParams(vmem_limit_bytes=4 << 20),
    )(*operands)


def collect(block, stage):
    return (
        block,
        permute(block, stage_shift(stage, -1)),
        permute(block, stage_shift(stage, 2)),
        permute(block, stage_shift(stage, 1)),
    )


def first_kernel(at_ref, one, two, three, four, wide_ref, narrow_ref, held_s):
    held_s[...] = jnp.zeros_like(held_s)
    for rel, ref in enumerate((one, two, three, four)):
        held_s[16 * rel : 16 * rel + 12, :] = ref[...]
    row = lax.broadcasted_iota(jnp.int32, (48, 64), 0)
    column = lax.broadcasted_iota(jnp.int32, (48, 64), 1)
    rel = lax.rem(row // 12 - at_ref[2] + 4, 4)
    pick = one_hot(column == 16 * rel + lax.rem(row, 12))
    wide_ref[...] = dot(pick, held_s[:, :WIDE_COLS], NN).astype(bf16)
    narrow_ref[...] = dot(pick, held_s[:, WIDE_COLS:], NN).astype(bf16)


def place_first(at, pieces):
    return pl.pallas_call(
        first_kernel,
        out_shape=(struct((48, WIDE_COLS), bf16), struct((48, NARROW_COLS), bf16)),
        in_specs=[SMEM] + [VMEM] * 4,
        out_specs=(VMEM,) * 2,
        scratch_shapes=[pltpu.VMEM((64, WIDE_COLS + NARROW_COLS), bf16)],
        compiler_params=pltpu.CompilerParams(vmem_limit_bytes=6 << 20),
    )(at, *pieces)


def second_kernel(at_ref, one, two, three, four, to_ref):
    for rel, ref in enumerate((one, two, three, four)):
        begin = pl.multiple_of(48 * lax.rem(at_ref[1] + rel, 4), 16)
        to_ref[pl.ds(begin, 48), :] = ref[...]


def place_second(at, pieces):
    return pl.pallas_call(
        second_kernel,
        out_shape=struct((192, pieces[0].shape[1]), bf16),
        in_specs=[SMEM] + [VMEM] * 4,
        out_specs=VMEM,
        compiler_params=pltpu.CompilerParams(vmem_limit_bytes=6 << 20),
    )(at, *pieces)


def place_third(at_ref, refs, target, sems):
    copies = []
    for rel, ref in enumerate(refs):
        begin = pl.multiple_of(192 * lax.rem(at_ref[0] + rel, 4), 64)
        copies.append(pltpu.make_async_copy(ref, target.at[pl.ds(begin, 192), :], sems.at[rel]))
        copies[-1].start()
    return copies


def spread_small(table, maps_ref, rows_ref):
    step = 2432
    for at in range(0, WIDE, step):
        index = lax.broadcasted_iota(jnp.int32, (128, step), 0)
        hot = one_hot(index == maps_ref[1:2, at : at + step])
        spread = dot(table, hot, NN)
        held = jnp.where(index == maps_ref[0:1, at : at + step], spread, 0.0)
        rows_ref[:, at : at + step] = jnp.sum(held, axis=0, keepdims=True)


def norm_back(upstream, scaled, inverse, gain):
    weighted = upstream * gain
    middle = jnp.mean(weighted, axis=-1, keepdims=True)
    slope = jnp.mean(weighted * scaled, axis=-1, keepdims=True)
    grad_in = inverse * (weighted - middle - scaled * slope)
    gain_sum = jnp.sum(upstream * scaled, axis=0, keepdims=True)
    return grad_in, gain_sum, jnp.sum(upstream, axis=0, keepdims=True)


def mlp_kernel(
    at_ref, maps_ref, p0, p1, p2, p3, scaled_ref, inverse_ref, g_ref, spread_ref,
    mlp0, mlp1, back0, back1, sums_ref, rows_ref, w0, w1, w2, w3,
    held_s, down_ref,
    h_s, ht_s, act_s, order_s, gp_s, gh_s, sems,
):
    copies = place_third(at_ref, (p0, p1, p2, p3), held_s, sems)
    step = 384
    row = lax.broadcasted_iota(jnp.int32, (step, step), 0)
    column = lax.broadcasted_iota(jnp.int32, (step, step), 1)
    block = lax.rem(row, 192) // 12
    wanted = block * 24 + lax.rem(row, 12) + jnp.where(row >= 192, 12, 0)
    deal = one_hot(column == wanted)
    for copy in copies:
        copy.wait()
    table = dot(spread_ref[...], held_s[:, 2 * HF :], TN).astype(bf16)
    spread_small(table, maps_ref, rows_ref)
    for part in range(4):
        rs = slice(192 * part, 192 * part + 192)
        down_ref[step * part : step * (part + 1), :] = (
            dot(deal[:192], held_s[rs, HF : HF + D], TN)
            + dot(deal[192:], held_s[rs, HF + D : 2 * HF], TN)
        ).astype(bf16)
    gain = rows_ref[:, spot("ln2g")]
    h = scaled_ref[...] * gain + rows_ref[:, spot("ln2b")]
    h_s[...] = h.astype(bf16)
    ht_s[...] = h.T.astype(bf16)
    first = spot("upb").start
    for turn_at, at in enumerate(range(0, HF, step)):
        cut = slice(at, at + step)
        pre = dot(h_s[...], held_s[:, cut], NN) + rows_ref[:, first + at : first + at + step]
        cumulative = 0.5 * (1.0 + lax.erf(pre * inv_sqrt_two))
        density = jnp.exp(-0.5 * pre * pre) * inv_sqrt_two_pi
        act = (pre * cumulative).astype(bf16)
        act_s[:, cut] = act
        order_s[turn_at] = dot(deal, act, NT).astype(bf16)
        grad_act = dot(g_ref[...], down_ref[cut, :], NT)
        grad_pre = (grad_act * (cumulative + pre * density)).astype(bf16)
        gp_s[:, cut] = grad_pre
        sums_ref[0:1, cut] = jnp.sum(grad_pre.astype(f32), axis=0, keepdims=True)
    for rel, ref in enumerate((w0, w1, w2, w3)):
        which = lax.rem(at_ref[0] + rel, 4)
        begin = pl.multiple_of(192 * which, 64)
        ref[:, :HF] = dot(ht_s[pl.ds(begin, 192), :], gp_s[...], NN).astype(bf16)
        dealt = order_s[which]
        ref[:, HF : HF + D] = dot(dealt[:192], g_ref[...], NN).astype(bf16)
        ref[:, HF + D :] = dot(dealt[192:], g_ref[...], NN).astype(bf16)
    mlp0[...] = dot(act_s[:ROWS, :], down_ref[...], NN)
    mlp1[...] = dot(act_s[ROWS:, :], down_ref[...], NN)
    gh_s[...] = dot(gp_s[...], held_s[:, :HF], NT)
    back, gain_sum, shift_sum = norm_back(gh_s[...], scaled_ref[...], inverse_ref[...], gain)
    back0[...] = back[:ROWS]
    back1[...] = back[ROWS:]
    sums_ref[1:2, :D] = gain_sum
    sums_ref[2:3, :D] = shift_sum
    sums_ref[3:4, :D] = jnp.sum(g_ref[:ROWS, :].astype(f32), axis=0, keepdims=True)


def run_mlp(*operands):
    return pl.pallas_call(
        mlp_kernel,
        out_shape=(struct((ROWS, D), f32),) * 4
        + (struct((8, HF), f32), struct((1, WIDE), f32))
        + (struct((192, 2 * HF), bf16),) * 4,
        in_specs=[SMEM, VMEM] + [ANY] * 4 + [VMEM] * 4,
        out_specs=(VMEM,) * 10,
        scratch_shapes=[
            pltpu.VMEM((D, WIDE_COLS), bf16),
            pltpu.VMEM((HF, D), bf16),
            pltpu.VMEM((ALL, D), bf16),
            pltpu.VMEM((D, ALL), bf16),
            pltpu.VMEM((ALL, HF), bf16),
            pltpu.VMEM((4, 384, ALL), bf16),
            pltpu.VMEM((ALL, HF), bf16),
            pltpu.VMEM((ALL, D), f32),
            pltpu.SemaphoreType.DMA((4,)),
        ],
        compiler_params=pltpu.CompilerParams(vmem_limit_bytes=38 << 20),
        cost_estimate=pl.CostEstimate(
            flops=8 * 2 * ALL * D * HF, bytes_accessed=20 << 20, transcendentals=2 * ALL * HF
        ),
    )(*operands)


def turn(values, cosine, sine_a, sine_b):
    parts = []
    for at in range(0, values.shape[1], 128):
        part = values[:, at : at + 128]
        parts.append(
            part * cosine
            + pltpu.roll(part, 120, 1) * sine_a
            + pltpu.roll(part, 8, 1) * sine_b
        )
    return jnp.concatenate(parts, axis=1) if len(parts) > 1 else parts[0]


def attention_kernel(
    at_ref, p0, p1, p2, p3, scaled_ref, inverse_ref, g_ref, rows_ref, cos_ref, sina_ref, sinb_ref,
    bias_ref, scramble_ref, spread_ref, maps_ref, sums_ref,
    out0, out1, grad0, grad1, b0, b1, b2, b3,
    held_s, ow_ref,
    h_s, ht_s, q_s, k_s, v_s, ga_s, attn_s, gj_s, gh_s, sa_s, sems,
):
    copies = place_third(at_ref, (p0, p1, p2, p3), held_s, sems)
    gain = rows_ref[:, spot("ln1g")]
    h = scaled_ref[...] * gain + rows_ref[:, spot("ln1b")]
    h_s[...] = h.astype(bf16)
    ht_s[...] = h.T.astype(bf16)
    for copy in copies:
        copy.wait()
    inner = lax.rem(lax.broadcasted_iota(jnp.int32, (D, HD), 0), 12)
    left = scramble_ref[...] * one_hot(inner < 6)
    right = scramble_ref[...] * one_hot(inner >= 6)
    ow_ref[:, :HD] = dot(left, held_s[:, :HD], TN).astype(bf16)
    ow_ref[:, HD:] = dot(right, held_s[:, :HD], TN).astype(bf16)
    first = spot("qkvb").start
    cosine, sine_a, sine_b = cos_ref[...], sina_ref[...], sinb_ref[...]
    for part, ref in enumerate((q_s, k_s, v_s)):
        cut = slice(HD + part * HD, 2 * HD + part * HD)
        bias = rows_ref[:, first + part * HD : first + (part + 1) * HD]
        joint = dot(h_s[...], held_s[:, cut], NN) + bias
        if part < 2:
            joint = turn(joint, cosine, sine_a, sine_b)
        ref[...] = joint.astype(bf16)
    ga_s[...] = dot(g_ref[...], ow_ref[...], NT).astype(bf16)

    scale = HEAD_DIM ** (-0.5)
    lanes = lax.broadcasted_iota(jnp.int32, (MB_ROWS, 128), 1) < HEAD_DIM
    low = lanes.astype(f32).astype(bf16)
    high = (1.0 - lanes.astype(f32)).astype(bf16)

    def one_block(block, carry):
        rs = pl.ds(pl.multiple_of(block * MB_ROWS, MB_ROWS), MB_ROWS)
        bias = bias_ref[rs, :]
        bias = jnp.concatenate([bias, bias], axis=0)
        turn_c, turn_a, turn_b = cos_ref[rs, :], -sina_ref[rs, :], -sinb_ref[rs, :]
        for pair in range(HH // 2):
            cs = slice(pair * 128, pair * 128 + 128)
            qp, kp, vp, ga = q_s[rs, cs], k_s[rs, cs], v_s[rs, cs], ga_s[rs, cs]
            qm = jnp.concatenate([qp * low, qp * high], axis=0)
            gm = jnp.concatenate([ga * low, ga * high], axis=0)
            scores = dot(qm, kp, NT) * scale + bias
            expd = jnp.exp(scores - jnp.max(scores, axis=-1, keepdims=True))
            probs = expd / jnp.sum(expd, axis=-1, keepdims=True)
            p = probs.astype(bf16)
            mixed = dot(p, vp, NN)
            attn_s[rs, cs] = jnp.where(lanes, mixed[:MB_ROWS], mixed[MB_ROWS:]).astype(bf16)
            grad_p = dot(gm, vp, NT)
            grad_v = dot(p, gm, TN)
            delta = jnp.sum(probs * grad_p, axis=-1, keepdims=True)
            ds = (probs * (grad_p - delta)).astype(bf16)
            both = dot(ds, kp, NN)
            grad_q = jnp.where(lanes, both[:MB_ROWS], both[MB_ROWS:]) * scale
            grad_k = dot(ds, qm, TN) * scale
            gj_s[rs, cs] = turn(grad_q, turn_c, turn_a, turn_b).astype(bf16)
            ck = slice(HD + pair * 128, HD + pair * 128 + 128)
            cv = slice(2 * HD + pair * 128, 2 * HD + pair * 128 + 128)
            gj_s[rs, ck] = turn(grad_k, turn_c, turn_a, turn_b).astype(bf16)
            gj_s[rs, cv] = grad_v.astype(bf16)
        return carry

    lax.fori_loop(0, BLOCKS, one_block, 0)

    sa_s[...] = dot(scramble_ref[...], attn_s[...], NT).astype(bf16)
    gh_s[...] = dot(gj_s[...], held_s[:, HD:], NT)
    back, gain_sum, shift_sum = norm_back(gh_s[...], scaled_ref[...], inverse_ref[...], gain)
    grad0[...] = back[:ROWS]
    grad1[...] = back[ROWS:]
    part = dot(attn_s[...], ow_ref[...], NN)
    out0[...] = part[:ROWS]
    out1[...] = part[ROWS:]

    branch = sums_ref[3:4, :D]
    joint_sum = jnp.sum(gj_s[...].astype(f32), axis=0, keepdims=True)
    values = {
        "ln1g": gain_sum,
        "ln1b": shift_sum,
        "qkvb": joint_sum,
        "outb": branch,
        "ln2g": sums_ref[1:2, :D],
        "ln2b": sums_ref[2:3, :D],
        "upb": sums_ref[0:1, :],
        "downb": branch,
    }
    table = jnp.zeros((128, 128), f32)
    for key, _ in SMALL:
        span = spot(key)
        index = lax.broadcasted_iota(jnp.int32, (128, span.stop - span.start), 0)
        hot = (index == maps_ref[1:2, span]).astype(f32).astype(bf16)
        held = jnp.where(index == maps_ref[0:1, span], values[key], 0.0).astype(bf16)
        table = table + dot(held, hot, NT)
    table = table.astype(bf16)
    for rel, ref in enumerate((b0, b1, b2, b3)):
        rs = pl.ds(pl.multiple_of(192 * lax.rem(at_ref[0] + rel, 4), 64), 192)
        one = dot(sa_s[rs, :], g_ref[:, :HD], NN)
        two = dot(sa_s[rs, :], g_ref[:, HD:], NN)
        inner = lax.rem(lax.broadcasted_iota(jnp.int32, (192, HD), 0), 12)
        ref[:, :HD] = jnp.where(inner >= 6, two, one).astype(bf16)
        ref[:, HD : HD + QW] = dot(ht_s[rs, :], gj_s[...], NN).astype(bf16)
        ref[:, HD + QW :] = dot(spread_ref[rs, :], table, NN).astype(bf16)


def run_attention(*operands):
    half = (struct((ROWS, D), f32),) * 4
    return pl.pallas_call(
        attention_kernel,
        out_shape=half + (struct((192, CUT), bf16),) * 4,
        in_specs=[SMEM] + [ANY] * 4 + [VMEM] * (len(operands) - 5),
        out_specs=(VMEM,) * 8,
        scratch_shapes=[
            pltpu.VMEM((D, NARROW_COLS), bf16),
            pltpu.VMEM((HD, D), bf16),
            pltpu.VMEM((ALL, D), bf16),
            pltpu.VMEM((D, ALL), bf16),
            pltpu.VMEM((ALL, HD), bf16),
            pltpu.VMEM((ALL, HD), bf16),
            pltpu.VMEM((ALL, HD), bf16),
            pltpu.VMEM((ALL, HD), bf16),
            pltpu.VMEM((ALL, HD), bf16),
            pltpu.VMEM((ALL, QW), bf16),
            pltpu.VMEM((ALL, D), f32),
            pltpu.VMEM((D, ALL), bf16),
            pltpu.SemaphoreType.DMA((4,)),
        ],
        compiler_params=pltpu.CompilerParams(vmem_limit_bytes=34 << 20),
        cost_estimate=pl.CostEstimate(
            flops=6 * 2 * ALL * D * (QW + HD), bytes_accessed=20 << 20, transcendentals=ALL * 128 * HH
        ),
    )(*operands)


def prepare(tokens, cotangent, segment):
    rows32 = tokens.astype(f32)
    centred = rows32 - jnp.mean(rows32, axis=-1, keepdims=True)
    inverse = lax.rsqrt(jnp.mean(centred * centred, axis=-1, keepdims=True) + epsilon)
    live = (segment >= 0).astype(f32)[:, None]
    g = (cotangent.astype(f32) * live).astype(bf16)
    blocks = segment.reshape(BLOCKS, MB_ROWS)
    same = blocks[:, :, None] == blocks[:, None, :]
    earlier = jnp.arange(MB_ROWS)[None, :] <= jnp.arange(MB_ROWS)[:, None]
    allowed = (same & earlier[None]).reshape(ALL, MB_ROWS)
    bias = jnp.where(allowed, 0.0, masked_score)
    place = (jnp.sum(allowed.astype(jnp.int32), axis=1) - 1).astype(f32)
    lane = jnp.arange(128) % HEAD_DIM
    frequency = jnp.exp(
        (lane % 8).astype(f32) * (-2.0 * math.log(10000.0) / ROTARY)
    )
    angle = place[:, None] * frequency[None, :]
    cosine = jnp.where(lane < 16, jnp.cos(angle), 1.0)
    sine = jnp.sin(angle)
    sine_a = jnp.where(lane < 8, -sine, 0.0)
    sine_b = jnp.where((lane >= 8) & (lane < 16), sine, 0.0)
    return centred * inverse, inverse, g, cosine, sine_a, sine_b, bias


def row_maps(core):
    place = jnp.arange(D)[:, None]
    block, inner = place // 12, place % 12
    first, second, third = block // 16, (block // 4) % 4, block % 4
    x = jnp.where(core == 0, first, third)
    z = jnp.where(core == 0, third, first)
    natural = ((x * 4 + second) * 4 + z) * 12 + inner
    order = (natural == jnp.arange(D)[None]).astype(bf16)
    scramble = (block * 6 + inner % 6 == jnp.arange(HD)[None]).astype(bf16)
    spread = (natural == 6 * jnp.arange(128)[None]).astype(bf16)
    return natural[:, 0], order, scramble, spread


def body(
    tokens,
    cotangent,
    segment,
    ln1_gain,
    ln1_bias,
    qkv_weight,
    qkv_bias,
    out_weight,
    out_bias,
    ln2_gain,
    ln2_bias,
    up_weight,
    up_bias,
    down_weight,
    down_bias,
):
    me = lax.axis_index("fsdp")
    core, z, y, x = me % 2, (me // 2) % 4, (me // 8) % 4, me // 32

    digits = (jnp.where(core == 0, x, z), y, jnp.where(core == 0, z, x))
    at = jnp.stack(digits + (core,)).astype(jnp.int32)
    extra = jnp.zeros((1, 128), bf16)
    start = 0
    for vector in (
        ln1_gain, ln1_bias, qkv_bias, out_bias, ln2_gain, ln2_bias, up_bias, down_bias
    ):
        width = vector.shape[0]
        extra = extra + jnp.pad(vector[None], ((0, 0), (start, 128 - start - width)))
        start += width
    mine, theirs, whole_rows = pack_weights(
        at, qkv_weight, out_weight, up_weight, extra, down_weight
    )
    joint = join_weights(at, mine, swap(theirs), permute(whole_rows, ROW_FROM))
    joint, tokens, cotangent, segment, later = lax.optimization_barrier(
        (joint, tokens, cotangent, segment, core)
    )
    both_tokens = jnp.concatenate([tokens, swap(tokens)], axis=0)
    both_cot = jnp.concatenate([cotangent, swap(cotangent)], axis=0)
    both_segment = jnp.concatenate([segment, swap(segment)], axis=0)
    natural, order, scramble, spread = row_maps(later)
    maps = small_maps(later, natural)
    scaled, inverse, g, cosine, sine_a, sine_b, bias = prepare(
        dot(both_tokens, order, NT).astype(bf16), both_cot, both_segment
    )

    wide_w, narrow_w = place_first(at, collect(joint, 2))
    wide_w = place_second(at, collect(wide_w, 1))
    wide_w, narrow_w = lax.optimization_barrier((wide_w, narrow_w))
    wide_w = collect(wide_w, 0)
    narrow_w = place_second(at, collect(narrow_w, 1))
    narrow_w = collect(narrow_w, 0)
    mlp0, mlp1, back0, back1, sums, vectors, w0, w1, w2, w3 = run_mlp(
        at, maps, *wide_w, scaled, inverse, g, spread
    )
    wide = exchange((w0, w1, w2, w3), 0)
    out0, out1, grad0, grad1, b0, b1, b2, b3 = run_attention(
        at, *narrow_w, scaled, inverse, g, vectors, cosine, sine_a, sine_b, bias,
        scramble, spread, maps, sums,
    )
    wide, b0, b1, b2, b3 = lax.optimization_barrier((wide, b0, b1, b2, b3))
    narrow = exchange((b0, b1, b2, b3), 0)
    wide = sum_first(at, w0, wide)
    wide = added(wide[0], exchange(wide, 1))
    narrow = sum_first(at, b0, narrow)
    narrow = added(narrow[0], exchange(narrow, 1))
    blocks = jnp.concatenate([narrow, wide], axis=1).reshape(4, 12, CUT + 2 * HF)
    last = [
        lax.dynamic_index_in_dim(blocks, (digits[2] + rel) % 4, 0, keepdims=False)
        for rel in range(4)
    ]
    last = added(last[0], exchange([last[0]] + [part.astype(bf16) for part in last[1:]], 2))
    narrow, wide = last[:, :CUT], last[:, CUT:]

    down_rows = jnp.concatenate([wide[:, HF : HF + D], wide[:, HF + D :]], axis=0)
    out_rows = jnp.concatenate([narrow[:6, :HD], narrow[6:, :HD]], axis=1)
    own_rows = permute(jnp.concatenate([down_rows, out_rows], axis=0), ROW_PAIRS)
    own_down, own_out = own_rows[:24], own_rows[24:]
    both = jnp.concatenate([narrow[:, HD:], wide[:, :HF]], axis=1).reshape(2, 6, QW + 128 + HF)
    mine = lax.dynamic_index_in_dim(both, core, 0, keepdims=False)
    theirs = swap(lax.dynamic_index_in_dim(both, 1 - core, 0, keepdims=False))
    low = jnp.where(core == 0, mine, theirs)
    high = jnp.where(core == 0, theirs, mine)
    own_qkv = jnp.stack(
        [low[:, :QW].reshape(6, 3, HD), high[:, :QW].reshape(6, 3, HD)], axis=2
    ).reshape(6, 3 * D)
    own_up = jnp.concatenate([low[:, QW + 128 :], high[:, QW + 128 :]], axis=1)
    line = (low + high)[0, QW : QW + 128]
    own = {}
    start = 0
    for name, width in SMALL:
        own[name] = line[start : start + width]
        start += width

    live = (segment >= 0).astype(f32)[:, None]
    out_sum = out0 + mlp0 + swap(out1 + mlp1) + vectors[:, spot("outb")] + vectors[:, spot("downb")]
    output = (tokens.astype(f32) + live * out_sum).astype(bf16)
    def restore(values):
        return lax.dot_general(
            values, order.astype(f32), (NN, ((), ())), precision=lax.Precision.HIGHEST
        )

    grad_tokens = cotangent.astype(f32) + (restore(grad0 + back0) + swap(restore(grad1 + back1)))
    return (
        output,
        grad_tokens,
        own["ln1g"],
        own["ln1b"],
        own_qkv,
        own["qkvb"],
        own_out,
        own["outb"],
        own["ln2g"],
        own["ln2b"],
        own_up,
        own["upb"],
        own_down,
        own["downb"],
    )


def solution(mesh):
    row = P("fsdp", None)
    flat = P("fsdp")
    return jax.shard_map(
        body,
        mesh=mesh,
        in_specs=(
            row, row, flat, flat, flat, row, flat, row, flat, flat, flat, row, flat, row, flat,
        ),
        out_specs=(
            row, row, flat, flat, row, flat, row, flat, flat, flat, row, flat, row, flat,
        ),
        check_vma=False,
    )
```

```python
import math

import jax
import jax.numpy as jnp
from jax import lax
from jax.experimental import pallas as pl
from jax.experimental.pallas import tpu as pltpu
from jax.sharding import PartitionSpec as P

D = 768
HEADS = 12
HEAD_DIM = 64
ROTARY = 16
FF = 3072
MB_ROWS = 128
ROWS = 256
HH = HEADS // 2
HD = D // 2
HF = FF // 2
QW = 3 * HD

epsilon = 1e-05
masked_score = -1e30
inv_sqrt_two = 1.0 / math.sqrt(2.0)
inv_sqrt_two_pi = 1.0 / math.sqrt(2.0 * math.pi)
bf16 = jnp.bfloat16
f32 = jnp.float32

STRIDE = {"x": 32, "y": 8, "z": 2, "c": 1}
SIZE = {"x": 4, "y": 4, "z": 4, "c": 2}
SMALL = (("ln1g", 6), ("ln1b", 6), ("qkvb", 18), ("outb", 6), ("ln2g", 6), ("ln2b", 6), ("upb", 24), ("downb", 6))


def digit(index, axis):
    return (index // STRIDE[axis]) % SIZE[axis]


ORDER = (("x", "y", "z"), ("z", "y", "x"))


def shift(axis, step):
    pairs = []
    for source in range(128):
        at = digit(source, axis)
        target = source + ((at + step) % SIZE[axis] - at) * STRIDE[axis]
        pairs.append((source, target))
    return pairs


def stage_shift(stage, step):
    pairs = []
    for source in range(128):
        axis = ORDER[source % 2][stage]
        at = digit(source, axis)
        pairs.append((source, source + ((at + step) % 4 - at) * STRIDE[axis]))
    return pairs


def holder(half, block):
    digits = (block // 16, (block // 4) % 4, block % 4)
    return half + sum(STRIDE[axis] * at for axis, at in zip(ORDER[half], digits))


ROW_PAIRS = [
    (holder(half, block), 64 * half + block) for half in range(2) for block in range(64)
]


ROW_FROM = [(source, target) for target, source in ROW_PAIRS]


def permute(values, pairs):
    return lax.ppermute(values, "fsdp", pairs)


def swap(values):
    return permute(values, shift("c", 1))


def exchange(parts, stage):
    _, after, across, before = parts
    return (
        permute(after, stage_shift(stage, 1)),
        permute(before, stage_shift(stage, -1)),
        permute(across, stage_shift(stage, 2)),
    )


def added(own, arrived):
    total = own.astype(f32)
    for piece in arrived:
        total = total + piece.astype(f32)
    return total


def sum_kernel(at_ref, own_ref, one_ref, two_ref, three_ref, own_out, *outs):
    refs = (own_ref, one_ref, two_ref, three_ref)
    for rel in range(4):
        rs = pl.ds(pl.multiple_of(48 * lax.rem(at_ref[1] + rel, 4), 16), 48)
        total = added(own_ref[rs, :], [ref[rs, :] for ref in refs[1:]])
        if rel == 0:
            own_out[...] = total
        else:
            outs[rel - 1][...] = total.astype(bf16)


def second_sum_kernel(at_ref, n0, n1, n2, n3, w0, w1, w2, w3, own_out, one_out, two_out, three_out, held_s):
    narrow = added(n0[...], [n1[...], n2[...], n3[...]])
    wide = added(w0[...], [w1[...], w2[...], w3[...]])
    for part in range(4):
        held_s[part, 0:12, :CUT] = narrow[12 * part : 12 * part + 12, :]
        held_s[part, 0:12, CUT:] = wide[12 * part : 12 * part + 12, :]
    for rel, ref in enumerate((own_out, one_out, two_out, three_out)):
        rows = held_s[lax.rem(at_ref[2] + rel, 4), 0:12, :]
        ref[...] = rows.astype(ref.dtype)


def sum_second(at, narrow, wide):
    return pl.pallas_call(
        second_sum_kernel,
        out_shape=(struct((12, LAST), f32),) + (struct((12, LAST), bf16),) * 3,
        in_specs=[SMEM] + [VMEM] * 8,
        out_specs=(VMEM,) * 4,
        scratch_shapes=[pltpu.VMEM((4, 16, LAST), f32)],
        compiler_params=pltpu.CompilerParams(vmem_limit_bytes=8 << 20),
    )(at, *narrow, *wide)


def last_sum_kernel(at_ref, own, one, two, three, mine_ref, theirs_ref, rows_ref):
    total = added(own[...], [one[...], two[...], three[...]])
    first = at_ref[3] == 0
    low, high = total[0:6, :], total[6:12, :]
    for ref, rows in (
        (mine_ref, jnp.where(first, low, high)),
        (theirs_ref, jnp.where(first, high, low)),
    ):
        ref[:, : QW + 128] = rows[:, HD:CUT]
        ref[:, QW + 128 :] = rows[:, CUT : CUT + HF]
    rows_ref[0:12, :] = total[:, CUT + HF : CUT + HF + D]
    rows_ref[12:24, :] = total[:, CUT + HF + D :]
    rows_ref[24:30, :HD] = low[:, :HD]
    rows_ref[24:30, HD:] = high[:, :HD]
    rows_ref[30:32, :] = jnp.zeros((2, D), f32)


def sum_last(at, *parts):
    return pl.pallas_call(
        last_sum_kernel,
        out_shape=(struct((6, PAIR), f32), struct((6, PAIR), f32), struct((32, D), f32)),
        in_specs=[SMEM] + [VMEM] * 4,
        out_specs=(VMEM,) * 3,
        compiler_params=pltpu.CompilerParams(vmem_limit_bytes=4 << 20),
    )(at, *parts)


def sum_first(at, own, arrived):
    width = own.shape[1]
    return pl.pallas_call(
        sum_kernel,
        out_shape=(struct((48, width), f32),) + (struct((48, width), bf16),) * 3,
        in_specs=[SMEM] + [VMEM] * 4,
        out_specs=(VMEM,) * 4,
        compiler_params=pltpu.CompilerParams(vmem_limit_bytes=12 << 20),
        cost_estimate=pl.CostEstimate(
            flops=4 * 192 * width, bytes_accessed=10 * 192 * width, transcendentals=0
        ),
    )(at, own, *arrived)


CUT = HD + QW + 128
PAIR = QW + HF + 128
WIDE_COLS = 2 * HF + 128
LAST = CUT + 2 * HF
NARROW_COLS = HD + QW


def dot(a, b, dims):
    return lax.dot_general(a, b, (dims, ((), ())), preferred_element_type=f32)


NN = ((1,), (0,))
NT = ((1,), (1,))
TN = ((0,), (0,))
ALL = 2 * ROWS
BLOCKS = ALL // MB_ROWS
WIDE = 6 * D + QW + HF
VMEM = pl.BlockSpec(memory_space=pltpu.VMEM)
SMEM = pl.BlockSpec(memory_space=pltpu.SMEM)
ANY = pl.BlockSpec(memory_space=pl.ANY)


def struct(shape, kind):
    return jax.ShapeDtypeStruct(shape, kind)


def spot(name):
    at = 0
    for key, width in SMALL:
        span = QW if key == "qkvb" else HF if key == "upb" else 128 * width
        if key == name:
            return slice(at, at + span)
        at += span


def small_maps(core, natural):
    device, lane = [], []
    at = 0
    for key, width in SMALL:
        if key == "qkvb":
            flat = (jnp.arange(3)[:, None] * D + core * HD + jnp.arange(HD)[None]).reshape(QW)
        elif key == "upb":
            flat = core * HF + jnp.arange(HF)
        else:
            flat = natural if key.startswith("ln") else jnp.arange(128 * width)
        device.append(flat // width)
        lane.append(at + flat % width)
        at += width
    return jnp.stack([jnp.concatenate(device), jnp.concatenate(lane)]).astype(jnp.int32)


def one_hot(condition):
    return condition.astype(f32).astype(bf16)


def pack_kernel(at_ref, qkv_ref, out_ref, up_ref, extra_ref, down_ref, mine_ref, theirs_ref, rows_ref):
    core = at_ref[3]
    for half, to_ref in ((core, mine_ref), (1 - core, theirs_ref)):
        to_ref[:, QW + HF :] = jnp.zeros((6, 128), bf16)
        to_ref[0:1, QW + HF :] = extra_ref[...]
        for part in range(3):
            begin = pl.multiple_of(part * D + half * HD, 128)
            to_ref[:, part * HD : (part + 1) * HD] = qkv_ref[:, pl.ds(begin, HD)]
        begin = pl.multiple_of(half * HF, 128)
        to_ref[:, QW : QW + HF] = up_ref[:, pl.ds(begin, HF)]
    rows_ref[24:32, :] = jnp.zeros((8, D), bf16)
    rows_ref[0:24, :] = down_ref[...]
    rows_ref[24:30, :] = out_ref[...]


def pack_weights(*operands):
    return pl.pallas_call(
        pack_kernel,
        out_shape=(struct((6, PAIR), bf16), struct((6, PAIR), bf16), struct((32, D), bf16)),
        in_specs=[SMEM] + [VMEM] * 5,
        out_specs=(VMEM,) * 3,
        compiler_params=pltpu.CompilerParams(vmem_limit_bytes=4 << 20),
    )(*operands)


def join_kernel(at_ref, mine_ref, got_ref, rows_ref, to_ref):
    first = at_ref[3] == 0
    mine, got = mine_ref[...].astype(f32), got_ref[...].astype(f32)
    low = jnp.where(first, mine, got).astype(bf16)
    high = jnp.where(first, got, mine).astype(bf16)
    for at, rows in ((0, low), (6, high)):
        to_ref[at : at + 6, :HF] = rows[:, QW : QW + HF]
        to_ref[at : at + 6, 2 * HF : WIDE_COLS] = rows[:, QW + HF :]
        to_ref[at : at + 6, WIDE_COLS + HD :] = rows[:, :QW]
    to_ref[:, HF : HF + D] = rows_ref[0:12, :]
    to_ref[:, HF + D : 2 * HF] = rows_ref[12:24, :]
    to_ref[0:6, WIDE_COLS : WIDE_COLS + HD] = rows_ref[24:30, :HD]
    to_ref[6:12, WIDE_COLS : WIDE_COLS + HD] = rows_ref[24:30, HD:]


def join_weights(*operands):
    return pl.pallas_call(
        join_kernel,
        out_shape=struct((12, WIDE_COLS + NARROW_COLS), bf16),
        in_specs=[SMEM] + [VMEM] * 3,
        out_specs=VMEM,
        compiler_params=pltpu.CompilerParams(vmem_limit_bytes=4 << 20),
    )(*operands)


def collect(block, stage):
    return (
        block,
        permute(block, stage_shift(stage, -1)),
        permute(block, stage_shift(stage, 2)),
        permute(block, stage_shift(stage, 1)),
    )


def first_kernel(at_ref, one, two, three, four, wide_ref, narrow_ref, held_s):
    held_s[...] = jnp.zeros_like(held_s)
    for rel, ref in enumerate((one, two, three, four)):
        held_s[16 * rel : 16 * rel + 12, :] = ref[...]
    row = lax.broadcasted_iota(jnp.int32, (48, 64), 0)
    column = lax.broadcasted_iota(jnp.int32, (48, 64), 1)
    rel = lax.rem(row // 12 - at_ref[2] + 4, 4)
    pick = one_hot(column == 16 * rel + lax.rem(row, 12))
    wide_ref[...] = dot(pick, held_s[:, :WIDE_COLS], NN).astype(bf16)
    narrow_ref[...] = dot(pick, held_s[:, WIDE_COLS:], NN).astype(bf16)


def place_first(at, pieces):
    return pl.pallas_call(
        first_kernel,
        out_shape=(struct((48, WIDE_COLS), bf16), struct((48, NARROW_COLS), bf16)),
        in_specs=[SMEM] + [VMEM] * 4,
        out_specs=(VMEM,) * 2,
        scratch_shapes=[pltpu.VMEM((64, WIDE_COLS + NARROW_COLS), bf16)],
        compiler_params=pltpu.CompilerParams(vmem_limit_bytes=6 << 20),
    )(at, *pieces)


def second_kernel(at_ref, one, two, three, four, to_ref):
    for rel, ref in enumerate((one, two, three, four)):
        begin = pl.multiple_of(48 * lax.rem(at_ref[1] + rel, 4), 16)
        to_ref[pl.ds(begin, 48), :] = ref[...]


def place_second(at, pieces):
    return pl.pallas_call(
        second_kernel,
        out_shape=struct((192, pieces[0].shape[1]), bf16),
        in_specs=[SMEM] + [VMEM] * 4,
        out_specs=VMEM,
        compiler_params=pltpu.CompilerParams(vmem_limit_bytes=6 << 20),
    )(at, *pieces)


def place_third(at_ref, refs, target, sems):
    copies = []
    for rel, ref in enumerate(refs):
        begin = pl.multiple_of(192 * lax.rem(at_ref[0] + rel, 4), 64)
        copies.append(pltpu.make_async_copy(ref, target.at[pl.ds(begin, 192), :], sems.at[rel]))
        copies[-1].start()
    return copies


def spread_small(table, maps_ref, rows_ref):
    step = 2432
    for at in range(0, WIDE, step):
        index = lax.broadcasted_iota(jnp.int32, (128, step), 0)
        hot = one_hot(index == maps_ref[1:2, at : at + step])
        spread = dot(table, hot, NN)
        held = jnp.where(index == maps_ref[0:1, at : at + step], spread, 0.0)
        rows_ref[:, at : at + step] = jnp.sum(held, axis=0, keepdims=True)


def norm_back(upstream, scaled, inverse, gain):
    weighted = upstream * gain
    middle = jnp.mean(weighted, axis=-1, keepdims=True)
    slope = jnp.mean(weighted * scaled, axis=-1, keepdims=True)
    grad_in = inverse * (weighted - middle - scaled * slope)
    gain_sum = jnp.sum(upstream * scaled, axis=0, keepdims=True)
    return grad_in, gain_sum, jnp.sum(upstream, axis=0, keepdims=True)


def mlp_kernel(
    at_ref, maps_ref, p0, p1, p2, p3, scaled_ref, inverse_ref, g_ref, spread_ref,
    mlp0, mlp1, back0, back1, sums_ref, rows_ref, w0, w1, w2, w3,
    held_s, down_ref,
    h_s, ht_s, act_s, order_s, gp_s, gh_s, sems,
):
    copies = place_third(at_ref, (p0, p1, p2, p3), held_s, sems)
    step = 384
    row = lax.broadcasted_iota(jnp.int32, (step, step), 0)
    column = lax.broadcasted_iota(jnp.int32, (step, step), 1)
    block = lax.rem(row, 192) // 12
    wanted = block * 24 + lax.rem(row, 12) + jnp.where(row >= 192, 12, 0)
    deal = one_hot(column == wanted)
    for copy in copies:
        copy.wait()
    table = dot(spread_ref[...], held_s[:, 2 * HF :], TN).astype(bf16)
    spread_small(table, maps_ref, rows_ref)
    for part in range(4):
        rs = slice(192 * part, 192 * part + 192)
        down_ref[step * part : step * (part + 1), :] = (
            dot(deal[:192], held_s[rs, HF : HF + D], TN)
            + dot(deal[192:], held_s[rs, HF + D : 2 * HF], TN)
        ).astype(bf16)
    gain = rows_ref[:, spot("ln2g")]
    h = scaled_ref[...] * gain + rows_ref[:, spot("ln2b")]
    h_s[...] = h.astype(bf16)
    ht_s[...] = h.T.astype(bf16)
    first = spot("upb").start
    for turn_at, at in enumerate(range(0, HF, step)):
        cut = slice(at, at + step)
        pre = dot(h_s[...], held_s[:, cut], NN) + rows_ref[:, first + at : first + at + step]
        cumulative = 0.5 * (1.0 + lax.erf(pre * inv_sqrt_two))
        density = jnp.exp(-0.5 * pre * pre) * inv_sqrt_two_pi
        act = (pre * cumulative).astype(bf16)
        act_s[:, cut] = act
        order_s[turn_at] = dot(deal, act, NT).astype(bf16)
        grad_act = dot(g_ref[...], down_ref[cut, :], NT)
        grad_pre = (grad_act * (cumulative + pre * density)).astype(bf16)
        gp_s[:, cut] = grad_pre
        sums_ref[0:1, cut] = jnp.sum(grad_pre.astype(f32), axis=0, keepdims=True)
    for rel, ref in enumerate((w0, w1, w2, w3)):
        which = lax.rem(at_ref[0] + rel, 4)
        begin = pl.multiple_of(192 * which, 64)
        ref[:, :HF] = dot(ht_s[pl.ds(begin, 192), :], gp_s[...], NN).astype(bf16)
        dealt = order_s[which]
        ref[:, HF : HF + D] = dot(dealt[:192], g_ref[...], NN).astype(bf16)
        ref[:, HF + D :] = dot(dealt[192:], g_ref[...], NN).astype(bf16)
    mlp0[...] = dot(act_s[:ROWS, :], down_ref[...], NN)
    mlp1[...] = dot(act_s[ROWS:, :], down_ref[...], NN)
    gh_s[...] = dot(gp_s[...], held_s[:, :HF], NT)
    back, gain_sum, shift_sum = norm_back(gh_s[...], scaled_ref[...], inverse_ref[...], gain)
    back0[...] = back[:ROWS]
    back1[...] = back[ROWS:]
    sums_ref[1:2, :D] = gain_sum
    sums_ref[2:3, :D] = shift_sum
    sums_ref[3:4, :D] = jnp.sum(g_ref[:ROWS, :].astype(f32), axis=0, keepdims=True)


def run_mlp(*operands):
    return pl.pallas_call(
        mlp_kernel,
        out_shape=(struct((ROWS, D), f32),) * 4
        + (struct((8, HF), f32), struct((1, WIDE), f32))
        + (struct((192, 2 * HF), bf16),) * 4,
        in_specs=[SMEM, VMEM] + [ANY] * 4 + [VMEM] * 4,
        out_specs=(VMEM,) * 10,
        scratch_shapes=[
            pltpu.VMEM((D, WIDE_COLS), bf16),
            pltpu.VMEM((HF, D), bf16),
            pltpu.VMEM((ALL, D), bf16),
            pltpu.VMEM((D, ALL), bf16),
            pltpu.VMEM((ALL, HF), bf16),
            pltpu.VMEM((4, 384, ALL), bf16),
            pltpu.VMEM((ALL, HF), bf16),
            pltpu.VMEM((ALL, D), f32),
            pltpu.SemaphoreType.DMA((4,)),
        ],
        compiler_params=pltpu.CompilerParams(vmem_limit_bytes=33 << 20),
        cost_estimate=pl.CostEstimate(
            flops=8 * 2 * ALL * D * HF, bytes_accessed=20 << 20, transcendentals=2 * ALL * HF
        ),
    )(*operands)


def turn(values, cosine, sine_a, sine_b):
    parts = []
    for at in range(0, values.shape[1], 128):
        part = values[:, at : at + 128]
        parts.append(
            part * cosine
            + pltpu.roll(part, 120, 1) * sine_a
            + pltpu.roll(part, 8, 1) * sine_b
        )
    return jnp.concatenate(parts, axis=1) if len(parts) > 1 else parts[0]


def attention_kernel(
    at_ref, p0, p1, p2, p3, scaled_ref, inverse_ref, g_ref, rows_ref, cos_ref, sina_ref, sinb_ref,
    bias_ref, scramble_ref, spread_ref, maps_ref, sums_ref,
    out0, out1, grad0, grad1, b0, b1, b2, b3,
    held_s, ow_ref,
    h_s, ht_s, q_s, k_s, v_s, ga_s, attn_s, gj_s, gh_s, sa_s, sems,
):
    copies = place_third(at_ref, (p0, p1, p2, p3), held_s, sems)
    gain = rows_ref[:, spot("ln1g")]
    h = scaled_ref[...] * gain + rows_ref[:, spot("ln1b")]
    h_s[...] = h.astype(bf16)
    ht_s[...] = h.T.astype(bf16)
    for copy in copies:
        copy.wait()
    inner = lax.rem(lax.broadcasted_iota(jnp.int32, (D, HD), 0), 12)
    left = scramble_ref[...] * one_hot(inner < 6)
    right = scramble_ref[...] * one_hot(inner >= 6)
    ow_ref[:, :HD] = dot(left, held_s[:, :HD], TN).astype(bf16)
    ow_ref[:, HD:] = dot(right, held_s[:, :HD], TN).astype(bf16)
    first = spot("qkvb").start
    cosine, sine_a, sine_b = cos_ref[...], sina_ref[...], sinb_ref[...]
    for part, ref in enumerate((q_s, k_s, v_s)):
        cut = slice(HD + part * HD, 2 * HD + part * HD)
        bias = rows_ref[:, first + part * HD : first + (part + 1) * HD]
        joint = dot(h_s[...], held_s[:, cut], NN) + bias
        if part < 2:
            joint = turn(joint, cosine, sine_a, sine_b)
        ref[...] = joint.astype(bf16)
    ga_s[...] = dot(g_ref[...], ow_ref[...], NT).astype(bf16)

    scale = HEAD_DIM ** (-0.5)
    lanes = lax.broadcasted_iota(jnp.int32, (MB_ROWS, 128), 1) < HEAD_DIM
    low = lanes.astype(f32).astype(bf16)
    high = (1.0 - lanes.astype(f32)).astype(bf16)

    def one_block(block, carry):
        rs = pl.ds(pl.multiple_of(block * MB_ROWS, MB_ROWS), MB_ROWS)
        bias = bias_ref[rs, :]
        bias = jnp.concatenate([bias, bias], axis=0)
        turn_c, turn_a, turn_b = cos_ref[rs, :], -sina_ref[rs, :], -sinb_ref[rs, :]
        for pair in range(HH // 2):
            cs = slice(pair * 128, pair * 128 + 128)
            qp, kp, vp, ga = q_s[rs, cs], k_s[rs, cs], v_s[rs, cs], ga_s[rs, cs]
            qm = jnp.concatenate([qp * low, qp * high], axis=0)
            gm = jnp.concatenate([ga * low, ga * high], axis=0)
            scores = dot(qm, kp, NT) * scale + bias
            expd = jnp.exp(scores - jnp.max(scores, axis=-1, keepdims=True))
            probs = expd / jnp.sum(expd, axis=-1, keepdims=True)
            p = probs.astype(bf16)
            mixed = dot(p, vp, NN)
            attn_s[rs, cs] = jnp.where(lanes, mixed[:MB_ROWS], mixed[MB_ROWS:]).astype(bf16)
            grad_p = dot(gm, vp, NT)
            grad_v = dot(p, gm, TN)
            delta = jnp.sum(probs * grad_p, axis=-1, keepdims=True)
            ds = (probs * (grad_p - delta)).astype(bf16)
            both = dot(ds, kp, NN)
            grad_q = jnp.where(lanes, both[:MB_ROWS], both[MB_ROWS:]) * scale
            grad_k = dot(ds, qm, TN) * scale
            gj_s[rs, cs] = turn(grad_q, turn_c, turn_a, turn_b).astype(bf16)
            ck = slice(HD + pair * 128, HD + pair * 128 + 128)
            cv = slice(2 * HD + pair * 128, 2 * HD + pair * 128 + 128)
            gj_s[rs, ck] = turn(grad_k, turn_c, turn_a, turn_b).astype(bf16)
            gj_s[rs, cv] = grad_v.astype(bf16)
        return carry

    lax.fori_loop(0, BLOCKS, one_block, 0)

    sa_s[...] = dot(scramble_ref[...], attn_s[...], NT).astype(bf16)
    gh_s[...] = dot(gj_s[...], held_s[:, HD:], NT)
    back, gain_sum, shift_sum = norm_back(gh_s[...], scaled_ref[...], inverse_ref[...], gain)
    grad0[...] = back[:ROWS]
    grad1[...] = back[ROWS:]
    part = dot(attn_s[...], ow_ref[...], NN)
    out0[...] = part[:ROWS]
    out1[...] = part[ROWS:]

    branch = sums_ref[3:4, :D]
    joint_sum = jnp.sum(gj_s[...].astype(f32), axis=0, keepdims=True)
    values = {
        "ln1g": gain_sum,
        "ln1b": shift_sum,
        "qkvb": joint_sum,
        "outb": branch,
        "ln2g": sums_ref[1:2, :D],
        "ln2b": sums_ref[2:3, :D],
        "upb": sums_ref[0:1, :],
        "downb": branch,
    }
    table = jnp.zeros((128, 128), f32)
    for key, _ in SMALL:
        span = spot(key)
        index = lax.broadcasted_iota(jnp.int32, (128, span.stop - span.start), 0)
        hot = (index == maps_ref[1:2, span]).astype(f32).astype(bf16)
        held = jnp.where(index == maps_ref[0:1, span], values[key], 0.0).astype(bf16)
        table = table + dot(held, hot, NT)
    table = table.astype(bf16)
    for rel, ref in enumerate((b0, b1, b2, b3)):
        rs = pl.ds(pl.multiple_of(192 * lax.rem(at_ref[0] + rel, 4), 64), 192)
        one = dot(sa_s[rs, :], g_ref[:, :HD], NN)
        two = dot(sa_s[rs, :], g_ref[:, HD:], NN)
        inner = lax.rem(lax.broadcasted_iota(jnp.int32, (192, HD), 0), 12)
        ref[:, :HD] = jnp.where(inner >= 6, two, one).astype(bf16)
        ref[:, HD : HD + QW] = dot(ht_s[rs, :], gj_s[...], NN).astype(bf16)
        ref[:, HD + QW :] = dot(spread_ref[rs, :], table, NN).astype(bf16)


def run_attention(*operands):
    half = (struct((ROWS, D), f32),) * 4
    return pl.pallas_call(
        attention_kernel,
        out_shape=half + (struct((192, CUT), bf16),) * 4,
        in_specs=[SMEM] + [ANY] * 4 + [VMEM] * (len(operands) - 5),
        out_specs=(VMEM,) * 8,
        scratch_shapes=[
            pltpu.VMEM((D, NARROW_COLS), bf16),
            pltpu.VMEM((HD, D), bf16),
            pltpu.VMEM((ALL, D), bf16),
            pltpu.VMEM((D, ALL), bf16),
            pltpu.VMEM((ALL, HD), bf16),
            pltpu.VMEM((ALL, HD), bf16),
            pltpu.VMEM((ALL, HD), bf16),
            pltpu.VMEM((ALL, HD), bf16),
            pltpu.VMEM((ALL, HD), bf16),
            pltpu.VMEM((ALL, QW), bf16),
            pltpu.VMEM((ALL, D), f32),
            pltpu.VMEM((D, ALL), bf16),
            pltpu.SemaphoreType.DMA((4,)),
        ],
        compiler_params=pltpu.CompilerParams(vmem_limit_bytes=28 << 20),
        cost_estimate=pl.CostEstimate(
            flops=6 * 2 * ALL * D * (QW + HD), bytes_accessed=20 << 20, transcendentals=ALL * 128 * HH
        ),
    )(*operands)


def prepare(tokens, cotangent, segment):
    rows32 = tokens.astype(f32)
    centred = rows32 - jnp.mean(rows32, axis=-1, keepdims=True)
    inverse = lax.rsqrt(jnp.mean(centred * centred, axis=-1, keepdims=True) + epsilon)
    live = (segment >= 0).astype(f32)[:, None]
    g = (cotangent.astype(f32) * live).astype(bf16)
    blocks = segment.reshape(BLOCKS, MB_ROWS)
    same = blocks[:, :, None] == blocks[:, None, :]
    earlier = jnp.arange(MB_ROWS)[None, :] <= jnp.arange(MB_ROWS)[:, None]
    allowed = (same & earlier[None]).reshape(ALL, MB_ROWS)
    bias = jnp.where(allowed, 0.0, masked_score)
    place = (jnp.sum(allowed.astype(jnp.int32), axis=1) - 1).astype(f32)
    lane = jnp.arange(128) % HEAD_DIM
    frequency = jnp.exp(
        (lane % 8).astype(f32) * (-2.0 * math.log(10000.0) / ROTARY)
    )
    angle = place[:, None] * frequency[None, :]
    cosine = jnp.where(lane < 16, jnp.cos(angle), 1.0)
    sine = jnp.sin(angle)
    sine_a = jnp.where(lane < 8, -sine, 0.0)
    sine_b = jnp.where((lane >= 8) & (lane < 16), sine, 0.0)
    return centred * inverse, inverse, g, cosine, sine_a, sine_b, bias


def row_maps(core):
    place = jnp.arange(D)[:, None]
    block, inner = place // 12, place % 12
    first, second, third = block // 16, (block // 4) % 4, block % 4
    x = jnp.where(core == 0, first, third)
    z = jnp.where(core == 0, third, first)
    natural = ((x * 4 + second) * 4 + z) * 12 + inner
    order = (natural == jnp.arange(D)[None]).astype(bf16)
    scramble = (block * 6 + inner % 6 == jnp.arange(HD)[None]).astype(bf16)
    spread = (natural == 6 * jnp.arange(128)[None]).astype(bf16)
    return natural[:, 0], order, scramble, spread


def body(
    tokens,
    cotangent,
    segment,
    ln1_gain,
    ln1_bias,
    qkv_weight,
    qkv_bias,
    out_weight,
    out_bias,
    ln2_gain,
    ln2_bias,
    up_weight,
    up_bias,
    down_weight,
    down_bias,
):
    me = lax.axis_index("fsdp")
    core, z, y, x = me % 2, (me // 2) % 4, (me // 8) % 4, me // 32

    digits = (jnp.where(core == 0, x, z), y, jnp.where(core == 0, z, x))
    at = jnp.stack(digits + (core,)).astype(jnp.int32)
    extra = jnp.zeros((1, 128), bf16)
    start = 0
    for vector in (
        ln1_gain, ln1_bias, qkv_bias, out_bias, ln2_gain, ln2_bias, up_bias, down_bias
    ):
        width = vector.shape[0]
        extra = extra + jnp.pad(vector[None], ((0, 0), (start, 128 - start - width)))
        start += width
    mine, theirs, whole_rows = pack_weights(
        at, qkv_weight, out_weight, up_weight, extra, down_weight
    )
    joint = join_weights(at, mine, swap(theirs), permute(whole_rows, ROW_FROM))
    joint, tokens, cotangent, segment, later = lax.optimization_barrier(
        (joint, tokens, cotangent, segment, core)
    )
    both_tokens = jnp.concatenate([tokens, swap(tokens)], axis=0)
    both_cot = jnp.concatenate([cotangent, swap(cotangent)], axis=0)
    both_segment = jnp.concatenate([segment, swap(segment)], axis=0)
    natural, order, scramble, spread = row_maps(later)
    maps = small_maps(later, natural)
    scaled, inverse, g, cosine, sine_a, sine_b, bias = prepare(
        dot(both_tokens, order, NT).astype(bf16), both_cot, both_segment
    )

    wide_w, narrow_w = place_first(at, collect(joint, 2))
    wide_w = place_second(at, collect(wide_w, 1))
    wide_w, narrow_w = lax.optimization_barrier((wide_w, narrow_w))
    wide_w = collect(wide_w, 0)
    narrow_w = place_second(at, collect(narrow_w, 1))
    narrow_w = collect(narrow_w, 0)
    mlp0, mlp1, back0, back1, sums, vectors, w0, w1, w2, w3 = run_mlp(
        at, maps, *wide_w, scaled, inverse, g, spread
    )
    wide = exchange((w0, w1, w2, w3), 0)
    out0, out1, grad0, grad1, b0, b1, b2, b3 = run_attention(
        at, *narrow_w, scaled, inverse, g, vectors, cosine, sine_a, sine_b, bias,
        scramble, spread, maps, sums,
    )
    wide, b0, b1, b2, b3 = lax.optimization_barrier((wide, b0, b1, b2, b3))
    narrow = exchange((b0, b1, b2, b3), 0)
    wide = sum_first(at, w0, wide)
    wide = (wide[0],) + exchange(wide, 1)
    narrow = sum_first(at, b0, narrow)
    narrow = (narrow[0],) + exchange(narrow, 1)
    last = sum_second(at, narrow, wide)
    mine, theirs, rows = sum_last(at, last[0], *exchange(last, 2))
    own_rows = permute(rows, ROW_PAIRS)
    own_down, own_out = own_rows[:24], own_rows[24:30]
    theirs = swap(theirs)
    low = jnp.where(core == 0, mine, theirs)
    high = jnp.where(core == 0, theirs, mine)
    own_qkv = jnp.stack(
        [low[:, :QW].reshape(6, 3, HD), high[:, :QW].reshape(6, 3, HD)], axis=2
    ).reshape(6, 3 * D)
    own_up = jnp.concatenate([low[:, QW + 128 :], high[:, QW + 128 :]], axis=1)
    line = (low + high)[0, QW : QW + 128]
    own = {}
    start = 0
    for name, width in SMALL:
        own[name] = line[start : start + width]
        start += width

    live = (segment >= 0).astype(f32)[:, None]
    out_sum = out0 + mlp0 + swap(out1 + mlp1) + vectors[:, spot("outb")] + vectors[:, spot("downb")]
    output = (tokens.astype(f32) + live * out_sum).astype(bf16)
    def restore(values):
        return lax.dot_general(
            values, order.astype(f32), (NN, ((), ())), precision=lax.Precision.HIGHEST
        )

    grad_tokens = cotangent.astype(f32) + (restore(grad0 + back0) + swap(restore(grad1 + back1)))
    return (
        output,
        grad_tokens,
        own["ln1g"],
        own["ln1b"],
        own_qkv,
        own["qkvb"],
        own_out,
        own["outb"],
        own["ln2g"],
        own["ln2b"],
        own_up,
        own["upb"],
        own_down,
        own["downb"],
    )


def solution(mesh):
    row = P("fsdp", None)
    flat = P("fsdp")
    return jax.shard_map(
        body,
        mesh=mesh,
        in_specs=(
            row, row, flat, flat, flat, row, flat, row, flat, flat, flat, row, flat, row, flat,
        ),
        out_specs=(
            row, row, flat, flat, row, flat, row, flat, flat, flat, row, flat, row, flat,
        ),
        check_vma=False,
    )
```
